32 devices in a mesh: seq: 8 (over z, y), rows: 4 (over x, core).
Axes of the slice: x: 2, y: 2, z: 4, core: 2. Of those that a mesh axis runs over, the one named last changes fastest.
Arguments:
- tokens: bfloat16 [4, 1024, 768], P('rows', 'seq'), may hold values from -6 to 6
- cotangent: bfloat16 [4, 1024, 768], P('rows', 'seq'), may hold values from -6 to 6
- segment_ids: int32 [4, 1024], P('rows', 'seq'), may hold values from 0 to 126, as said below
- restarts: int32 [4, 1024], P('rows', 'seq'), may hold values from 0 to 1, as said below
- position_table: bfloat16 [514, 768], replicated, may hold values from -3 to 3
- query_weight: bfloat16 [768, 768], replicated, may hold values from -0.21875 to 0.21875
- query_bias: bfloat16 [768], replicated, may hold values from -3 to 3
- key_weight: bfloat16 [768, 768], replicated, may hold values from -0.21875 to 0.21875
- value_weight: bfloat16 [768, 768], replicated, may hold values from -0.21875 to 0.21875
- value_bias: bfloat16 [768], replicated, may hold values from -2 to 2
- out_weight: bfloat16 [768, 768], replicated, may hold values from -1.25 to 1.25
- out_bias: bfloat16 [768], replicated, may hold values from -2 to 2
- first_gain: bfloat16 [768], replicated, may hold values from 0.5 to 1.5
- first_shift: bfloat16 [768], replicated, may hold values from -2 to 2
- inner_weight: bfloat16 [768, 3072], replicated, may hold values from -0.21875 to 0.21875
- inner_bias: bfloat16 [3072], replicated, may hold values from -3 to 3
- outer_weight: bfloat16 [3072, 768], replicated, may hold values from -0.109375 to 0.109375
- outer_bias: bfloat16 [768], replicated, may hold values from -2 to 2
- second_gain: bfloat16 [768], replicated, may hold values from 0.5 to 1.5
- second_shift: bfloat16 [768], replicated, may hold values from -2 to 2
Outputs:
- layer_out: bfloat16 [4, 1024, 768], P('rows', 'seq')
- grad_tokens: bfloat16 [4, 1024, 768], P('rows', 'seq')
- grad_table: float32 [514, 768], replicated
- grad_wquery: float32 [768, 768], replicated
- grad_bquery: float32 [768], replicated
- grad_wkey: float32 [768, 768], replicated
- grad_wvalue: float32 [768, 768], replicated
- grad_bvalue: float32 [768], replicated
- grad_wout: float32 [768, 768], replicated
- grad_bout: float32 [768], replicated
- grad_gfirst: float32 [768], replicated
- grad_sfirst: float32 [768], replicated
- grad_winner: float32 [768, 3072], replicated
- grad_binner: float32 [3072], replicated
- grad_wouter: float32 [3072, 768], replicated
- grad_bouter: float32 [768], replicated
- grad_gsecond: float32 [768], replicated
- grad_ssecond: float32 [768], replicated
The draws below stay inside these ranges and needn't reach their ends.
Inputs may be any that keep to these rules, and one draw needn't show every extreme that they name: `segment_ids`: along each row the ids start at 0 and never fall, rising by at most one from token to token; in every row one segment covers tokens of the first and of the last block of 128 tokens; the largest id of some row is 126. Every segment's first token restarts; a token's position, 2 plus its distance from the last restart at or before it, reaches 513 in every row and never more.
All inputs are finite; a program needn't handle non-finite values.
Results may differ from the reference program's by a relative error of at most 0.04.
Values may be sent and summed in bfloat16 or wider, within the bound.
A program may use at most 256 MiB of HBM per device.

```python
import math
import jax
import jax.numpy as jnp
from jax import lax

D = 768
HEADS = 12
HEAD_DIM = 64
FF = 3072
POS_ROWS = 514
TOK_DEV = 128
ROWS = 4
ROW_LEN = 1024


def layout(key):
    first_key, second_key, third_key, fourth_key = jax.random.split(key, 4)
    halfway = max(2, TOK_DEV // 2)
    row_index = jnp.arange(ROWS, dtype=jnp.int32)[:, None]
    leading = jax.random.randint(first_key, (ROWS, 1), 1, halfway)
    trailing = jax.random.randint(second_key, (ROWS, 1), 1, halfway)
    leading = jnp.where(row_index == 0, halfway - 1, leading)
    trailing = jnp.where(row_index == 0, halfway - 1, trailing)
    places = jnp.arange(ROW_LEN, dtype=jnp.int32)[None, :]
    finish = ROW_LEN - trailing
    inside = (places >= leading) & (places < finish)
    flipped = (jax.random.randint(third_key, (ROWS, ROW_LEN), 0, 4) == 0) | (row_index == 0)
    starts = (places == 0) | (places == leading) | (places == finish) | flipped & jnp.logical_not(inside)
    segment = jnp.cumsum(starts.astype(jnp.int32), axis=1) - 1
    distance = places - leading
    period = POS_ROWS - 2
    regular = inside & (distance % period == 0)
    anchor = ROW_LEN // 2 + TOK_DEV - 1
    forced = inside & (places == anchor)
    guarded = places == anchor + 1
    sprinkled = inside & (distance >= period) & (jax.random.randint(fourth_key, (ROWS, ROW_LEN), 0, 97) == 0) & jnp.logical_not(guarded)
    flags = starts | regular | sprinkled | forced
    return (segment.astype(jnp.int32), flags.astype(jnp.int32))


def draw_segment_ids(key, part):
    shared = layout(key)
    return shared[0]


def draw_restarts(key, part):
    shared = layout(key)
    return shared[1]


def steps_of(stream_key, extent, cuts, low, largest):
    def one(axis_at, blocks):
        heights = jax.random.uniform(jax.random.fold_in(jax.random.fold_in(stream_key, 6), axis_at), (blocks,), jnp.float32, low / len(cuts), largest / len(cuts))
        return jnp.repeat(jnp.exp(heights), extent[axis_at] // blocks).reshape((-1,) + (1,) * (len(extent) - axis_at - 1))

    factor_of = one(*cuts[0])
    for cut in cuts[1:]:
        factor_of = factor_of * one(*cut)
    return factor_of


def normal_values(stream_key, shape, scale, reach, cuts=(), held_as=jnp.bfloat16):
    entries = jax.random.normal(stream_key, shape, jnp.float32) * scale
    if len(cuts) > 0:
        entries = steps_of(stream_key, shape, cuts, -0.22, 0.18) * entries
    return jnp.clip(entries, min=-reach, max=reach).astype(held_as)


def setup_inputs(seed: int = 0) -> dict:
    key_list = jax.random.split(jax.random.key(seed), 21)
    tokens = normal_values(key_list[0], (ROWS, ROW_LEN, D), 1.0, 6.0, ((0, 4), (1, 8)))
    cotangent = normal_values(key_list[1], (ROWS, ROW_LEN, D), 1.0, 6.0, ((0, 4), (1, 8)))
    segment_ids = draw_segment_ids(jax.random.fold_in(key_list[20], 71), 0)
    restarts = draw_restarts(jax.random.fold_in(key_list[20], 71), 0)
    position_table = normal_values(key_list[4], (POS_ROWS, D), 0.5, 3.0)
    query_weight = normal_values(key_list[5], (D, D), D ** -0.5, 0.21875)
    query_bias = normal_values(key_list[6], (D,), 0.5, 3.0)
    key_weight = normal_values(key_list[7], (D, D), D ** -0.5, 0.21875)
    value_weight = normal_values(key_list[8], (D, D), D ** -0.5, 0.21875)
    value_bias = normal_values(key_list[9], (D,), 0.3, 2.0)
    out_weight = normal_values(key_list[10], (D, D), (max(1, D * 32 // ROW_LEN)) ** -0.5, 1.25)
    out_bias = normal_values(key_list[11], (D,), 0.3, 2.0)
    first_gain = jnp.clip(1.0 + 0.1 * jax.random.normal(key_list[12], (D,), jnp.float32), 0.5, 1.5).astype(jnp.bfloat16)
    first_shift = normal_values(key_list[13], (D,), 0.3, 2.0)
    inner_weight = normal_values(key_list[14], (D, FF), D ** -0.5, 0.21875)
    inner_bias = normal_values(key_list[15], (FF,), 0.5, 3.0)
    outer_weight = normal_values(key_list[16], (FF, D), FF ** -0.5, 0.109375)
    outer_bias = normal_values(key_list[17], (D,), 0.3, 2.0)
    second_gain = jnp.clip(1.0 + 0.1 * jax.random.normal(key_list[18], (D,), jnp.float32), 0.5, 1.5).astype(jnp.bfloat16)
    second_shift = normal_values(key_list[19], (D,), 0.3, 2.0)
    return {"tokens": tokens, "cotangent": cotangent, "segment_ids": segment_ids, "restarts": restarts, "position_table": position_table, "query_weight": query_weight, "query_bias": query_bias, "key_weight": key_weight, "value_weight": value_weight, "value_bias": value_bias, "out_weight": out_weight, "out_bias": out_bias, "first_gain": first_gain, "first_shift": first_shift, "inner_weight": inner_weight, "inner_bias": inner_bias, "outer_weight": outer_weight, "outer_bias": outer_bias, "second_gain": second_gain, "second_shift": second_shift}


@jax.custom_vjp
def low(v):
    return lax.optimization_barrier(v.astype(jnp.bfloat16)).astype(jnp.float32)

@jax.custom_vjp
def low_back(v):
    return v

def low_keep(v):
    return (low(v), None)

def low_pass(kept, grad):
    return (grad,)

def back_keep(v):
    return (v, None)

def back_low(kept, grad):
    return (low(grad),)
low.defvjp(low_keep, low_pass)
low_back.defvjp(back_keep, back_low)
epsilon = 1e-05

def exact_dot(left, right):
    return jnp.dot(left, right, precision=lax.Precision.HIGHEST, preferred_element_type=jnp.float32)

def layer_norm(value, gain, shift):
    centered = value - lax.optimization_barrier(jnp.mean(value, axis=-1, keepdims=True))
    spread = lax.optimization_barrier(jnp.mean(centered * centered, axis=-1, keepdims=True))
    return centered * lax.rsqrt(spread + epsilon) * gain + shift

def row_attention(queries, keys, values, segments):
    block = math.gcd(ROW_LEN, 512)
    query_blocks = queries.reshape(ROW_LEN // block, block, HEADS, HEAD_DIM)
    segment_blocks = segments.reshape(ROW_LEN // block, block)

    def one_block(pair):
        part, part_segments = pair
        raw = low_back(jnp.einsum('bhd,khd->hbk', part, keys, precision=lax.Precision.HIGHEST))
        scores = raw * HEAD_DIM ** (-0.5)
        allowed = part_segments[None, :, None] == segments[None, None, :]
        scores = jnp.where(allowed, scores, -1e+30)
        highest = lax.optimization_barrier(jnp.max(scores, axis=-1, keepdims=True))
        weights = jnp.exp(scores - highest)
        weights = weights / lax.optimization_barrier(jnp.sum(weights, axis=-1, keepdims=True))
        return jnp.einsum('hbk,khd->bhd', low(weights), values, precision=lax.Precision.HIGHEST)
    result = lax.map(jax.checkpoint(one_block), (query_blocks, segment_blocks))
    return result.reshape(ROW_LEN, HEADS, HEAD_DIM)

def reference(tokens, cotangent, segment_ids, restarts, position_table, query_weight, query_bias, key_weight, value_weight, value_bias, out_weight, out_bias, first_gain, first_shift, inner_weight, inner_bias, outer_weight, outer_bias, second_gain, second_shift):
    places = jnp.arange(ROW_LEN, dtype=jnp.int32)[None, :]
    latest = lax.cummax(jnp.where(restarts == 1, places, -1), axis=1)
    positions = (places - latest + 2).astype(jnp.int32)

    def forward(tokens_f, table_f, wquery, bquery, wkey, wvalue, bvalue, wout, bout, gfirst, sfirst, winner, binner, wouter, bouter, gsecond, ssecond):
        entry = tokens_f + table_f[positions]
        entry_flat = entry.reshape(ROWS * ROW_LEN, D)
        entry_low = low(entry_flat)
        queries = low(low_back(exact_dot(entry_low, wquery) + bquery))
        keys = low(low_back(exact_dot(entry_low, wkey)))
        values = low(low_back(exact_dot(entry_low, wvalue) + bvalue))
        shape4 = (ROWS, ROW_LEN, HEADS, HEAD_DIM)

        def per_row(group):
            return row_attention(group[0], group[1], group[2], group[3])
        attended = lax.map(per_row, (queries.reshape(shape4), keys.reshape(shape4), values.reshape(shape4), segment_ids))
        attended_low = low(low_back(attended.reshape(ROWS * ROW_LEN, D)))
        branch = low_back(exact_dot(attended_low, wout) + bout)
        first = layer_norm(entry_flat + branch, gfirst, sfirst)
        first_low = low(first)
        inner = low_back(exact_dot(first_low, winner) + binner)
        active_low = low(jax.nn.gelu(inner, approximate=False))
        second = low_back(exact_dot(active_low, wouter) + bouter)
        result = layer_norm(first + second, gsecond, ssecond)
        return result.reshape(ROWS, ROW_LEN, D)
    floats = (tokens.astype(jnp.float32), position_table.astype(jnp.float32), query_weight.astype(jnp.float32), query_bias.astype(jnp.float32), key_weight.astype(jnp.float32), value_weight.astype(jnp.float32), value_bias.astype(jnp.float32), out_weight.astype(jnp.float32), out_bias.astype(jnp.float32), first_gain.astype(jnp.float32), first_shift.astype(jnp.float32), inner_weight.astype(jnp.float32), inner_bias.astype(jnp.float32), outer_weight.astype(jnp.float32), outer_bias.astype(jnp.float32), second_gain.astype(jnp.float32), second_shift.astype(jnp.float32))
    result, backward = jax.vjp(forward, *floats)
    grads = backward(cotangent.astype(jnp.float32))
    return (result.astype(jnp.bfloat16), grads[0].astype(jnp.bfloat16), grads[1], grads[2], grads[3], grads[4], grads[5], grads[6], grads[7], grads[8], grads[9], grads[10], grads[11], grads[12], grads[13], grads[14], grads[15], grads[16])
```

```python
from functools import partial
from types import SimpleNamespace

import jax
import jax.numpy as jnp
from jax import lax
from jax.experimental import pallas as pl
from jax.experimental.pallas import tpu as pltpu
from jax.sharding import PartitionSpec as P

MESH = pl.DeviceIdType.MESH
VMEM = pltpu.VMEM
BF, F32, I32 = jnp.bfloat16, jnp.float32, jnp.int32
T, D, F, L, HD = 128, 768, 3072, 1024, 64
EPS = 1e-5
CHANNELS = 200


def dot(a, b, ca=1, cb=0):
    return lax.dot_general(a, b, (((ca,), (cb,)), ((), ())), preferred_element_type=F32)


def ds(start, size, step=None):
    return pl.ds(pl.multiple_of(start, step or size), size)


def scratch():
    s = {}
    s["tok"] = VMEM((8, T, D), BF)
    s["meta"] = VMEM((8, 8, T), I32)
    s["tail"] = VMEM((16, D), BF)
    s["pos"] = VMEM((8, 8, T), I32)
    s["segc"] = VMEM((L, T), F32)
    s["segq"] = VMEM((2, 8, 256), F32)
    s["elow"] = VMEM((8 * T, D), BF)
    s["q3"] = VMEM((3, 512, HD), BF)
    s["k3"] = VMEM((3, L, HD), BF)
    s["v3"] = VMEM((3, L, HD), BF)
    s["pt"] = VMEM((3, L, 512), BF)
    s["att3"] = VMEM((3, 512, HD), BF)
    s["attcat"] = VMEM((4, T, 192), BF)
    s["attg"] = VMEM((4, T, 192), BF)
    s["own"] = VMEM((T, D), F32)
    for n in ("wq", "wk", "wv", "wo"):
        s[n] = VMEM((D, D), BF)
    s["w1"] = VMEM((D, F), BF)
    s["w2"] = VMEM((F, D), BF)
    for n in ("first", "act", "gs", "gi", "gb"):
        s["x" + n] = VMEM((4 * T, D), BF)
    s["xatt"] = VMEM((4 * T, 192), BF)
    s["actout"] = VMEM((4, T, D), BF)
    s["giout"] = VMEM((4, T, D), BF)
    s["gp"] = VMEM((4, T, D), F32)
    s["gfi"] = VMEM((T, D), F32)
    s["gaout"] = VMEM((4, T, 192), BF)
    s["gag"] = VMEM((4, T, 192), BF)
    s["ga3"] = VMEM((3, 512, HD), BF)
    s["dk3"] = VMEM((3, L, HD), F32)
    s["dv3"] = VMEM((3, L, HD), F32)
    s["dq3"] = VMEM((3, 512, HD), BF)
    s["kvs"] = VMEM((512, 384), BF)
    s["kvr"] = VMEM((512, 384), BF)
    s["gqkv"] = VMEM((512, 576), BF)
    s["dqin"] = VMEM((4, T, 576), BF)
    for n, m in (("2", 768), ("1", 768), ("o", 192)):
        s["ys" + n] = VMEM((m, 384), BF)
        s["yr" + n] = VMEM((m, 384), BF)
        s["ac" + n] = VMEM((m, 384), F32)
        s["zs" + n] = VMEM((m, 384), BF)
        s["zr" + n] = VMEM((4, m // 4, 384), BF)
        s["fin" + n] = VMEM((m // 4, 384), BF)
    s["qp"] = VMEM((768, 576), F32)
    for i, m in ((0, 384), (1, 192), (2, 96)):
        s["qs%d" % i] = VMEM((m, 576), BF)
        s["qr%d" % i] = VMEM((m, 576), BF)
    s["finq"] = VMEM((96, 576), BF)
    s["tp"] = VMEM((512, D), F32)
    for i, m in ((0, 256), (1, 128)):
        s["ts%d" % i] = VMEM((m, D), BF)
        s["tr%d" % i] = VMEM((m, D), BF)
    s["ts2"] = VMEM((128, 384), BF)
    s["tr2"] = VMEM((128, 384), BF)
    s["ts3"] = VMEM((128, 384), BF)
    s["tr3"] = VMEM((4, 32, 384), BF)
    s["fint"] = VMEM((32, 384), BF)
    s["sm"] = VMEM((16, D), F32)
    s["sms"] = VMEM((4, 16, D), F32)
    s["smr"] = VMEM((6, 16, D), F32)
    s["wsem"] = pltpu.SemaphoreType.DMA((16,))
    s["ss"] = pltpu.SemaphoreType.DMA((CHANNELS,))
    s["rs"] = pltpu.SemaphoreType.DMA((CHANNELS,))
    return s


INPUTS = ("tokens", "cot", "segs", "rests", "table", "small", "hq", "hk", "hv", "ho", "h1", "h2")
OUTPUTS = ("layer", "gtok", "G2", "G1", "Go", "Gq", "Gt", "Gs")


def kernel(*refs):
    names = INPUTS + OUTPUTS + tuple(scratch())
    R = SimpleNamespace(**dict(zip(names, refs, strict=True)))
    seq, row = lax.axis_index("seq"), lax.axis_index("rows")
    z, y, x, c = seq // 2, seq % 2, row // 2, row % 2
    zk = [(z + k) % 4 for k in range(4)]
    zb = [(z + 4 - k) % 4 for k in range(4)]
    rk = [row, x * 2 + (1 - c), (1 - x) * 2 + c, (1 - x) * 2 + (1 - c)]
    zdev = [(zk[k] * 2 + y, row) for k in range(4)]
    ydev = (z * 2 + (1 - y), row)
    rdev = [(seq, rk[k]) for k in range(4)]
    counter = [0]
    pending = []

    def chan(n=1):
        counter[0] += n
        assert counter[0] <= CHANNELS
        return counter[0] - n

    def copy(src, dst, i, dev):
        return pltpu.make_async_remote_copy(src, dst, R.ss.at[i], R.rs.at[i], device_id=dev, device_id_type=MESH)

    def send(src, dst, i, dev):
        cp = copy(src, dst, i, dev)
        cp.start()
        pending.append(cp)

    def recv(dst, i):
        copy(dst, dst, i, ydev).wait_recv()

    loads = {}
    for i, (h, w) in enumerate((("hk", "wk"), ("hv", "wv"), ("hq", "wq"), ("ho", "wo"), ("h1", "w1"), ("h2", "w2"))):
        cp = pltpu.make_async_copy(getattr(R, h), getattr(R, w), R.wsem.at[i])
        cp.start()
        loads[w] = cp

    me = y * 4 + z
    R.meta[me] = jnp.zeros((8, T), I32)
    R.meta[me, 0:1, :] = R.rests[...]
    R.meta[me, 1:2, :] = R.segs[...]
    R.tok[me] = R.tokens[...]
    seqpeers = [zdev[1], zdev[2], zdev[3]] + [(zk[k] * 2 + (1 - y), row) for k in range(4)]
    peers = seqpeers + rdev[1:]
    bar = pltpu.get_barrier_semaphore()
    for p in peers:
        pl.semaphore_signal(bar, inc=1, device_id=p, device_id_type=MESH)
    pl.semaphore_wait(bar, len(peers))
    cm = chan(7)
    metas = []
    for i, dev in enumerate(seqpeers):
        cp = copy(R.meta.at[me], R.meta.at[me], cm + i, dev)
        cp.start()
        metas.append(cp)
    ct = chan(8)
    for k in (1, 2, 3):
        send(R.tok.at[me], R.tok.at[me], ct + k, zdev[k])
    send(R.tok.at[me], R.tok.at[me], ct + 4, ydev)
    R.tail[...] = jnp.zeros((16, D), BF)
    R.tail[0:2, :] = R.table[512:514, :]
    for cp in metas:
        cp.wait()
    lane = lax.broadcasted_iota(I32, (8, T), 1)
    spot = lax.broadcasted_iota(I32, (8, T), 0) * T + lane
    block_of = [(s % 2) * 4 + s // 2 for s in range(8)]
    flags = jnp.concatenate([R.meta[b, 0:1, :] for b in block_of], axis=0)
    mk = jnp.where(flags == 1, spot, -1)
    k = 1
    while k < T:
        mk = jnp.where(lane >= k, jnp.maximum(mk, pltpu.roll(mk, k, axis=1)), mk)
        k *= 2
    tot = jnp.max(mk, axis=1, keepdims=True)
    carry = jnp.full((1, 1), -1, I32)
    for s, b in enumerate(block_of):
        late = jnp.maximum(mk[s:s + 1, :], carry)
        R.pos[b, 0:1, :] = spot[s:s + 1, :] - late + 2
        carry = jnp.maximum(carry, tot[s:s + 1, :])
    for b in range(8):
        R.segc[b * T:(b + 1) * T, :] = jnp.broadcast_to(R.meta[b, 1:2, :], (T, T)).astype(F32).T
    for j in range(2):
        R.segq[j, 0:1, :] = jnp.concatenate([R.meta[y * 4 + 2 * j + i, 1:2, :] for i in range(2)], axis=1).astype(F32)

    off = pl.multiple_of(128 * ((3 * z) // 2), 128)
    odd = (z % 2) == 1

    def window(v):
        return jnp.where(odd, v[:, 64:256], v[:, 0:192])

    bq = R.small[0:1, pl.ds(off, 256)]
    bv = R.small[1:2, pl.ds(off, 256)]
    for n in ("wk", "wv", "wq"):
        loads[n].wait()

    def hot_of(b, size, start):
        return (lax.broadcasted_iota(I32, (size, T), 0) + start == R.pos[b, 0:1, :]).astype(BF)

    def block(b, with_q):
        e = dot(hot_of(b, 512, 0), R.table[0:512, :], 0, 0) + dot(hot_of(b, 16, 512), R.tail[...], 0, 0)
        e = e + R.tok[b].astype(F32)
        el = e.astype(BF)
        here = ds(b * T, T)
        R.elow[here, :] = el
        kk = window(dot(el, R.wk[:, pl.ds(off, 256)])).astype(BF)
        vv = window(dot(el, R.wv[:, pl.ds(off, 256)]) + bv).astype(BF)
        for h in range(3):
            R.k3[h, here, :] = kk[:, 64 * h:64 * h + 64]
            R.v3[h, here, :] = vv[:, 64 * h:64 * h + 64]
        if with_q:
            qq = (window(dot(el, R.wq[:, pl.ds(off, 256)]) + bq) * 0.125).astype(BF)
            there = ds((b - y * 4) * T, T)
            for h in range(3):
                R.q3[h, there, :] = qq[:, 64 * h:64 * h + 64]
        return e

    R.own[...] = block(me, True)

    def from_z(k, _):
        b = y * 4 + (z + 4 - k) % 4
        recv(R.tok.at[b], ct + k)
        copy(R.tok.at[b], R.tok.at[b], ct + 4 + k, ydev).start()
        block(b, True)
        return 0

    lax.fori_loop(1, 4, from_z, 0)

    def from_y(k, _):
        b = (1 - y) * 4 + (z + 4 - k) % 4
        recv(R.tok.at[b], ct + 4 + k)
        block(b, False)
        return 0

    lax.fori_loop(0, 4, from_y, 0)
    for k in (1, 2, 3):
        b = y * 4 + zb[k]
        copy(R.tok.at[b], R.tok.at[b], ct + 4 + k, ydev).wait_send()

    def attend(i, _):
        h, j = i // 2, i % 2
        qs = ds(j * 256, 256)
        s = dot(R.k3[h], R.q3[h, qs, :], 1, 1)
        sc = R.segc[...]
        s = jnp.where(jnp.concatenate([sc, sc], axis=1) == R.segq[j, 0:1, :], s, -1e30)
        p = jnp.exp(s - jnp.max(s, axis=0, keepdims=True))
        low = (p * (1.0 / jnp.sum(p, axis=0, keepdims=True))).astype(BF)
        R.pt[h, :, qs] = low
        R.att3[h, qs, :] = dot(low, R.v3[h], 0, 0).astype(BF)
        return 0

    lax.fori_loop(0, 6, attend, 0)
    for j in range(4):
        R.attcat[j] = jnp.concatenate([R.att3[h, j * T:(j + 1) * T, :] for h in range(3)], axis=1)
    ca = chan(4)
    for k in (2, 1, 3):
        send(R.attcat.at[zk[k]], R.attg.at[z], ca + k, zdev[k])
    R.attg[z] = R.attcat[z]
    for n in ("wo", "w1", "w2"):
        loads[n].wait()
    for k in (1, 2, 3):
        recv(R.attg.at[zb[k]], ca + k)

    mine = ds(row * T, T)

    def rows_at(k):
        return ds(rk[k] * T, T)

    def small(i):
        return R.small[i:i + 1, :]

    def colsum(v):
        return jnp.sum(v, axis=0, keepdims=True)

    def mean(v):
        return jnp.mean(v, axis=-1, keepdims=True)

    R.sm[...] = jnp.zeros((16, D), F32)
    cx = {n: chan(4) for n in ("first", "act", "att", "gs", "gi", "gb")}

    def share(n, ref):
        send(ref.at[mine, :], ref.at[mine, :], cx[n] + 2, rdev[2])
        send(ref.at[mine, :], ref.at[mine, :], cx[n] + 1, rdev[1])

    def pass_on(n, ref):
        recv(ref.at[rows_at(2), :], cx[n] + 2)
        send(ref.at[rows_at(2), :], ref.at[rows_at(2), :], cx[n] + 3, rdev[1])

    att = jnp.concatenate([R.attg[j] for j in range(4)], axis=1)
    u = R.own[...] + dot(att, R.wo[...]) + small(2)
    u = u - mean(u)
    inv1 = lax.rsqrt(mean(u * u) + EPS)
    n1 = u * inv1
    first = n1 * small(3) + small(4)
    first_low = first.astype(BF)
    R.xfirst[mine, :] = first_low
    share("first", R.xfirst)
    second = jnp.zeros((T, D), F32)
    for k in (2, 3, 1, 0):
        cols = ds(rk[k] * D, D)
        inner = dot(first_low, R.w1[:, cols]) + R.small[pl.ds(8 + rk[k], 1), :]
        phi = 0.5 * (1.0 + lax.erf(inner * 0.7071067811865476))
        R.gp[k] = phi + inner * (0.3989422804014327 * jnp.exp(-0.5 * inner * inner))
        act = (inner * phi).astype(BF)
        if k:
            R.actout[k] = act
            send(R.actout.at[k], R.xact.at[mine, :], cx["act"] + k, rdev[k])
        else:
            R.xact[mine, :] = act
        second = second + dot(act, R.w2[cols, :])
    for k in (1, 2, 3):
        send(R.attg.at[rk[k]], R.xatt.at[mine, :], cx["att"] + k, rdev[k])
    R.xatt[mine, :] = R.attg[row]
    u = first + second + small(5)
    u = u - mean(u)
    inv2 = lax.rsqrt(mean(u * u) + EPS)
    n2 = u * inv2
    R.layer[...] = (n2 * small(6) + small(7)).astype(BF)
    g = R.cot[...].astype(F32)
    R.sm[6:7, :] = colsum(g * n2)
    R.sm[7:8, :] = colsum(g)
    sc = g * small(6)
    gs = inv2 * (sc - mean(sc) - n2 * mean(sc * n2))
    gs_low = gs.astype(BF)
    R.xgs[mine, :] = gs_low
    share("gs", R.xgs)
    R.sm[5:6, :] = colsum(gs_low.astype(F32))
    pass_on("first", R.xfirst)
    for k in (2, 3, 1, 0):
        cols = ds(rk[k] * D, D)
        gi = (dot(gs_low, R.w2[cols, :], 1, 1) * R.gp[k]).astype(BF)
        if k:
            R.giout[k] = gi
            send(R.giout.at[k], R.xgi.at[mine, :], cx["gi"] + k, rdev[k])
        else:
            R.xgi[mine, :] = gi
        R.sm[pl.ds(8 + rk[k], 1), :] = colsum(gi.astype(F32))
        gs = gs + dot(gi, R.w1[:, cols], 1, 1)
    R.sm[3:4, :] = colsum(gs * n1)
    R.sm[4:5, :] = colsum(gs)
    sc = gs * small(3)
    gfi = inv1 * (sc - mean(sc) - n1 * mean(sc * n1))
    R.gfi[...] = gfi
    gb = gfi.astype(BF)
    R.xgb[mine, :] = gb
    share("gb", R.xgb)
    R.sm[2:3, :] = colsum(gb.astype(F32))
    ga = dot(gb, R.wo[...], 1, 1).astype(BF)
    for j in range(4):
        R.gaout[j] = ga[:, 192 * j:192 * j + 192]
    cg = chan(4)
    for k in (2, 1, 3):
        send(R.gaout.at[zk[k]], R.gag.at[z], cg + k, zdev[k])
    R.gag[z] = R.gaout[z]
    pass_on("gs", R.xgs)

    halves = {
        "2": lambda r, yy: R.G2.at[ds(r * 768, 768), ds(yy * 384, 384)],
        "1": lambda r, yy: R.G1.at[:, ds(r * 768 + yy * 384, 384)],
        "o": lambda r, yy: R.Go.at[ds(r * 192, 192), ds(yy * 384, 384)],
        "q": lambda r, yy: R.Gq.at[:, ds((r % 2) * 384 + (r // 2) * 192 + yy * 96, 96), :],
        "t": lambda r, yy: R.Gt.at[ds((r % 2) * 256 + (r // 2) * 128, 128), ds(yy * 384, 384)],
    }
    pieces = {
        "2": lambda zz: R.G2.at[ds(row * 768 + zz * 192, 192), ds(y * 384, 384)],
        "1": lambda zz: R.G1.at[ds(zz * 192, 192), ds(row * 768 + y * 384, 384)],
        "o": lambda zz: R.Go.at[ds(row * 192 + zz * 48, 48), ds(y * 384, 384)],
        "q": lambda zz: R.Gq.at[zz, ds(c * 384 + x * 192 + y * 96, 96), :],
        "t": lambda zz: R.Gt.at[ds(c * 256 + x * 128 + zz * 32, 32), ds(y * 384, 384)],
    }
    cs = {n: chan(15) for n in "21oqt"}

    def stage1(n, lhs, rhs, rows):
        acc, ys, yr = getattr(R, "ac" + n), getattr(R, "ys" + n), getattr(R, "yr" + n)
        step = min(rows, 256)

        def other(i, _):
            m = ds(i * step, step)
            ys[m, :] = dot(lhs[:, m] if rows > step else lhs[...], rhs[:, ds((1 - y) * 384, 384)], 0, 0).astype(BF)
            return 0

        lax.fori_loop(0, rows // step, other, 0)
        send(ys, yr, cs[n], ydev)

        def same(i, _):
            m = ds(i * step, step)
            acc[m, :] = dot(lhs[:, m] if rows > step else lhs[...], rhs[:, ds(y * 384, 384)], 0, 0)
            return 0

        lax.fori_loop(0, rows // step, same, 0)

    def stage2(n, rows):
        acc, zs, yr, zr = (getattr(R, a + n) for a in ("ac", "zs", "yr", "zr"))
        recv(yr, cs[n])
        q = rows // 4
        for k in (2, 1, 3, 0):
            m = ds(zk[k] * q, q)
            v = acc[m, :] + yr[m, :].astype(F32)
            if k:
                zs[m, :] = v.astype(BF)
                send(zs.at[m, :], zr.at[k], cs[n] + k, zdev[k])
            else:
                acc[m, :] = v

    def stage3(n, rows):
        acc, zr, fin = (getattr(R, a + n) for a in ("ac", "zr", "fin"))
        q = rows // 4
        v = acc[ds(z * q, q), :]
        for k in (1, 2, 3):
            recv(zr.at[k], cs[n] + k)
            v = v + zr[k].astype(F32)
        fin[...] = v.astype(BF)
        gatherA(n, fin)

    def gatherA(n, fin):
        for k in (2, 1, 3):
            send(fin, pieces[n](z), cs[n] + 3 + k, zdev[k])
        i = "21oqt".index(n)
        cp = pltpu.make_async_copy(fin, pieces[n](z), R.wsem.at[8 + i])
        cp.start()
        loads["fin" + n] = cp

    def gatherB(n):
        for k in (1, 2, 3):
            recv(pieces[n](zb[k]), cs[n] + 3 + k)
        loads["fin" + n].wait()
        h = halves[n](row, y)
        send(h, h, cs[n] + 7, ydev)
        send(h, h, cs[n] + 8, rdev[2])
        send(h, h, cs[n] + 9, rdev[1])

    def gatherC(n):
        h = halves[n](row, 1 - y)
        recv(h, cs[n] + 7)
        send(h, h, cs[n] + 10, rdev[2])
        send(h, h, cs[n] + 11, rdev[1])

    def gatherD(n):
        h = halves[n](rk[2], y)
        recv(h, cs[n] + 8)
        send(h, h, cs[n] + 12, rdev[1])

    def gatherE(n):
        h = halves[n](rk[2], 1 - y)
        recv(h, cs[n] + 10)
        send(h, h, cs[n] + 13, rdev[1])

    def gatherF(n):
        recv(halves[n](rk[1], y), cs[n] + 9)
        recv(halves[n](rk[1], 1 - y), cs[n] + 11)
        recv(halves[n](rk[3], y), cs[n] + 12)
        recv(halves[n](rk[3], 1 - y), cs[n] + 13)

    def ready(n, ref, forwarded):
        for k in ((1, 3) if forwarded else (1, 2, 3)):
            recv(ref.at[rows_at(k), :], cx[n] + k)

    def backward(h):
        def part(j, _):
            qs = ds(j * 256, 256)
            gah = R.ga3[h, qs, :]
            low = R.pt[h, :, qs]
            p = low.astype(F32)
            pd = p * dot(R.v3[h], gah, 1, 1)
            gr = (pd - p * colsum(pd)).astype(BF)
            dk = dot(gr, R.q3[h, qs, :])
            dv = dot(low, gah)
            R.dk3[h] = jnp.where(j == 0, dk, R.dk3[h] + dk)
            R.dv3[h] = jnp.where(j == 0, dv, R.dv3[h] + dv)
            R.dq3[h, qs, :] = (dot(gr, R.k3[h], 0, 0) * 0.125).astype(BF)
            return 0

        R.dk3[h] = jnp.zeros((L, HD), F32)
        R.dv3[h] = jnp.zeros((L, HD), F32)
        lax.fori_loop(0, 2, part, 0)

    ready("act", R.xact, False)
    ready("gs", R.xgs, True)
    stage1("2", R.xact, R.xgs, 768)
    pass_on("gb", R.xgb)
    for k in (1, 2, 3):
        recv(R.gag.at[zb[k]], cg + k)
    for h in range(3):
        R.ga3[h] = jnp.concatenate([R.gag[j, :, 64 * h:64 * h + 64] for j in range(4)], axis=0)
    backward(0)
    ready("gi", R.xgi, False)
    ready("first", R.xfirst, True)
    stage1("1", R.xfirst, R.xgi, 768)
    stage2("2", 768)
    backward(1)
    ready("att", R.xatt, False)
    ready("gb", R.xgb, True)
    stage1("o", R.xatt, R.xgb, 192)
    stage3("2", 768)
    backward(2)
    ck = chan(1)

    def heads(ref, rows):
        return [ref[h, rows, :] for h in range(3)]

    theirs, ours = ds((1 - y) * 512, 512), ds(y * 512, 512)
    R.kvs[...] = jnp.concatenate(heads(R.dk3, theirs) + heads(R.dv3, theirs), axis=1).astype(BF)
    send(R.kvs, R.kvr, ck, ydev)
    stage2("1", 768)
    gatherB("2")
    stage2("o", 192)
    recv(R.kvr, ck)
    both = jnp.concatenate(heads(R.dk3, ours) + heads(R.dv3, ours), axis=1) + R.kvr[...].astype(F32)
    R.gqkv[...] = jnp.concatenate(heads(R.dq3, slice(None)) + [both.astype(BF)], axis=1)
    cd = chan(4)
    for k in (2, 1, 3):
        send(R.gqkv.at[ds(zk[k] * T, T), :], R.dqin.at[z], cd + k, zdev[k])
    R.dqin[z] = R.gqkv[ds(z * T, T), :]

    def qgrad(i, _):
        m = ds(i * 256, 256)
        R.qp[m, :] = dot(R.elow[ours, m], R.gqkv[...], 0, 0)
        return 0

    lax.fori_loop(0, 3, qgrad, 0)
    cq = cs["q"]
    R.qs0[...] = R.qp[ds((1 - c) * 384, 384), :].astype(BF)
    send(R.qs0, R.qr0, cq, rdev[1])
    stage3("1", 768)
    stage3("o", 192)
    gatherC("2")
    gatherD("2")
    gatherE("2")
    recv(R.qr0, cq)
    base = c * 384
    R.qs1[...] = (R.qp[ds(base + (1 - x) * 192, 192), :] + R.qr0[ds((1 - x) * 192, 192), :].astype(F32)).astype(BF)
    send(R.qs1, R.qr1, cq + 1, rdev[2])
    for k in (1, 2, 3):
        recv(R.dqin.at[zb[k]], cd + k)
    gq, gk, gv = (jnp.concatenate([R.dqin[j, :, 192 * i:192 * i + 192] for j in range(4)], axis=1) for i in range(3))
    R.sm[0:1, :] = colsum(gq.astype(F32))
    R.sm[1:2, :] = colsum(gv.astype(F32))
    ge = R.gfi[...] + dot(gq, R.wq[...], 1, 1) + dot(gk, R.wk[...], 1, 1) + dot(gv, R.wv[...], 1, 1)
    gel = ge.astype(BF)
    R.gtok[...] = gel
    R.tp[...] = dot(hot_of(me, 512, 0), gel)
    R.sm[12:14, :] = dot(hot_of(me, 16, 512), gel)[0:2, :]
    ctb = cs["t"]
    csm = chan(6)
    R.ts0[...] = R.tp[ds((1 - c) * 256, 256), :].astype(BF)
    send(R.ts0, R.tr0, ctb, rdev[1])
    R.sms[0] = R.sm[...]
    send(R.sms.at[0], R.smr.at[0], csm, rdev[1])
    recv(R.qr1, cq + 1)
    base = c * 384 + x * 192
    far, near = (1 - y) * 96, y * 96

    def qsum(o):
        return (R.qp[ds(base + o, 96), :] + R.qr0[ds(x * 192 + o, 96), :].astype(F32)
                + R.qr1[ds(o, 96), :].astype(F32))

    R.qs2[...] = qsum(far).astype(BF)
    send(R.qs2, R.qr2, cq + 2, ydev)
    recv(R.tr0, ctb)
    R.ts1[...] = (R.tp[ds(c * 256 + (1 - x) * 128, 128), :] + R.tr0[ds((1 - x) * 128, 128), :].astype(F32)).astype(BF)
    send(R.ts1, R.tr1, ctb + 1, rdev[2])
    recv(R.smr.at[0], csm)
    R.sms[1] = R.sms[0] + R.smr[0]
    send(R.sms.at[1], R.smr.at[1], csm + 1, rdev[2])
    recv(R.qr2, cq + 2)
    R.finq[...] = (qsum(near) + R.qr2[...].astype(F32)).astype(BF)
    gatherA("q", R.finq)
    gatherB("1")
    gatherB("o")
    recv(R.tr1, ctb + 1)

    def tsum(lanes):
        return (R.tp[ds(c * 256 + x * 128, 128), lanes] + R.tr0[ds(x * 128, 128), lanes].astype(F32)
                + R.tr1[:, lanes].astype(F32))

    R.ts2[...] = tsum(ds((1 - y) * 384, 384)).astype(BF)
    send(R.ts2, R.tr2, ctb + 2, ydev)
    recv(R.smr.at[1], csm + 1)
    R.sms[2] = R.sms[1] + R.smr[1]
    send(R.sms.at[2], R.smr.at[2], csm + 2, ydev)
    gatherC("1")
    gatherC("o")
    gatherB("q")
    recv(R.tr2, ctb + 2)
    tv = tsum(ds(y * 384, 384)) + R.tr2[...].astype(F32)
    R.ts3[...] = tv.astype(BF)
    ctz = chan(4)
    for k in (2, 1, 3):
        send(R.ts3.at[ds(zk[k] * 32, 32), :], R.tr3.at[k], ctz + k, zdev[k])
    recv(R.smr.at[2], csm + 2)
    R.sms[3] = R.sms[2] + R.smr[2]
    for k in (2, 1, 3):
        send(R.sms.at[3], R.smr.at[2 + k], csm + 2 + k, zdev[k])
    tfin = jnp.zeros((32, 384), F32)
    R.tp[0:128, 0:384] = tv
    tfin = R.tp[ds(z * 32, 32), 0:384]
    for k in (1, 2, 3):
        recv(R.tr3.at[k], ctz + k)
        tfin = tfin + R.tr3[k].astype(F32)
    R.fint[...] = tfin.astype(BF)
    gatherA("t", R.fint)
    gatherC("q")
    gatherB("t")
    gatherC("t")
    total = R.sms[3]
    for k in (1, 2, 3):
        recv(R.smr.at[2 + k], csm + 2 + k)
        total = total + R.smr[2 + k]
    R.Gs[...] = total
    for n in "1oqt":
        gatherD(n)
        gatherE(n)
    for n in "21oqt":
        gatherF(n)
    for cp in pending:
        cp.wait_send()


def mega(*args):
    S = jax.ShapeDtypeStruct
    any_, vm = pl.BlockSpec(memory_space=pl.ANY), pl.BlockSpec(memory_space=VMEM)
    return pl.pallas_call(
        kernel,
        out_shape=(S((T, D), BF), S((T, D), BF), S((F, D), BF), S((D, F), BF), S((D, D), BF), S((4, D, 576), BF),
                   S((512, D), BF), S((16, D), F32)),
        in_specs=[vm] * 6 + [any_] * 6,
        out_specs=(vm, vm) + (any_,) * 5 + (vm,),
        scratch_shapes=list(scratch().values()),
        compiler_params=pltpu.CompilerParams(collective_id=0, has_side_effects=True, vmem_limit_bytes=63 << 20),
    )(*args)


def fast_device(tokens, cotangent, segment_ids, restarts, position_table, query_weight, query_bias, key_weight,
                value_weight, value_bias, out_weight, out_bias, first_gain, first_shift, inner_weight, inner_bias,
                outer_weight, outer_bias, second_gain, second_shift):
    vectors = (query_bias, value_bias, out_bias, first_gain, first_shift, outer_bias, second_gain, second_shift)
    small = jnp.concatenate([v.astype(F32) for v in vectors] + [inner_bias.astype(F32), jnp.zeros((4 * D,), F32)])
    layer, gtok, g2, g1, go, gq, gt, gs = mega(
        tokens[0], cotangent[0], segment_ids, restarts, position_table, small.reshape(16, D), query_weight,
        key_weight, value_weight, out_weight, inner_weight, outer_weight)

    def heads(i):
        return jnp.swapaxes(gq[:, :, 192 * i:192 * i + 192], 0, 1).reshape(D, D).astype(F32)

    table = jnp.concatenate([gt.astype(F32), gs[12:14]], axis=0)
    return (layer[None], gtok[None], table, heads(0), gs[0], heads(1), heads(2), gs[1], go.astype(F32), gs[2], gs[3],
            gs[4], g1.astype(F32), gs[8:12].reshape(F), g2.astype(F32), gs[5], gs[6], gs[7])


HEADS = 12


epsilon = 1e-05


def carried_in(array, axis, combine, identity):
    count, place = (lax.axis_size(axis), lax.axis_index(axis))
    everything = lax.all_gather(array, axis)
    start = jnp.broadcast_to(jnp.asarray(identity, array.dtype), array.shape)

    def hop(k, before):
        reached = k < place
        new = combine(before, everything[k])
        return jnp.where(reached, new, before)

    return lax.fori_loop(0, count, hop, start)


def matmul(left, right):
    return jnp.dot(left, right, preferred_element_type=jnp.float32)


def matmul_t(left, right):
    return lax.dot_general(
        left, right, (((1,), (1,)), ((), ())), preferred_element_type=jnp.float32
    )


def outer_sum(left, right):
    return lax.dot_general(
        left, right, (((0,), (0,)), ((), ())), preferred_element_type=jnp.float32
    )


def norm_forward(value, gain, shift):
    centered = value - jnp.mean(value, axis=-1, keepdims=True)
    spread = jnp.mean(centered * centered, axis=-1, keepdims=True)
    inverse = lax.rsqrt(spread + epsilon)
    normal = centered * inverse
    return (normal * gain.astype(jnp.float32) + shift.astype(jnp.float32), normal, inverse)


def norm_backward(incoming, normal, inverse, gain):
    scaled = incoming * gain.astype(jnp.float32)
    centred = scaled - jnp.mean(scaled, axis=-1, keepdims=True)
    outgoing = inverse * (centred - normal * jnp.mean(scaled * normal, axis=-1, keepdims=True))
    return (outgoing, jnp.sum(incoming * normal, axis=0), jnp.sum(incoming, axis=0))


def block_size(key_count):
    for option in (1024, 512):
        return option
    return key_count


def make_forward(queries, query_segs, score_scale):
    rows_here, tok_count, head_count, head_depth = queries.shape

    def step(carry, piece, start):
        key_rows, value_rows, key_segs = piece
        key_count = key_rows.shape[1]
        size = block_size(key_count)

        def one_block(index, state):
            highest, denom, accum = state
            begin = index * size
            keys_blk = lax.dynamic_slice_in_dim(key_rows, begin, size, 1).reshape(
                rows_here, size, head_count, head_depth
            )
            values_blk = lax.dynamic_slice_in_dim(value_rows, begin, size, 1).reshape(
                rows_here, size, head_count, head_depth
            )
            segs_blk = lax.dynamic_slice_in_dim(key_segs, begin, size, 1)
            scores = (
                jnp.einsum("rqhd,rkhd->rhqk", queries, keys_blk, preferred_element_type=jnp.float32)
                * score_scale
            )
            allowed = query_segs[:, None, :, None] == segs_blk[:, None, None, :]
            scores = jnp.where(allowed, scores, -jnp.inf)
            newest = jnp.maximum(highest, jnp.max(scores, axis=-1))
            weights = jnp.exp(scores - newest[..., None])
            factor = jnp.exp(highest - newest)
            denom = denom * factor + jnp.sum(weights, axis=-1)
            update = jnp.einsum(
                "rhqk,rkhd->rqhd",
                weights.astype(jnp.bfloat16),
                values_blk,
                preferred_element_type=jnp.float32,
            )
            accum = accum * jnp.swapaxes(factor, 1, 2)[..., None] + update
            return (newest, denom, accum)

        return lax.fori_loop(0, key_count // size, one_block, carry)

    return step


def make_backward(queries, query_segs, grad_attend, delta, logsum, score_scale):
    rows_here, tok_count, head_count, head_depth = queries.shape

    def step(carry, piece, start):
        key_rows, value_rows, key_segs = piece
        key_count = key_rows.shape[1]
        size = block_size(key_count)

        def one_block(index, state):
            begin = index * size
            keys_blk = lax.dynamic_slice_in_dim(key_rows, begin, size, 1).reshape(
                rows_here, size, head_count, head_depth
            )
            values_blk = lax.dynamic_slice_in_dim(value_rows, begin, size, 1).reshape(
                rows_here, size, head_count, head_depth
            )
            segs_blk = lax.dynamic_slice_in_dim(key_segs, begin, size, 1)
            scores = (
                jnp.einsum("rqhd,rkhd->rhqk", queries, keys_blk, preferred_element_type=jnp.float32)
                * score_scale
            )
            allowed = query_segs[:, None, :, None] == segs_blk[:, None, None, :]
            scores = jnp.where(allowed, scores, -jnp.inf)
            probs = jnp.exp(scores - logsum[..., None])
            grad_p = jnp.einsum(
                "rqhd,rkhd->rhqk", grad_attend, values_blk, preferred_element_type=jnp.float32
            )
            grad_s = (probs * (grad_p - delta[..., None]) * score_scale).astype(jnp.bfloat16)
            grad_q = state[0] + jnp.einsum(
                "rhqk,rkhd->rqhd", grad_s, keys_blk, preferred_element_type=jnp.float32
            )
            grad_k, grad_v = (state[1], state[2])
            grad_v_blk = jnp.einsum(
                "rhqk,rqhd->rkhd",
                probs.astype(jnp.bfloat16),
                grad_attend,
                preferred_element_type=jnp.float32,
            )
            grad_k_blk = jnp.einsum(
                "rhqk,rqhd->rkhd", grad_s, queries, preferred_element_type=jnp.float32
            )
            grad_k = lax.dynamic_update_slice_in_dim(
                grad_k, grad_k_blk.reshape(rows_here, size, head_count * head_depth), begin, 1
            )
            grad_v = lax.dynamic_update_slice_in_dim(
                grad_v, grad_v_blk.reshape(rows_here, size, head_count * head_depth), begin, 1
            )
            return (grad_q, grad_k, grad_v)

        return lax.fori_loop(0, key_count // size, one_block, carry)

    return step


def per_device(
    tokens,
    cotangent,
    segment_ids,
    restarts,
    position_table,
    query_weight,
    query_bias,
    key_weight,
    value_weight,
    value_bias,
    out_weight,
    out_bias,
    first_gain,
    first_shift,
    inner_weight,
    inner_bias,
    outer_weight,
    outer_bias,
    second_gain,
    second_shift,
):
    rows_here, tok_count, model_width = tokens.shape
    head_count = HEADS
    head_depth = model_width // head_count
    score_scale = head_depth ** (-0.5)
    flat_count = rows_here * tok_count
    row_length = tok_count * lax.axis_size("seq")
    offset = lax.axis_index("seq") * tok_count
    places = offset + jnp.arange(tok_count, dtype=jnp.int32)[None, :]
    marked = jnp.where(restarts == 1, places, -1)
    earlier = carried_in(
        jnp.max(marked, axis=1), "seq", jnp.maximum, jnp.full((rows_here,), -1, jnp.int32)
    )
    latest = jnp.maximum(lax.cummax(marked, axis=1), earlier[:, None])
    positions = places - latest + 2
    onehot = (
        positions.reshape(flat_count, 1)
        == jnp.arange(position_table.shape[0], dtype=jnp.int32)[None, :]
    )
    entry = tokens.reshape(flat_count, model_width).astype(jnp.float32) + matmul(
        onehot.astype(jnp.bfloat16), position_table
    )
    entry_low = entry.astype(jnp.bfloat16)
    queries = (matmul(entry_low, query_weight) + query_bias.astype(jnp.float32)).astype(
        jnp.bfloat16
    )
    keys_low = matmul(entry_low, key_weight).astype(jnp.bfloat16)
    values_low = (matmul(entry_low, value_weight) + value_bias.astype(jnp.float32)).astype(
        jnp.bfloat16
    )
    query_heads = queries.reshape(rows_here, tok_count, head_count, head_depth)
    key_rows = keys_low.reshape(rows_here, tok_count, model_width)
    value_rows = values_low.reshape(rows_here, tok_count, model_width)
    start_state = (
        jnp.full((rows_here, head_count, tok_count), -1e30, jnp.float32),
        jnp.zeros((rows_here, head_count, tok_count), jnp.float32),
        jnp.zeros((rows_here, tok_count, head_count, head_depth), jnp.float32),
    )
    forward_step = make_forward(query_heads, segment_ids, score_scale)
    highest, denom, accum = forward_step(
        start_state,
        (
            lax.all_gather(key_rows, "seq", axis=1, tiled=True),
            lax.all_gather(value_rows, "seq", axis=1, tiled=True),
            lax.all_gather(segment_ids, "seq", axis=1, tiled=True),
        ),
        jnp.int32(0),
    )
    attend = accum / jnp.swapaxes(denom, 1, 2)[..., None]
    logsum = highest + jnp.log(denom)
    attended_low = attend.reshape(flat_count, model_width).astype(jnp.bfloat16)
    branch = matmul(attended_low, out_weight) + out_bias.astype(jnp.float32)
    first, first_normal, first_inverse = norm_forward(entry + branch, first_gain, first_shift)
    first_low = first.astype(jnp.bfloat16)
    inner = matmul(first_low, inner_weight) + inner_bias.astype(jnp.float32)
    activation, gelu_back = jax.vjp(partial(jax.nn.gelu, approximate=False), inner)
    active_low = activation.astype(jnp.bfloat16)
    second_in = first + matmul(active_low, outer_weight) + outer_bias.astype(jnp.float32)
    result, second_normal, second_inverse = norm_forward(second_in, second_gain, second_shift)
    layer_out = result.astype(jnp.bfloat16).reshape(rows_here, tok_count, model_width)
    incoming = cotangent.reshape(flat_count, model_width).astype(jnp.float32)
    grad_second, grad_gsecond, grad_ssecond = norm_backward(
        incoming, second_normal, second_inverse, second_gain
    )
    grad_second_low = grad_second.astype(jnp.bfloat16)
    grad_wouter = outer_sum(active_low, grad_second_low)
    grad_bouter = jnp.sum(grad_second_low.astype(jnp.float32), axis=0)
    grad_inner_low = gelu_back(matmul_t(grad_second_low, outer_weight))[0].astype(jnp.bfloat16)
    grad_winner = outer_sum(first_low, grad_inner_low)
    grad_binner = jnp.sum(grad_inner_low.astype(jnp.float32), axis=0)
    grad_first = grad_second + matmul_t(grad_inner_low, inner_weight)
    grad_first_in, grad_gfirst, grad_sfirst = norm_backward(
        grad_first, first_normal, first_inverse, first_gain
    )
    grad_branch_low = grad_first_in.astype(jnp.bfloat16)
    grad_wout = outer_sum(attended_low, grad_branch_low)
    grad_bout = jnp.sum(grad_branch_low.astype(jnp.float32), axis=0)
    grad_attend = (
        matmul_t(grad_branch_low, out_weight)
        .astype(jnp.bfloat16)
        .reshape(rows_here, tok_count, head_count, head_depth)
    )
    delta_rows = jnp.sum(grad_attend.astype(jnp.float32) * attend, axis=-1)
    delta = jnp.swapaxes(delta_rows, 1, 2)
    query_zero = jnp.zeros((rows_here, tok_count, head_count, head_depth), jnp.float32)
    back_state = (
        query_zero,
        jnp.zeros((rows_here, row_length, model_width), jnp.float32),
        jnp.zeros((rows_here, row_length, model_width), jnp.float32),
    )
    backward_step = make_backward(query_heads, segment_ids, grad_attend, delta, logsum, score_scale)
    back_out = backward_step(
        back_state,
        (
            lax.all_gather(key_rows, "seq", axis=1, tiled=True),
            lax.all_gather(value_rows, "seq", axis=1, tiled=True),
            lax.all_gather(segment_ids, "seq", axis=1, tiled=True),
        ),
        jnp.int32(0),
    )
    grad_q = back_out[0]
    grad_keys, grad_values = (
        lax.psum_scatter(back_out[1], "seq", scatter_dimension=1, tiled=True),
        lax.psum_scatter(back_out[2], "seq", scatter_dimension=1, tiled=True),
    )
    grad_query_low = grad_q.reshape(flat_count, model_width).astype(jnp.bfloat16)
    grad_key_low = grad_keys.reshape(flat_count, model_width).astype(jnp.bfloat16)
    grad_value_low = grad_values.reshape(flat_count, model_width).astype(jnp.bfloat16)
    grad_entry = (
        grad_first_in
        + matmul_t(grad_query_low, query_weight)
        + matmul_t(grad_key_low, key_weight)
        + matmul_t(grad_value_low, value_weight)
    )
    grad_wquery = outer_sum(entry_low, grad_query_low)
    grad_bquery = jnp.sum(grad_query_low.astype(jnp.float32), axis=0)
    grad_wkey = outer_sum(entry_low, grad_key_low)
    grad_wvalue = outer_sum(entry_low, grad_value_low)
    grad_bvalue = jnp.sum(grad_value_low.astype(jnp.float32), axis=0)
    grad_table = lax.dot_general(
        onehot.astype(jnp.float32),
        grad_entry,
        (((0,), (0,)), ((), ())),
        precision=lax.Precision.HIGHEST,
        preferred_element_type=jnp.float32,
    )
    grad_tokens = grad_entry.astype(jnp.bfloat16).reshape(rows_here, tok_count, model_width)
    pieces = (
        lax.psum_scatter(grad_wquery, "seq", scatter_dimension=0, tiled=True),
        lax.psum_scatter(grad_wkey, "seq", scatter_dimension=0, tiled=True),
        lax.psum_scatter(grad_wvalue, "seq", scatter_dimension=0, tiled=True),
        lax.psum_scatter(grad_wout, "seq", scatter_dimension=0, tiled=True),
        lax.psum_scatter(grad_winner, "seq", scatter_dimension=0, tiled=True),
        lax.psum_scatter(grad_wouter, "seq", scatter_dimension=0, tiled=True),
    )
    pieces = (
        lax.psum(pieces[0].astype(jnp.bfloat16), "rows").astype(jnp.float32),
        lax.psum(pieces[1].astype(jnp.bfloat16), "rows").astype(jnp.float32),
        lax.psum(pieces[2].astype(jnp.bfloat16), "rows").astype(jnp.float32),
        lax.psum(pieces[3].astype(jnp.bfloat16), "rows").astype(jnp.float32),
        lax.psum(pieces[4].astype(jnp.bfloat16), "rows").astype(jnp.float32),
        lax.psum(pieces[5].astype(jnp.bfloat16), "rows").astype(jnp.float32),
    )
    total_wquery, total_wkey, total_wvalue, total_wout, total_winner, total_wouter = (
        lax.all_gather(pieces[0].astype(jnp.bfloat16), "seq", axis=0, tiled=True).astype(
            jnp.float32
        ),
        lax.all_gather(pieces[1].astype(jnp.bfloat16), "seq", axis=0, tiled=True).astype(
            jnp.float32
        ),
        lax.all_gather(pieces[2].astype(jnp.bfloat16), "seq", axis=0, tiled=True).astype(
            jnp.float32
        ),
        lax.all_gather(pieces[3].astype(jnp.bfloat16), "seq", axis=0, tiled=True).astype(
            jnp.float32
        ),
        lax.all_gather(pieces[4].astype(jnp.bfloat16), "seq", axis=0, tiled=True).astype(
            jnp.float32
        ),
        lax.all_gather(pieces[5].astype(jnp.bfloat16), "seq", axis=0, tiled=True).astype(
            jnp.float32
        ),
    )
    smalls = lax.psum(
        (
            grad_table,
            grad_bquery,
            grad_bvalue,
            grad_bout,
            grad_gfirst,
            grad_sfirst,
            grad_binner,
            grad_bouter,
            grad_gsecond,
            grad_ssecond,
        ),
        ("seq", "rows"),
    )
    (
        total_table,
        total_bquery,
        total_bvalue,
        total_bout,
        total_gfirst,
        total_sfirst,
        total_binner,
        total_bouter,
        total_gsecond,
        total_ssecond,
    ) = smalls
    return (
        layer_out,
        grad_tokens,
        total_table,
        total_wquery,
        total_bquery,
        total_wkey,
        total_wvalue,
        total_bvalue,
        total_wout,
        total_bout,
        total_gfirst,
        total_sfirst,
        total_winner,
        total_binner,
        total_wouter,
        total_bouter,
        total_gsecond,
        total_ssecond,
    )


def solution(mesh):
    in_specs = (
        P("rows", "seq", None),
        P("rows", "seq", None),
        P("rows", "seq"),
        P("rows", "seq"),
        P(),
        P(),
        P(),
        P(),
        P(),
        P(),
        P(),
        P(),
        P(),
        P(),
        P(),
        P(),
        P(),
        P(),
        P(),
        P(),
    )
    out_specs = (
        P("rows", "seq", None),
        P("rows", "seq", None),
        P(),
        P(),
        P(),
        P(),
        P(),
        P(),
        P(),
        P(),
        P(),
        P(),
        P(),
        P(),
        P(),
        P(),
        P(),
        P(),
    )
    body = fast_device if mesh.shape["seq"] == 8 and mesh.shape["rows"] == 4 else per_device
    return jax.shard_map(
        body, mesh=mesh, in_specs=in_specs, out_specs=out_specs, check_vma=False
    )
```

```python
from functools import partial
from types import SimpleNamespace

import jax
import jax.numpy as jnp
from jax import lax
from jax.experimental import pallas as pl
from jax.experimental.pallas import tpu as pltpu
from jax.sharding import PartitionSpec as P

MESH = pl.DeviceIdType.MESH
VMEM = pltpu.VMEM
BF, F32, I32 = jnp.bfloat16, jnp.float32, jnp.int32
T, D, F, L, HD = 128, 768, 3072, 1024, 64
EPS = 1e-5
CHANNELS = 220
ROWS_OF = {"2a": 384, "2b": 384, "1a": 384, "1b": 384, "o": 192}
STREAMS = tuple(ROWS_OF) + ("q", "t")
ORDER = (
    "gs", "12a", "12b", "in", "h0", "11a", "11b", "gb", "h1", "22a", "1o", "h2", "kv", "21a", "22b", "21b", "32a", "vk", "q0",
    "2o", "31a", "q1", "32b", "B2a", "31b", "3o", "B1a", "q2", "en", "C2a", "C1a", "D2a", "D1a", "B2b", "B1b", "t1", "q3",
    "Bo", "C2b", "C1b", "E2a", "E1a", "t2", "Co", "Bq", "t3", "D2b", "D1b", "Do", "t4", "Cq", "E2b", "E1b", "Eo", "Bt", "Dq",
    "Ct", "Eq", "Dt", "Et", "F2a", "F1a", "F2b", "F1b", "Fo", "as", "Ft")


def dot(a, b, ca=1, cb=0):
    return lax.dot_general(a, b, (((ca,), (cb,)), ((), ())), preferred_element_type=F32)


def ds(start, size, step=None):
    return pl.ds(pl.multiple_of(start, step or size), size)


def scratch():
    s = {}
    s["tok"] = VMEM((8, T, D), BF)
    s["meta"] = VMEM((8, 8, T), I32)
    s["tail"] = VMEM((16, D), BF)
    s["table"] = VMEM((514, D), BF)
    s["cot"] = VMEM((T, D), BF)
    s["pos"] = VMEM((8, 8, T), I32)
    s["segc"] = VMEM((L, T), F32)
    s["segq"] = VMEM((2, 8, 256), F32)
    s["elow"] = VMEM((4 * T, D), BF)
    s["q3"] = VMEM((3, 512, HD), BF)
    s["k3"] = VMEM((3, L, HD), BF)
    s["v3"] = VMEM((3, L, HD), BF)
    s["pt"] = VMEM((3, L, 512), BF)
    s["stat"] = VMEM((3, 2, 8, 256), F32)
    s["half"] = VMEM((3, HD, 512), F32)
    s["attcat"] = VMEM((4, 192, T), BF)
    s["attg"] = VMEM((4, 192, T), BF)
    s["own"] = VMEM((T, D), F32)
    for n in ("first", "act", "gs", "gi", "gb"):
        s["x" + n] = VMEM((4 * T, D), BF)
    s["xatt"] = VMEM((192, 4 * T), BF)
    s["gp"] = VMEM((4 * T, D), F32)
    s["gaout"] = VMEM((4, T, 192), BF)
    s["gag"] = VMEM((4, T, 192), BF)
    s["ga3"] = VMEM((3, 512, HD), BF)
    s["dk"] = VMEM((L, HD), F32)
    s["dv"] = VMEM((L, HD), F32)
    s["kvo"] = VMEM((512, 384), F32)
    s["kvs"] = VMEM((512, 384), BF)
    s["kvr"] = VMEM((512, 384), BF)
    s["gqkv"] = VMEM((512, 576), BF)
    s["dqin"] = VMEM((4, T, 576), BF)
    for n, m in ROWS_OF.items():
        s["bs" + n] = VMEM((m, 384), BF)
        s["br" + n] = VMEM((m, 384), BF)
        s["ac" + n] = VMEM((m, 384), F32)
        s["zr" + n] = VMEM((3, m // 4, 384), BF)
    s["qp"] = VMEM((384, 576), F32)
    for i, m in ((0, 384), (1, 192), (2, 96)):
        s["qs%d" % i] = VMEM((m, 576), BF)
        s["qr%d" % i] = VMEM((m, 576), BF)
    s["Gq"] = VMEM((4, D, 576), BF)
    for i, m in ((0, 256), (1, 128)):
        s["ts%d" % i] = VMEM((m, D), BF)
        s["tr%d" % i] = VMEM((m, D), BF)
    s["ts2"] = VMEM((128, 384), BF)
    s["tr2"] = VMEM((128, 384), BF)
    s["ts3"] = VMEM((128, 384), BF)
    s["tr3"] = VMEM((4, 32, 384), BF)
    s["sm"] = VMEM((16, D), F32)
    s["sms"] = VMEM((4, 16, D), F32)
    s["smr"] = VMEM((6, 16, D), F32)
    s["wsem"] = pltpu.SemaphoreType.DMA((9,))
    s["ss"] = pltpu.SemaphoreType.DMA((CHANNELS,))
    s["rs"] = pltpu.SemaphoreType.DMA((CHANNELS,))
    return s


INPUTS = ("tokens", "hcot", "segs", "rests", "htable", "small", "hq", "hk", "hv", "ho", "h1", "h2")
OUTPUTS = ("layer", "gtok", "G2", "G1", "Go", "Gwq", "Gwk", "Gwv", "Gt", "Gs")


def kernel(*refs):
    names = INPUTS + OUTPUTS + tuple(scratch())
    R = SimpleNamespace(**dict(zip(names, refs, strict=True)))
    seq, row = lax.axis_index("seq"), lax.axis_index("rows")
    z, y, x, c = seq // 2, seq % 2, row // 2, row % 2
    zk = [(z + k) % 4 for k in range(4)]
    zb = [(z + 4 - k) % 4 for k in range(4)]
    rk = [row, x * 2 + (1 - c), (1 - x) * 2 + c, (1 - x) * 2 + (1 - c)]
    zdev = [(zk[k] * 2 + y, row) for k in range(4)]
    ydev = (z * 2 + (1 - y), row)
    rdev = [(seq, rk[k]) for k in range(4)]
    counter = [0]
    pending = []

    def chan(n=1):
        counter[0] += n
        assert counter[0] <= CHANNELS
        return counter[0] - n

    def copy(src, dst, i, dev):
        return pltpu.make_async_remote_copy(src, dst, R.ss.at[i], R.rs.at[i], device_id=dev, device_id_type=MESH)

    def send(src, dst, i, dev):
        cp = copy(src, dst, i, dev)
        cp.start()
        pending.append(cp)

    def recv(dst, i):
        copy(dst, dst, i, ydev).wait_recv()

    yxdev = (z * 2 + (1 - y), x * 2 + (1 - c))
    gx = SimpleNamespace(w=[row, *rk[1:]], dev=rdev, b=y, bdev=ydev)
    wy = y * 2 + c
    gy = SimpleNamespace(w=[wy, y * 2 + (1 - c), (1 - y) * 2 + c, (1 - y) * 2 + (1 - c)],
                         dev=[(seq, row), rdev[1], ydev, yxdev], b=x, bdev=rdev[2])
    group = {n: gy if n[0] in "1o" else gx for n in STREAMS}
    group.update(first=gy, gi=gy, att=gy, gb=gy, act=gx, gs=gx)

    loads = {}
    weights = (("n", R.tokens, R.tok.at[y * 4 + z]), ("t", R.htable, R.table), ("k", R.hk, R.Gwk), ("v", R.hv, R.Gwv), ("q", R.hq, R.Gwq), ("c", R.hcot, R.cot), ("o", R.ho, R.Go), ("1", R.h1, R.G1), ("2", R.h2, R.G2))

    def load(i):
        n, src, dst = weights[i]
        loads[n] = pltpu.make_async_copy(src, dst, R.wsem.at[i])
        loads[n].start()

    for i in range(5):
        load(i)

    me = y * 4 + z
    R.meta[me] = jnp.zeros((8, T), I32)
    R.meta[me, 0:1, :] = R.rests[...]
    R.meta[me, 1:2, :] = R.segs[...]
    seqpeers = [zdev[1], zdev[2], zdev[3]] + [(zk[k] * 2 + (1 - y), row) for k in range(4)]
    peers = seqpeers + rdev[1:] + [yxdev]
    bar = pltpu.get_barrier_semaphore()
    for p in peers:
        pl.semaphore_signal(bar, inc=1, device_id=p, device_id_type=MESH)
    pl.semaphore_wait(bar, len(peers))
    loads["n"].wait()
    cm = chan(7)
    metas = []
    for i, dev in enumerate(seqpeers):
        cp = copy(R.meta.at[me], R.meta.at[me], cm + i, dev)
        cp.start()
        metas.append(cp)
    ct = chan(8)
    tokens_out = []

    def forward(b, i, dev):
        tokens_out.append(copy(R.tok.at[b], R.tok.at[b], i, dev))
        tokens_out[-1].start()

    for k in (1, 2, 3):
        forward(me, ct + k, zdev[k])
    forward(me, ct + 4, ydev)
    for i in range(5, 9):
        load(i)
    loads["t"].wait()
    R.tail[...] = jnp.zeros((16, D), BF)
    R.tail[0:2, :] = R.table[512:514, :]
    for cp in metas:
        cp.wait()
    lane = lax.broadcasted_iota(I32, (8, T), 1)
    spot = lax.broadcasted_iota(I32, (8, T), 0) * T + lane
    block_of = [(s % 2) * 4 + s // 2 for s in range(8)]
    flags = jnp.concatenate([R.meta[b, 0:1, :] for b in block_of], axis=0)
    mk = jnp.where(flags == 1, spot, -1)
    k = 1
    while k < T:
        mk = jnp.where(lane >= k, jnp.maximum(mk, pltpu.roll(mk, k, axis=1)), mk)
        k *= 2
    tot = jnp.max(mk, axis=1, keepdims=True)
    carry = jnp.full((1, 1), -1, I32)
    for s, b in enumerate(block_of):
        late = jnp.maximum(mk[s:s + 1, :], carry)
        R.pos[b, 0:1, :] = spot[s:s + 1, :] - late + 2
        carry = jnp.maximum(carry, tot[s:s + 1, :])
    for b in range(8):
        R.segc[b * T:(b + 1) * T, :] = jnp.broadcast_to(R.meta[b, 1:2, :], (T, T)).astype(F32).T
    for j in range(2):
        R.segq[j, 0:1, :] = jnp.concatenate([R.meta[y * 4 + 2 * j + i, 1:2, :] for i in range(2)], axis=1).astype(F32)

    off = pl.multiple_of(128 * ((3 * z) // 2), 128)
    odd = (z % 2) == 1

    def window(v):
        return jnp.where(odd, v[:, 64:256], v[:, 0:192])

    bq = R.small[0:1, pl.ds(off, 256)]
    bv = R.small[1:2, pl.ds(off, 256)]
    for n in "kvq":
        loads[n].wait()

    def hot_of(b, size, start):
        return (lax.broadcasted_iota(I32, (size, T), 0) + start == R.pos[b, 0:1, :]).astype(BF)

    def block(b, with_q):
        e = dot(hot_of(b, 512, 0), R.table[0:512, :], 0, 0) + dot(hot_of(b, 16, 512), R.tail[...], 0, 0)
        e = e + R.tok[b].astype(F32)
        el = e.astype(BF)
        here = ds(b * T, T)
        kk = window(dot(el, R.Gwk[:, pl.ds(off, 256)])).astype(BF)
        vv = window(dot(el, R.Gwv[:, pl.ds(off, 256)]) + bv).astype(BF)
        for h in range(3):
            R.k3[h, here, :] = kk[:, 64 * h:64 * h + 64]
            R.v3[h, here, :] = vv[:, 64 * h:64 * h + 64]
        if with_q:
            qq = (window(dot(el, R.Gwq[:, pl.ds(off, 256)]) + bq) * 0.125).astype(BF)
            there = ds((b - y * 4) * T, T)
            R.elow[there, :] = el
            for h in range(3):
                R.q3[h, there, :] = qq[:, 64 * h:64 * h + 64]
        return e

    R.own[...] = block(me, True)

    for k in (1, 2, 3):
        b = y * 4 + zb[k]
        recv(R.tok.at[b], ct + k)
        forward(b, ct + 4 + k, ydev)
        block(b, True)

    def scores(h, j, parity):
        rows, qs = ds(parity * 512, 512), ds(j * 256, 256)
        s = dot(R.k3[h, rows, :], R.q3[h, qs, :], 1, 1)
        sc = R.segc[rows, :]
        s = jnp.where(jnp.concatenate([sc, sc], axis=1) == R.segq[j, 0:1, :], s, -1e30)
        top = jnp.max(s, axis=0, keepdims=True)
        p = jnp.exp(s - top)
        low = p.astype(BF)
        R.pt[h, rows, qs] = low
        return top, jnp.sum(p, axis=0, keepdims=True), dot(R.v3[h, rows, :], low, 0, 0)

    def attend_near(i, _):
        h, j = i // 2, i % 2
        top, den, acc = scores(h, j, y)
        R.stat[h, j, 2:3, :] = top
        R.stat[h, j, 3:4, :] = den
        R.half[h, :, ds(j * 256, 256)] = acc
        return 0

    def attend_far(i, _):
        h, j = i // 2, i % 2
        top, den, acc = scores(h, j, 1 - y)
        top0 = R.stat[h, j, 2:3, :]
        most = jnp.maximum(top, top0)
        f, f0 = jnp.exp(top - most), jnp.exp(top0 - most)
        inv = 1.0 / (den * f + R.stat[h, j, 3:4, :] * f0)
        f, f0 = f * inv, f0 * inv
        R.stat[h, j, pl.ds(y, 1), :] = f0
        R.stat[h, j, pl.ds(1 - y, 1), :] = f
        qs = ds(j * 256, 256)
        R.half[h, :, qs] = acc * f + R.half[h, :, qs] * f0
        return 0

    lax.fori_loop(0, 6, attend_near, 0)
    for k in (0, 1, 2, 3):
        b = (1 - y) * 4 + zb[k]
        recv(R.tok.at[b], ct + 4 + k)
        block(b, False)
    lax.fori_loop(0, 6, attend_far, 0)
    for j in range(4):
        R.attcat[j] = jnp.concatenate([R.half[h, :, j * T:(j + 1) * T] for h in range(3)], axis=0).astype(BF)
    ca = chan(4)
    for k in (2, 1, 3):
        send(R.attcat.at[zk[k]], R.attg.at[z], ca + k, zdev[k])
    R.attg[z] = R.attcat[z]
    for n in "co12":
        loads[n].wait()
    for cp in tokens_out:
        cp.wait_send()
    for k in (1, 2, 3):
        recv(R.attg.at[zb[k]], ca + k)

    def slot(n, k):
        return ds(group[n].w[k] * T, T)

    def small(i):
        return R.small[i:i + 1, :]

    def colsum(v):
        return jnp.sum(v, axis=0, keepdims=True)

    def mean(v):
        return jnp.mean(v, axis=-1, keepdims=True)

    R.sm[...] = jnp.zeros((16, D), F32)
    cx = {n: chan(4) for n in ("first", "act", "att", "gs", "gi", "gb")}

    def share(n, ref):
        mine = ref.at[slot(n, 0), :]
        send(mine, mine, cx[n] + 2, group[n].dev[2])
        send(mine, mine, cx[n] + 1, group[n].dev[1])

    def pass_on(n, ref):
        theirs = ref.at[slot(n, 2), :]
        recv(theirs, cx[n] + 2)
        send(theirs, theirs, cx[n] + 3, group[n].dev[1])

    u = R.own[...] + dot(jnp.concatenate([R.attg[j] for j in range(4)], axis=0), R.Go[...], 0, 0) + small(2)
    u = u - mean(u)
    inv1 = lax.rsqrt(mean(u * u) + EPS)
    n1 = u * inv1
    first = n1 * small(3) + small(4)
    first_low = first.astype(BF)
    R.xfirst[slot("first", 0), :] = first_low
    share("first", R.xfirst)
    second = jnp.zeros((T, D), F32)
    for k in (2, 3, 1, 0):
        q = gx.w[k]
        cols = ds(q * D, D)
        inner = dot(first_low, R.G1[:, cols]) + R.small[pl.ds(8 + q, 1), :]
        phi = 0.5 * (1.0 + lax.erf(inner * 0.7071067811865476))
        R.gp[ds(q * T, T), :] = phi + inner * (0.3989422804014327 * jnp.exp(-0.5 * inner * inner))
        act = (inner * phi).astype(BF)
        if k:
            R.tok[k] = act
            send(R.tok.at[k], R.xact.at[slot("act", 0), :], cx["act"] + k, gx.dev[k])
        else:
            R.xact[slot("act", 0), :] = act
        second = second + dot(act, R.G2[cols, :])
    for k in (1, 2, 3):
        send(R.attg.at[gy.w[k]], R.xatt.at[:, slot("att", 0)], cx["att"] + k, gy.dev[k])
    R.xatt[:, slot("att", 0)] = R.attg[gy.w[0]]
    u = first + second + small(5)
    u = u - mean(u)
    inv2 = lax.rsqrt(mean(u * u) + EPS)
    n2 = u * inv2
    R.layer[...] = (n2 * small(6) + small(7)).astype(BF)
    g = R.cot[...].astype(F32)
    R.sm[6:7, :] = colsum(g * n2)
    R.sm[7:8, :] = colsum(g)
    sc = g * small(6)
    gs = inv2 * (sc - mean(sc) - n2 * mean(sc * n2))
    gs_low = gs.astype(BF)
    R.xgs[slot("gs", 0), :] = gs_low
    share("gs", R.xgs)
    R.sm[5:6, :] = colsum(gs_low.astype(F32))
    pass_on("first", R.xfirst)
    for k in (2, 3, 1, 0):
        q = gy.w[k]
        cols = ds(q * D, D)
        gi = (dot(gs_low, R.G2[cols, :], 1, 1) * R.gp[ds(q * T, T), :]).astype(BF)
        if k:
            R.tok[4 + k] = gi
            send(R.tok.at[4 + k], R.xgi.at[slot("gi", 0), :], cx["gi"] + k, gy.dev[k])
        else:
            R.xgi[slot("gi", 0), :] = gi
        R.sm[pl.ds(8 + q, 1), :] = colsum(gi.astype(F32))
        gs = gs + dot(gi, R.G1[:, cols], 1, 1)
    R.sm[3:4, :] = colsum(gs * n1)
    R.sm[4:5, :] = colsum(gs)
    sc = gs * small(3)
    gfi = inv1 * (sc - mean(sc) - n1 * mean(sc * n1))
    R.own[...] = gfi
    gb = gfi.astype(BF)
    R.xgb[slot("gb", 0), :] = gb
    ga = dot(gb, R.Go[...], 1, 1).astype(BF)
    for j in range(4):
        R.gaout[j] = ga[:, 192 * j:192 * j + 192]
    cg = chan(4)
    for k in (2, 1, 3):
        send(R.gaout.at[zk[k]], R.gag.at[z], cg + k, zdev[k])
    R.gag[z] = R.gaout[z]
    share("gb", R.xgb)
    R.sm[2:3, :] = colsum(gb.astype(F32))

    def two(h):
        lo = 384 * h
        return (lambda w, b: R.G2.at[ds(w * 768 + lo, 384), ds(b * 384, 384)],
                lambda w, b, zz: R.G2.at[ds(w * 768 + lo + zz * 96, 96), ds(b * 384, 384)])

    def one(h):
        lo = 384 * h
        return (lambda w, b: R.G1.at[lo:lo + 384, ds(w * 768 + b * 384, 384)],
                lambda w, b, zz: R.G1.at[ds(lo + zz * 96, 96), ds(w * 768 + b * 384, 384)])

    regions = {
        "2a": two(0), "2b": two(1), "1a": one(0), "1b": one(1),
        "o": (lambda w, b: R.Go.at[ds(w * 192, 192), ds(b * 384, 384)],
              lambda w, b, zz: R.Go.at[ds(w * 192 + zz * 48, 48), ds(b * 384, 384)]),
        "q": (lambda w, b: R.Gq.at[:, ds((w % 2) * 384 + (w // 2) * 192 + b * 96, 96), :],
              lambda w, b, zz: R.Gq.at[zz, ds((w % 2) * 384 + (w // 2) * 192 + b * 96, 96), :]),
        "t": (lambda w, b: R.Gt.at[ds((w % 2) * 256 + (w // 2) * 128, 128), ds(b * 384, 384)],
              lambda w, b, zz: R.Gt.at[ds((w % 2) * 256 + (w // 2) * 128 + zz * 32, 32), ds(b * 384, 384)]),
    }
    operands = {"2a": (R.xact, 0, R.xgs), "2b": (R.xact, 384, R.xgs), "1a": (R.xfirst, 0, R.xgi), "1b": (R.xfirst, 384, R.xgi)}
    cs = {n: chan(15) for n in STREAMS}
    arrived = set()

    def ready(n, ref, forwarded=True):
        if n not in arrived:
            arrived.add(n)
            for k in ((1, 3) if forwarded else (1, 2, 3)):
                recv(ref.at[:, slot(n, k)] if n == "att" else ref.at[slot(n, k), :], cx[n] + k)

    def stage1(n):
        acc, bs, br = getattr(R, "ac" + n), getattr(R, "bs" + n), getattr(R, "br" + n)
        b = group[n].b
        if n == "o":
            ready("att", R.xatt, False)
            ready("gb", R.xgb)
            bs[...] = dot(R.xatt[...], R.xgb[:, ds((1 - b) * 384, 384)]).astype(BF)
            send(bs, br, cs[n], group[n].bdev)
            acc[...] = dot(R.xatt[...], R.xgb[:, ds(b * 384, 384)])
            return
        if n[0] == "2":
            ready("act", R.xact, False)
            ready("gs", R.xgs)
        else:
            ready("gi", R.xgi, False)
            ready("first", R.xfirst)
        lhs, lo, rhs = operands[n]

        def other(i, _):
            bs[ds(i * 128, 128), :] = dot(lhs[:, ds(lo + i * 128, 128)], rhs[:, ds((1 - b) * 384, 384)], 0, 0).astype(BF)
            return 0

        def same(i, _):
            acc[ds(i * 128, 128), :] = dot(lhs[:, ds(lo + i * 128, 128)], rhs[:, ds(b * 384, 384)], 0, 0)
            return 0

        lax.fori_loop(0, 3, other, 0)
        send(bs, br, cs[n], group[n].bdev)
        lax.fori_loop(0, 3, same, 0)

    def stage2(n):
        acc, br, zr = (getattr(R, a + n) for a in ("ac", "br", "zr"))
        recv(br, cs[n])
        q = ROWS_OF[n] // 4
        for k in (2, 1, 3, 0):
            m = ds(zk[k] * q, q)
            v = acc[m, :] + br[m, :].astype(F32)
            if k:
                br[m, :] = v.astype(BF)
                send(br.at[m, :], zr.at[k - 1], cs[n] + k, zdev[k])
            else:
                acc[m, :] = v

    def stage3(n):
        acc, zr = getattr(R, "ac" + n), getattr(R, "zr" + n)
        q = ROWS_OF[n] // 4
        v = acc[ds(z * q, q), :]
        for k in (1, 2, 3):
            recv(zr.at[k - 1], cs[n] + k)
            v = v + zr[k - 1].astype(F32)
        gatherA(n, v)

    def piece(n, zz):
        return regions[n][1](group[n].w[0], group[n].b, zz)

    def gatherA(n, v):
        p = piece(n, z)
        p[...] = v.astype(BF)
        for k in (2, 1, 3):
            send(p, p, cs[n] + 3 + k, zdev[k])

    def gatherB(n):
        for k in (1, 2, 3):
            recv(piece(n, zb[k]), cs[n] + 3 + k)
        h = regions[n][0](group[n].w[0], group[n].b)
        send(h, h, cs[n] + 8, group[n].dev[2])
        send(h, h, cs[n] + 7, group[n].bdev)
        send(h, h, cs[n] + 9, group[n].dev[1])

    def gatherC(n):
        h = regions[n][0](group[n].w[0], 1 - group[n].b)
        recv(h, cs[n] + 7)
        send(h, h, cs[n] + 10, group[n].dev[2])
        send(h, h, cs[n] + 11, group[n].dev[1])

    def gatherD(n):
        h = regions[n][0](group[n].w[2], group[n].b)
        recv(h, cs[n] + 8)
        send(h, h, cs[n] + 12, group[n].dev[1])

    def gatherE(n):
        h = regions[n][0](group[n].w[2], 1 - group[n].b)
        recv(h, cs[n] + 10)
        send(h, h, cs[n] + 13, group[n].dev[1])

    def gatherF(n):
        g = group[n]
        recv(regions[n][0](g.w[1], g.b), cs[n] + 9)
        recv(regions[n][0](g.w[1], 1 - g.b), cs[n] + 11)
        recv(regions[n][0](g.w[3], g.b), cs[n] + 12)
        recv(regions[n][0](g.w[3], 1 - g.b), cs[n] + 13)

    def heads_in():
        for k in (1, 2, 3):
            recv(R.gag.at[zb[k]], cg + k)
        for h in range(3):
            R.ga3[h] = jnp.concatenate([R.gag[j, :, 64 * h:64 * h + 64] for j in range(4)], axis=0)

    def backward(h):
        def part(j, _):
            qs = ds(j * 256, 256)
            gah = R.ga3[h, qs, :]
            p = jnp.concatenate([R.pt[h, 512 * i:512 * i + 512, qs].astype(F32) * R.stat[h, j, i:i + 1, :]
                                 for i in range(2)], axis=0)
            pd = p * dot(R.v3[h], gah, 1, 1)
            gr = (pd - p * colsum(pd)).astype(BF)
            dk = dot(gr, R.q3[h, qs, :])
            dv = dot(p.astype(BF), gah)
            R.dk[...] = R.dk[...] + dk
            R.dv[...] = R.dv[...] + dv
            R.half[h, :, qs] = dot(R.k3[h], gr, 0, 0) * 0.125
            return 0

        R.dk[...] = jnp.zeros((L, HD), F32)
        R.dv[...] = jnp.zeros((L, HD), F32)
        lax.fori_loop(0, 2, part, 0)
        for ref, lo in ((R.dk, 64 * h), (R.dv, 192 + 64 * h)):
            R.kvs[:, lo:lo + 64] = ref[theirs, :].astype(BF)
            R.kvo[:, lo:lo + 64] = ref[ours, :]

    ck, cd, cq, ctb, csm, ctz = chan(1), chan(4), cs["q"], cs["t"], chan(6), chan(4)
    theirs, ours = ds((1 - y) * 512, 512), ds(y * 512, 512)

    def kv_out():
        send(R.kvs, R.kvr, ck, ydev)

    def kv_in():
        recv(R.kvr, ck)
        kv = (R.kvo[...] + R.kvr[...].astype(F32)).astype(BF)
        gq = jnp.concatenate([R.half[h] for h in range(3)], axis=0).T.astype(BF)
        R.gqkv[...] = jnp.concatenate([gq, kv], axis=1)
        for k in (2, 1, 3):
            send(R.gqkv.at[ds(zk[k] * T, T), :], R.dqin.at[z], cd + k, zdev[k])
        R.dqin[z] = R.gqkv[ds(z * T, T), :]

    def q0():
        def other(i, _):
            R.qs0[ds(i * 128, 128), :] = dot(R.elow[:, ds((1 - c) * 384 + i * 128, 128)], R.gqkv[...], 0, 0).astype(BF)
            return 0

        def same(i, _):
            R.qp[ds(i * 128, 128), :] = dot(R.elow[:, ds(c * 384 + i * 128, 128)], R.gqkv[...], 0, 0)
            return 0

        lax.fori_loop(0, 3, other, 0)
        send(R.qs0, R.qr0, cq, rdev[1])
        lax.fori_loop(0, 3, same, 0)

    def q1():
        recv(R.qr0, cq)
        R.qs1[...] = (R.qp[ds((1 - x) * 192, 192), :]
                      + R.qr0[ds((1 - x) * 192, 192), :].astype(F32)).astype(BF)
        send(R.qs1, R.qr1, cq + 1, rdev[2])

    def qsum(o):
        return (R.qp[ds(x * 192 + o, 96), :] + R.qr0[ds(x * 192 + o, 96), :].astype(F32)
                + R.qr1[ds(o, 96), :].astype(F32))

    def q2():
        recv(R.qr1, cq + 1)
        R.qs2[...] = qsum((1 - y) * 96).astype(BF)
        send(R.qs2, R.qr2, cq + 2, ydev)

    def q3():
        recv(R.qr2, cq + 2)
        gatherA("q", qsum(y * 96) + R.qr2[...].astype(F32))

    def entry():
        for k in (1, 2, 3):
            recv(R.dqin.at[zb[k]], cd + k)
        gq, gk, gv = (jnp.concatenate([R.dqin[j, :, 192 * i:192 * i + 192] for j in range(4)], axis=1) for i in range(3))
        R.sm[0:1, :] = colsum(gq.astype(F32))
        R.sm[1:2, :] = colsum(gv.astype(F32))
        ge = R.own[...] + dot(gq, R.Gwq[...], 1, 1) + dot(gk, R.Gwk[...], 1, 1) + dot(gv, R.Gwv[...], 1, 1)
        gel = ge.astype(BF)
        R.gtok[...] = gel
        R.gp[...] = dot(hot_of(me, 512, 0), gel)
        R.sm[12:14, :] = dot(hot_of(me, 16, 512), gel)[0:2, :]
        R.ts0[...] = R.gp[ds((1 - c) * 256, 256), :].astype(BF)
        send(R.ts0, R.tr0, ctb, rdev[1])
        R.sms[0] = R.sm[...]
        send(R.sms.at[0], R.smr.at[0], csm, rdev[1])

    def t1():
        recv(R.tr0, ctb)
        R.ts1[...] = (R.gp[ds(c * 256 + (1 - x) * 128, 128), :]
                      + R.tr0[ds((1 - x) * 128, 128), :].astype(F32)).astype(BF)
        send(R.ts1, R.tr1, ctb + 1, rdev[2])
        recv(R.smr.at[0], csm)
        R.sms[1] = R.sms[0] + R.smr[0]
        send(R.sms.at[1], R.smr.at[1], csm + 1, rdev[2])

    def tsum(b):
        lanes = ds(b * 384, 384)
        return (R.gp[ds(c * 256 + x * 128, 128), lanes] + R.tr0[ds(x * 128, 128), lanes].astype(F32)
                + R.tr1[:, lanes].astype(F32))

    def t2():
        recv(R.tr1, ctb + 1)
        R.ts2[...] = tsum(1 - y).astype(BF)
        send(R.ts2, R.tr2, ctb + 2, ydev)
        recv(R.smr.at[1], csm + 1)
        R.sms[2] = R.sms[1] + R.smr[1]
        send(R.sms.at[2], R.smr.at[2], csm + 2, ydev)

    def t3():
        recv(R.tr2, ctb + 2)
        tv = tsum(y) + R.tr2[...].astype(F32)
        R.ts3[...] = tv.astype(BF)
        for k in (2, 1, 3):
            send(R.ts3.at[ds(zk[k] * 32, 32), :], R.tr3.at[k], ctz + k, zdev[k])
        R.gp[0:128, 0:384] = tv
        recv(R.smr.at[2], csm + 2)
        R.sms[3] = R.sms[2] + R.smr[2]
        for k in (2, 1, 3):
            send(R.sms.at[3], R.smr.at[2 + k], csm + 2 + k, zdev[k])

    def t4():
        fin = R.gp[ds(z * 32, 32), 0:384]
        for k in (1, 2, 3):
            recv(R.tr3.at[k], ctz + k)
            fin = fin + R.tr3[k].astype(F32)
        gatherA("t", fin)
        total = R.sms[3]
        for k in (1, 2, 3):
            recv(R.smr.at[2 + k], csm + 2 + k)
            total = total + R.smr[2 + k]
        R.Gs[...] = total

    def assemble():
        gatherF("q")

        def part(i, _):
            m = ds(i * 128, 128)
            for t, out in enumerate((R.Gwq, R.Gwk, R.Gwv)):
                out[m, :] = jnp.concatenate([R.Gq[j, m, 192 * t:192 * t + 192] for j in range(4)], axis=1)
            return 0

        lax.fori_loop(0, 6, part, 0)

    tasks = {"gs": lambda: pass_on("gs", R.xgs), "gb": lambda: pass_on("gb", R.xgb), "in": heads_in, "kv": kv_out,
             "vk": kv_in, "q0": q0, "q1": q1, "q2": q2, "q3": q3, "en": entry, "t1": t1, "t2": t2, "t3": t3, "t4": t4,
             "as": assemble}
    for h in range(3):
        tasks["h%d" % h] = partial(backward, h)
    for n in STREAMS:
        for stage, f in zip("123ABCDEF", (stage1, stage2, stage3, None, gatherB, gatherC, gatherD, gatherE, gatherF), strict=True):
            tasks[stage + n] = partial(f, n) if f else None
    for name in ORDER:
        tasks[name]()
    for cp in pending:
        cp.wait_send()


def mega(*args):
    any_, vm = pl.BlockSpec(memory_space=pltpu.HBM), pl.BlockSpec(memory_space=VMEM)
    square = VMEM((D, D), BF)
    return pl.pallas_call(
        kernel,
        out_shape=(VMEM((T, D), BF), VMEM((T, D), BF), VMEM((F, D), BF), VMEM((D, F), BF), square, square, square, square,
                   VMEM((512, D), BF), VMEM((16, D), F32)),
        in_specs=[any_, any_, vm, vm, any_, vm] + [any_] * 6,
        out_specs=(vm,) * 10,
        scratch_shapes=list(scratch().values()),
        compiler_params=pltpu.CompilerParams(collective_id=0, has_side_effects=True, vmem_limit_bytes=41 << 20),
    )(*args)


def finish_kernel(layer, gtok, g2, g1, go, gq, gk, gv, gt, gs, layer_o, gtok_o, t_o, q_o, k_o, v_o, o_o, o1, o2, tab, buf, wide, sem, sem2):
    whole = [pltpu.make_async_copy(a, b, sem2.at[i]) for i, (a, b) in enumerate(((layer, layer_o), (gtok, gtok_o)))]
    for cp in whole:
        cp.start()
    tab[0:512, :] = gt[...].astype(F32)
    tab[512:514, :] = gs[12:14, :]
    whole.append(pltpu.make_async_copy(tab, t_o, sem2.at[2]))
    whole[-1].start()
    chunks = [(g2, o2, buf, i) for i in range(12)] + [(g1, o1, wide, i) for i in range(12)]
    chunks += [(a, b, buf, i) for a, b in ((go, o_o), (gq, q_o), (gk, k_o), (gv, v_o)) for i in range(3)]
    flying = {}
    for n, (src, dst, stage, i) in enumerate(chunks):
        rows = 256 if stage is buf else 64
        slot = n % 4
        if n >= 4:
            flying[slot].wait()
        stage[slot] = src[i * rows:(i + 1) * rows, :].astype(F32)
        flying[slot] = pltpu.make_async_copy(stage.at[slot], dst.at[i * rows:(i + 1) * rows, :], sem.at[slot])
        flying[slot].start()
    for slot in range(4):
        flying[slot].wait()
    for cp in whole:
        cp.wait()


def finish(*args):
    S = jax.ShapeDtypeStruct
    square = S((D, D), F32)
    hbm, vm = pl.BlockSpec(memory_space=pltpu.HBM), pl.BlockSpec(memory_space=VMEM)
    return pl.pallas_call(
        finish_kernel,
        out_shape=(S((T, D), BF), S((T, D), BF), S((514, D), F32), square, square, square, square, S((D, F), F32), S((F, D), F32)),
        in_specs=[vm] * 10,
        out_specs=(hbm,) * 9,
        scratch_shapes=[VMEM((514, D), F32), VMEM((4, 256, D), F32), VMEM((4, 64, F), F32), pltpu.SemaphoreType.DMA((4,)),
                        pltpu.SemaphoreType.DMA((3,))],
        compiler_params=pltpu.CompilerParams(vmem_limit_bytes=20 << 20),
    )(*args)


def fast_device(tokens, cotangent, segment_ids, restarts, position_table, query_weight, query_bias, key_weight,
                value_weight, value_bias, out_weight, out_bias, first_gain, first_shift, inner_weight, inner_bias,
                outer_weight, outer_bias, second_gain, second_shift):
    vectors = (query_bias, value_bias, out_bias, first_gain, first_shift, outer_bias, second_gain, second_shift)
    small, at = jnp.zeros((16 * D,), F32), 0
    for v in vectors + (inner_bias,):
        small = small + jnp.pad(v.astype(F32), (at, 16 * D - at - v.shape[0]))
        at += v.shape[0]
    small = small.reshape(16, D)
    made = mega(
        tokens[0], cotangent[0], segment_ids, restarts, position_table, small, query_weight,
        key_weight, value_weight, out_weight, inner_weight, outer_weight)
    layer, gtok, table, gq, gk, gv, go, g1, g2 = finish(*made)
    gs = made[-1]
    return (layer[None], gtok[None], table, gq, gs[0], gk, gv, gs[1], go, gs[2], gs[3], gs[4], g1, gs[8:12].reshape(F), g2,
            gs[5], gs[6], gs[7])


HEADS = 12


epsilon = 1e-05


def carried_in(array, axis, combine, identity):
    count, place = (lax.axis_size(axis), lax.axis_index(axis))
    everything = lax.all_gather(array, axis)
    start = jnp.broadcast_to(jnp.asarray(identity, array.dtype), array.shape)

    def hop(k, before):
        reached = k < place
        new = combine(before, everything[k])
        return jnp.where(reached, new, before)

    return lax.fori_loop(0, count, hop, start)


def matmul(left, right):
    return jnp.dot(left, right, preferred_element_type=jnp.float32)


def matmul_t(left, right):
    return lax.dot_general(
        left, right, (((1,), (1,)), ((), ())), preferred_element_type=jnp.float32
    )


def outer_sum(left, right):
    return lax.dot_general(
        left, right, (((0,), (0,)), ((), ())), preferred_element_type=jnp.float32
    )


def norm_forward(value, gain, shift):
    centered = value - jnp.mean(value, axis=-1, keepdims=True)
    spread = jnp.mean(centered * centered, axis=-1, keepdims=True)
    inverse = lax.rsqrt(spread + epsilon)
    normal = centered * inverse
    return (normal * gain.astype(jnp.float32) + shift.astype(jnp.float32), normal, inverse)


def norm_backward(incoming, normal, inverse, gain):
    scaled = incoming * gain.astype(jnp.float32)
    centred = scaled - jnp.mean(scaled, axis=-1, keepdims=True)
    outgoing = inverse * (centred - normal * jnp.mean(scaled * normal, axis=-1, keepdims=True))
    return (outgoing, jnp.sum(incoming * normal, axis=0), jnp.sum(incoming, axis=0))


def block_size(key_count):
    for option in (1024, 512):
        return option
    return key_count


def make_forward(queries, query_segs, score_scale):
    rows_here, tok_count, head_count, head_depth = queries.shape

    def step(carry, piece, start):
        key_rows, value_rows, key_segs = piece
        key_count = key_rows.shape[1]
        size = block_size(key_count)

        def one_block(index, state):
            highest, denom, accum = state
            begin = index * size
            keys_blk = lax.dynamic_slice_in_dim(key_rows, begin, size, 1).reshape(
                rows_here, size, head_count, head_depth
            )
            values_blk = lax.dynamic_slice_in_dim(value_rows, begin, size, 1).reshape(
                rows_here, size, head_count, head_depth
            )
            segs_blk = lax.dynamic_slice_in_dim(key_segs, begin, size, 1)
            scores = (
                jnp.einsum("rqhd,rkhd->rhqk", queries, keys_blk, preferred_element_type=jnp.float32)
                * score_scale
            )
            allowed = query_segs[:, None, :, None] == segs_blk[:, None, None, :]
            scores = jnp.where(allowed, scores, -jnp.inf)
            newest = jnp.maximum(highest, jnp.max(scores, axis=-1))
            weights = jnp.exp(scores - newest[..., None])
            factor = jnp.exp(highest - newest)
            denom = denom * factor + jnp.sum(weights, axis=-1)
            update = jnp.einsum(
                "rhqk,rkhd->rqhd",
                weights.astype(jnp.bfloat16),
                values_blk,
                preferred_element_type=jnp.float32,
            )
            accum = accum * jnp.swapaxes(factor, 1, 2)[..., None] + update
            return (newest, denom, accum)

        return lax.fori_loop(0, key_count // size, one_block, carry)

    return step


def make_backward(queries, query_segs, grad_attend, delta, logsum, score_scale):
    rows_here, tok_count, head_count, head_depth = queries.shape

    def step(carry, piece, start):
        key_rows, value_rows, key_segs = piece
        key_count = key_rows.shape[1]
        size = block_size(key_count)

        def one_block(index, state):
            begin = index * size
            keys_blk = lax.dynamic_slice_in_dim(key_rows, begin, size, 1).reshape(
                rows_here, size, head_count, head_depth
            )
            values_blk = lax.dynamic_slice_in_dim(value_rows, begin, size, 1).reshape(
                rows_here, size, head_count, head_depth
            )
            segs_blk = lax.dynamic_slice_in_dim(key_segs, begin, size, 1)
            scores = (
                jnp.einsum("rqhd,rkhd->rhqk", queries, keys_blk, preferred_element_type=jnp.float32)
                * score_scale
            )
            allowed = query_segs[:, None, :, None] == segs_blk[:, None, None, :]
            scores = jnp.where(allowed, scores, -jnp.inf)
            probs = jnp.exp(scores - logsum[..., None])
            grad_p = jnp.einsum(
                "rqhd,rkhd->rhqk", grad_attend, values_blk, preferred_element_type=jnp.float32
            )
            grad_s = (probs * (grad_p - delta[..., None]) * score_scale).astype(jnp.bfloat16)
            grad_q = state[0] + jnp.einsum(
                "rhqk,rkhd->rqhd", grad_s, keys_blk, preferred_element_type=jnp.float32
            )
            grad_k, grad_v = (state[1], state[2])
            grad_v_blk = jnp.einsum(
                "rhqk,rqhd->rkhd",
                probs.astype(jnp.bfloat16),
                grad_attend,
                preferred_element_type=jnp.float32,
            )
            grad_k_blk = jnp.einsum(
                "rhqk,rqhd->rkhd", grad_s, queries, preferred_element_type=jnp.float32
            )
            grad_k = lax.dynamic_update_slice_in_dim(
                grad_k, grad_k_blk.reshape(rows_here, size, head_count * head_depth), begin, 1
            )
            grad_v = lax.dynamic_update_slice_in_dim(
                grad_v, grad_v_blk.reshape(rows_here, size, head_count * head_depth), begin, 1
            )
            return (grad_q, grad_k, grad_v)

        return lax.fori_loop(0, key_count // size, one_block, carry)

    return step


def per_device(
    tokens,
    cotangent,
    segment_ids,
    restarts,
    position_table,
    query_weight,
    query_bias,
    key_weight,
    value_weight,
    value_bias,
    out_weight,
    out_bias,
    first_gain,
    first_shift,
    inner_weight,
    inner_bias,
    outer_weight,
    outer_bias,
    second_gain,
    second_shift,
):
    rows_here, tok_count, model_width = tokens.shape
    head_count = HEADS
    head_depth = model_width // head_count
    score_scale = head_depth ** (-0.5)
    flat_count = rows_here * tok_count
    row_length = tok_count * lax.axis_size("seq")
    offset = lax.axis_index("seq") * tok_count
    places = offset + jnp.arange(tok_count, dtype=jnp.int32)[None, :]
    marked = jnp.where(restarts == 1, places, -1)
    earlier = carried_in(
        jnp.max(marked, axis=1), "seq", jnp.maximum, jnp.full((rows_here,), -1, jnp.int32)
    )
    latest = jnp.maximum(lax.cummax(marked, axis=1), earlier[:, None])
    positions = places - latest + 2
    onehot = (
        positions.reshape(flat_count, 1)
        == jnp.arange(position_table.shape[0], dtype=jnp.int32)[None, :]
    )
    entry = tokens.reshape(flat_count, model_width).astype(jnp.float32) + matmul(
        onehot.astype(jnp.bfloat16), position_table
    )
    entry_low = entry.astype(jnp.bfloat16)
    queries = (matmul(entry_low, query_weight) + query_bias.astype(jnp.float32)).astype(
        jnp.bfloat16
    )
    keys_low = matmul(entry_low, key_weight).astype(jnp.bfloat16)
    values_low = (matmul(entry_low, value_weight) + value_bias.astype(jnp.float32)).astype(
        jnp.bfloat16
    )
    query_heads = queries.reshape(rows_here, tok_count, head_count, head_depth)
    key_rows = keys_low.reshape(rows_here, tok_count, model_width)
    value_rows = values_low.reshape(rows_here, tok_count, model_width)
    start_state = (
        jnp.full((rows_here, head_count, tok_count), -1e30, jnp.float32),
        jnp.zeros((rows_here, head_count, tok_count), jnp.float32),
        jnp.zeros((rows_here, tok_count, head_count, head_depth), jnp.float32),
    )
    forward_step = make_forward(query_heads, segment_ids, score_scale)
    highest, denom, accum = forward_step(
        start_state,
        (
            lax.all_gather(key_rows, "seq", axis=1, tiled=True),
            lax.all_gather(value_rows, "seq", axis=1, tiled=True),
            lax.all_gather(segment_ids, "seq", axis=1, tiled=True),
        ),
        jnp.int32(0),
    )
    attend = accum / jnp.swapaxes(denom, 1, 2)[..., None]
    logsum = highest + jnp.log(denom)
    attended_low = attend.reshape(flat_count, model_width).astype(jnp.bfloat16)
    branch = matmul(attended_low, out_weight) + out_bias.astype(jnp.float32)
    first, first_normal, first_inverse = norm_forward(entry + branch, first_gain, first_shift)
    first_low = first.astype(jnp.bfloat16)
    inner = matmul(first_low, inner_weight) + inner_bias.astype(jnp.float32)
    activation, gelu_back = jax.vjp(partial(jax.nn.gelu, approximate=False), inner)
    active_low = activation.astype(jnp.bfloat16)
    second_in = first + matmul(active_low, outer_weight) + outer_bias.astype(jnp.float32)
    result, second_normal, second_inverse = norm_forward(second_in, second_gain, second_shift)
    layer_out = result.astype(jnp.bfloat16).reshape(rows_here, tok_count, model_width)
    incoming = cotangent.reshape(flat_count, model_width).astype(jnp.float32)
    grad_second, grad_gsecond, grad_ssecond = norm_backward(
        incoming, second_normal, second_inverse, second_gain
    )
    grad_second_low = grad_second.astype(jnp.bfloat16)
    grad_wouter = outer_sum(active_low, grad_second_low)
    grad_bouter = jnp.sum(grad_second_low.astype(jnp.float32), axis=0)
    grad_inner_low = gelu_back(matmul_t(grad_second_low, outer_weight))[0].astype(jnp.bfloat16)
    grad_winner = outer_sum(first_low, grad_inner_low)
    grad_binner = jnp.sum(grad_inner_low.astype(jnp.float32), axis=0)
    grad_first = grad_second + matmul_t(grad_inner_low, inner_weight)
    grad_first_in, grad_gfirst, grad_sfirst = norm_backward(
        grad_first, first_normal, first_inverse, first_gain
    )
    grad_branch_low = grad_first_in.astype(jnp.bfloat16)
    grad_wout = outer_sum(attended_low, grad_branch_low)
    grad_bout = jnp.sum(grad_branch_low.astype(jnp.float32), axis=0)
    grad_attend = (
        matmul_t(grad_branch_low, out_weight)
        .astype(jnp.bfloat16)
        .reshape(rows_here, tok_count, head_count, head_depth)
    )
    delta_rows = jnp.sum(grad_attend.astype(jnp.float32) * attend, axis=-1)
    delta = jnp.swapaxes(delta_rows, 1, 2)
    query_zero = jnp.zeros((rows_here, tok_count, head_count, head_depth), jnp.float32)
    back_state = (
        query_zero,
        jnp.zeros((rows_here, row_length, model_width), jnp.float32),
        jnp.zeros((rows_here, row_length, model_width), jnp.float32),
    )
    backward_step = make_backward(query_heads, segment_ids, grad_attend, delta, logsum, score_scale)
    back_out = backward_step(
        back_state,
        (
            lax.all_gather(key_rows, "seq", axis=1, tiled=True),
            lax.all_gather(value_rows, "seq", axis=1, tiled=True),
            lax.all_gather(segment_ids, "seq", axis=1, tiled=True),
        ),
        jnp.int32(0),
    )
    grad_q = back_out[0]
    grad_keys, grad_values = (
        lax.psum_scatter(back_out[1], "seq", scatter_dimension=1, tiled=True),
        lax.psum_scatter(back_out[2], "seq", scatter_dimension=1, tiled=True),
    )
    grad_query_low = grad_q.reshape(flat_count, model_width).astype(jnp.bfloat16)
    grad_key_low = grad_keys.reshape(flat_count, model_width).astype(jnp.bfloat16)
    grad_value_low = grad_values.reshape(flat_count, model_width).astype(jnp.bfloat16)
    grad_entry = (
        grad_first_in
        + matmul_t(grad_query_low, query_weight)
        + matmul_t(grad_key_low, key_weight)
        + matmul_t(grad_value_low, value_weight)
    )
    grad_wquery = outer_sum(entry_low, grad_query_low)
    grad_bquery = jnp.sum(grad_query_low.astype(jnp.float32), axis=0)
    grad_wkey = outer_sum(entry_low, grad_key_low)
    grad_wvalue = outer_sum(entry_low, grad_value_low)
    grad_bvalue = jnp.sum(grad_value_low.astype(jnp.float32), axis=0)
    grad_table = lax.dot_general(
        onehot.astype(jnp.float32),
        grad_entry,
        (((0,), (0,)), ((), ())),
        precision=lax.Precision.HIGHEST,
        preferred_element_type=jnp.float32,
    )
    grad_tokens = grad_entry.astype(jnp.bfloat16).reshape(rows_here, tok_count, model_width)
    pieces = (
        lax.psum_scatter(grad_wquery, "seq", scatter_dimension=0, tiled=True),
        lax.psum_scatter(grad_wkey, "seq", scatter_dimension=0, tiled=True),
        lax.psum_scatter(grad_wvalue, "seq", scatter_dimension=0, tiled=True),
        lax.psum_scatter(grad_wout, "seq", scatter_dimension=0, tiled=True),
        lax.psum_scatter(grad_winner, "seq", scatter_dimension=0, tiled=True),
        lax.psum_scatter(grad_wouter, "seq", scatter_dimension=0, tiled=True),
    )
    pieces = (
        lax.psum(pieces[0].astype(jnp.bfloat16), "rows").astype(jnp.float32),
        lax.psum(pieces[1].astype(jnp.bfloat16), "rows").astype(jnp.float32),
        lax.psum(pieces[2].astype(jnp.bfloat16), "rows").astype(jnp.float32),
        lax.psum(pieces[3].astype(jnp.bfloat16), "rows").astype(jnp.float32),
        lax.psum(pieces[4].astype(jnp.bfloat16), "rows").astype(jnp.float32),
        lax.psum(pieces[5].astype(jnp.bfloat16), "rows").astype(jnp.float32),
    )
    total_wquery, total_wkey, total_wvalue, total_wout, total_winner, total_wouter = (
        lax.all_gather(pieces[0].astype(jnp.bfloat16), "seq", axis=0, tiled=True).astype(
            jnp.float32
        ),
        lax.all_gather(pieces[1].astype(jnp.bfloat16), "seq", axis=0, tiled=True).astype(
            jnp.float32
        ),
        lax.all_gather(pieces[2].astype(jnp.bfloat16), "seq", axis=0, tiled=True).astype(
            jnp.float32
        ),
        lax.all_gather(pieces[3].astype(jnp.bfloat16), "seq", axis=0, tiled=True).astype(
            jnp.float32
        ),
        lax.all_gather(pieces[4].astype(jnp.bfloat16), "seq", axis=0, tiled=True).astype(
            jnp.float32
        ),
        lax.all_gather(pieces[5].astype(jnp.bfloat16), "seq", axis=0, tiled=True).astype(
            jnp.float32
        ),
    )
    smalls = lax.psum(
        (
            grad_table,
            grad_bquery,
            grad_bvalue,
            grad_bout,
            grad_gfirst,
            grad_sfirst,
            grad_binner,
            grad_bouter,
            grad_gsecond,
            grad_ssecond,
        ),
        ("seq", "rows"),
    )
    (
        total_table,
        total_bquery,
        total_bvalue,
        total_bout,
        total_gfirst,
        total_sfirst,
        total_binner,
        total_bouter,
        total_gsecond,
        total_ssecond,
    ) = smalls
    return (
        layer_out,
        grad_tokens,
        total_table,
        total_wquery,
        total_bquery,
        total_wkey,
        total_wvalue,
        total_bvalue,
        total_wout,
        total_bout,
        total_gfirst,
        total_sfirst,
        total_winner,
        total_binner,
        total_wouter,
        total_bouter,
        total_gsecond,
        total_ssecond,
    )


def solution(mesh):
    in_specs = (
        P("rows", "seq", None),
        P("rows", "seq", None),
        P("rows", "seq"),
        P("rows", "seq"),
        P(),
        P(),
        P(),
        P(),
        P(),
        P(),
        P(),
        P(),
        P(),
        P(),
        P(),
        P(),
        P(),
        P(),
        P(),
        P(),
    )
    out_specs = (
        P("rows", "seq", None),
        P("rows", "seq", None),
        P(),
        P(),
        P(),
        P(),
        P(),
        P(),
        P(),
        P(),
        P(),
        P(),
        P(),
        P(),
        P(),
        P(),
        P(),
        P(),
    )
    body = fast_device if mesh.shape["seq"] == 8 and mesh.shape["rows"] == 4 else per_device
    return jax.shard_map(
        body, mesh=mesh, in_specs=in_specs, out_specs=out_specs, check_vma=False
    )
```

```python
from functools import partial
from types import SimpleNamespace

import jax
import jax.numpy as jnp
from jax import lax
from jax.experimental import pallas as pl
from jax.experimental.pallas import tpu as pltpu
from jax.sharding import PartitionSpec as P

MESH = pl.DeviceIdType.MESH
VMEM = pltpu.VMEM
BF, F32, I32 = jnp.bfloat16, jnp.float32, jnp.int32
T, D, F, L, HD = 128, 768, 3072, 1024, 64
EPS = 1e-5
CHANNELS = 220
ROWS_OF = {"2a": 384, "2b": 384, "1a": 384, "1b": 384, "o": 192}
STREAMS = tuple(ROWS_OF) + ("q", "t")
ORDER = (
    "sb", "gs", "in", "11b", "12b", "11a", "h0", "h1", "12a", "21b", "gb", "h2", "22b", "z1b", "21a", "1o", "31b",
    "z2b", "kv", "z1a", "A1b", "32b", "2o", "B1b", "A2b", "vk", "q0", "q1", "B2b", "31a", "C2b", "D1b", "q2", "C1b",
    "en", "A1a", "zo", "q3", "t1", "B1a", "E1b", "Aq", "t2", "3o", "22a", "Bq", "Ao", "t3", "E2b", "Bo", "z2a", "Cq",
    "t4", "32a", "F1b", "C1a", "At", "A2a", "Do", "B2a", "D2b", "Eq", "Co", "Bt", "E1a", "C2a", "Dq", "Eo", "Ct",
    "Fo", "as", "Dt", "Et", "D2a", "D1a", "F2b", "E2a", "F1a", "Ft", "F2a",
)


def dot(a, b, ca=1, cb=0):
    return lax.dot_general(a, b, (((ca,), (cb,)), ((), ())), preferred_element_type=F32)


def ds(start, size, step=None):
    return pl.ds(pl.multiple_of(start, step or size), size)


def scratch():
    s = {}
    s["tok"] = VMEM((8, T, D), BF)
    s["meta"] = VMEM((8, 8, T), I32)
    s["tail"] = VMEM((16, D), BF)
    s["table"] = VMEM((514, D), BF)
    s["cot"] = VMEM((T, D), BF)
    s["pos"] = VMEM((8, 8, T), I32)
    s["segc"] = VMEM((L, T), F32)
    s["segq"] = VMEM((2, 8, 256), F32)
    s["elow"] = VMEM((4 * T, D), BF)
    s["q3"] = VMEM((3, 512, HD), BF)
    s["k3"] = VMEM((3, L, HD), BF)
    s["v3"] = VMEM((3, L, HD), BF)
    s["pt"] = VMEM((3, L, 512), BF)
    s["stat"] = VMEM((3, 2, 8, 256), F32)
    s["half"] = VMEM((3, HD, 512), F32)
    s["attcat"] = VMEM((4, 192, T), BF)
    s["attg"] = VMEM((4, 192, T), BF)
    s["own"] = VMEM((T, D), F32)
    for n in ("first", "act", "gs", "gi", "gb"):
        s["x" + n] = VMEM((4 * T, D), BF)
    s["xatt"] = VMEM((192, 4 * T), BF)
    s["gp"] = VMEM((4 * T, D), F32)
    s["gaout"] = VMEM((4, T, 192), BF)
    s["gag"] = VMEM((4, T, 192), BF)
    s["ga3"] = VMEM((3, 512, HD), BF)
    s["dk"] = VMEM((L, HD), F32)
    s["dv"] = VMEM((L, HD), F32)
    s["kvo"] = VMEM((512, 384), F32)
    s["kvs"] = VMEM((512, 384), BF)
    s["kvr"] = VMEM((512, 384), BF)
    s["gqkv"] = VMEM((512, 576), BF)
    s["dqin"] = VMEM((4, T, 576), BF)
    for n, m in ROWS_OF.items():
        s["bs" + n] = VMEM((m, 384), BF)
        s["br" + n] = VMEM((m, 384), BF)
        s["ac" + n] = VMEM((m, 384), F32)
        s["zr" + n] = VMEM((3, m // 4, 384), BF)
    s["qp"] = VMEM((384, 576), F32)
    for i, m in ((0, 384), (1, 192), (2, 96)):
        s["qs%d" % i] = VMEM((m, 576), BF)
        s["qr%d" % i] = VMEM((m, 576), BF)
    s["Gq"] = VMEM((4, D, 576), BF)
    for i, m in ((0, 256), (1, 128)):
        s["ts%d" % i] = VMEM((m, D), BF)
        s["tr%d" % i] = VMEM((m, D), BF)
    s["ts2"] = VMEM((128, 384), BF)
    s["tr2"] = VMEM((128, 384), BF)
    s["ts3"] = VMEM((128, 384), BF)
    s["tr3"] = VMEM((4, 32, 384), BF)
    s["sm"] = VMEM((16, D), F32)
    s["sms"] = VMEM((4, 16, D), F32)
    s["smr"] = VMEM((6, 16, D), F32)
    s["wsem"] = pltpu.SemaphoreType.DMA((9,))
    s["ss"] = pltpu.SemaphoreType.DMA((CHANNELS,))
    s["rs"] = pltpu.SemaphoreType.DMA((CHANNELS,))
    return s


INPUTS = ("tokens", "hcot", "segs", "rests", "htable", "small", "hq", "hk", "hv", "ho", "h1", "h2")
OUTPUTS = ("layer", "gtok", "G2", "G1", "Go", "Gwq", "Gwk", "Gwv", "Gt", "Gs")


def kernel(*refs):
    names = INPUTS + OUTPUTS + tuple(scratch())
    R = SimpleNamespace(**dict(zip(names, refs, strict=True)))
    seq, row = lax.axis_index("seq"), lax.axis_index("rows")
    z, y, x, c = seq // 2, seq % 2, row // 2, row % 2
    zk = [z, z + 1 - 2 * (z % 2), (z + 2) % 4, 3 - z]
    rk = [row, x * 2 + (1 - c), (1 - x) * 2 + c, (1 - x) * 2 + (1 - c)]
    zdev = [(zk[k] * 2 + y, row) for k in range(4)]
    ydev = (z * 2 + (1 - y), row)
    rdev = [(seq, rk[k]) for k in range(4)]
    counter = [0]
    pending = []

    def chan(n=1):
        counter[0] += n
        assert counter[0] <= CHANNELS
        return counter[0] - n

    def copy(src, dst, i, dev):
        return pltpu.make_async_remote_copy(src, dst, R.ss.at[i], R.rs.at[i], device_id=dev, device_id_type=MESH)

    def send(src, dst, i, dev):
        cp = copy(src, dst, i, dev)
        cp.start()
        pending.append(cp)

    def recv(dst, i):
        copy(dst, dst, i, ydev).wait_recv()

    yxdev = (z * 2 + (1 - y), x * 2 + (1 - c))
    gx = SimpleNamespace(w=[row, *rk[1:]], dev=rdev, b=y, bdev=ydev)
    wy = y * 2 + c
    gy = SimpleNamespace(w=[wy, y * 2 + (1 - c), (1 - y) * 2 + c, (1 - y) * 2 + (1 - c)],
                         dev=[(seq, row), rdev[1], ydev, yxdev], b=x, bdev=rdev[2])
    group = {n: gy if n[0] in "1ot" else gx for n in STREAMS}
    group.update(first=gy, gi=gy, att=gy, gb=gy, act=gx, gs=gx)

    seqpeers = [zdev[1], zdev[2], zdev[3]] + [(zk[k] * 2 + (1 - y), row) for k in range(4)]
    peers = seqpeers + rdev[1:] + [yxdev]
    bar = pltpu.get_barrier_semaphore()
    for p in peers:
        pl.semaphore_signal(bar, inc=1, device_id=p, device_id_type=MESH)

    loads = {}
    weights = (("n", R.tokens, R.tok.at[y * 4 + z]), ("t", R.htable, R.table), ("k", R.hk, R.Gwk), ("v", R.hv, R.Gwv), ("q", R.hq, R.Gwq), ("c", R.hcot, R.cot), ("o", R.ho, R.Go), ("1", R.h1, R.G1), ("2", R.h2, R.G2))

    def load(i):
        n, src, dst = weights[i]
        loads[n] = pltpu.make_async_copy(src, dst, R.wsem.at[i])
        loads[n].start()

    for i in range(5):
        load(i)

    me = y * 4 + z
    R.meta[me] = jnp.zeros((8, T), I32)
    R.meta[me, 0:1, :] = R.rests[...]
    R.meta[me, 1:2, :] = R.segs[...]
    pl.semaphore_wait(bar, len(peers))
    loads["n"].wait()
    cm = chan(7)
    metas = []
    for i, dev in enumerate(seqpeers):
        cp = copy(R.meta.at[me], R.meta.at[me], cm + i, dev)
        cp.start()
        metas.append(cp)
    ct = chan(8)
    tokens_out = []

    def forward(b, i, dev):
        tokens_out.append(copy(R.tok.at[b], R.tok.at[b], i, dev))
        tokens_out[-1].start()

    forward(me, ct + 1, zdev[1])
    forward(me, ct + 2, zdev[2])
    forward(me, ct + 4, ydev)
    for i in range(5, 9):
        load(i)
    loads["t"].wait()
    R.tail[...] = jnp.zeros((16, D), BF)
    R.tail[0:2, :] = R.table[512:514, :]
    for cp in metas:
        cp.wait()
    lane = lax.broadcasted_iota(I32, (8, T), 1)
    spot = lax.broadcasted_iota(I32, (8, T), 0) * T + lane
    block_of = [(s % 2) * 4 + s // 2 for s in range(8)]
    flags = jnp.concatenate([R.meta[b, 0:1, :] for b in block_of], axis=0)
    mk = jnp.where(flags == 1, spot, -1)
    k = 1
    while k < T:
        mk = jnp.where(lane >= k, jnp.maximum(mk, pltpu.roll(mk, k, axis=1)), mk)
        k *= 2
    tot = jnp.max(mk, axis=1, keepdims=True)
    carry = jnp.full((1, 1), -1, I32)
    for s, b in enumerate(block_of):
        late = jnp.maximum(mk[s:s + 1, :], carry)
        R.pos[b, 0:1, :] = spot[s:s + 1, :] - late + 2
        carry = jnp.maximum(carry, tot[s:s + 1, :])
    for b in range(8):
        R.segc[b * T:(b + 1) * T, :] = jnp.broadcast_to(R.meta[b, 1:2, :], (T, T)).astype(F32).T
    for j in range(2):
        R.segq[j, 0:1, :] = jnp.concatenate([R.meta[y * 4 + 2 * j + i, 1:2, :] for i in range(2)], axis=1).astype(F32)

    off = pl.multiple_of(128 * ((3 * z) // 2), 128)
    odd = (z % 2) == 1

    def window(v):
        return jnp.where(odd, v[:, 64:256], v[:, 0:192])

    bq = R.small[0:1, pl.ds(off, 256)]
    bv = R.small[1:2, pl.ds(off, 256)]
    for n in "kvq":
        loads[n].wait()

    def hot_of(b, size, start):
        return (lax.broadcasted_iota(I32, (size, T), 0) + start == R.pos[b, 0:1, :]).astype(BF)

    def block(b, with_q):
        e = dot(hot_of(b, 512, 0), R.table[0:512, :], 0, 0) + dot(hot_of(b, 16, 512), R.tail[...], 0, 0)
        e = e + R.tok[b].astype(F32)
        el = e.astype(BF)
        here = ds(b * T, T)
        kk = window(dot(el, R.Gwk[:, pl.ds(off, 256)])).astype(BF)
        vv = window(dot(el, R.Gwv[:, pl.ds(off, 256)]) + bv).astype(BF)
        for h in range(3):
            R.k3[h, here, :] = kk[:, 64 * h:64 * h + 64]
            R.v3[h, here, :] = vv[:, 64 * h:64 * h + 64]
        if with_q:
            qq = (window(dot(el, R.Gwq[:, pl.ds(off, 256)]) + bq) * 0.125).astype(BF)
            there = ds((b - y * 4) * T, T)
            R.elow[there, :] = el
            for h in range(3):
                R.q3[h, there, :] = qq[:, 64 * h:64 * h + 64]
        return e

    R.own[...] = block(me, True)

    for k in (1, 2, 3):
        b = y * 4 + zk[k]
        recv(R.tok.at[b], ct + k)
        if k == 2:
            forward(b, ct + 3, zdev[1])
        forward(b, ct + 4 + k, ydev)
        block(b, True)

    def scores(h, j, parity):
        rows, qs = ds(parity * 512, 512), ds(j * 256, 256)
        s = dot(R.k3[h, rows, :], R.q3[h, qs, :], 1, 1)
        sc = R.segc[rows, :]
        s = jnp.where(jnp.concatenate([sc, sc], axis=1) == R.segq[j, 0:1, :], s, -1e30)
        top = jnp.max(s, axis=0, keepdims=True)
        p = jnp.exp(s - top)
        low = p.astype(BF)
        R.pt[h, rows, qs] = low
        return top, jnp.sum(p, axis=0, keepdims=True), dot(R.v3[h, rows, :], low, 0, 0)

    def attend_near(i, _):
        h, j = i // 2, i % 2
        top, den, acc = scores(h, j, y)
        R.stat[h, j, 2:3, :] = top
        R.stat[h, j, 3:4, :] = den
        R.half[h, :, ds(j * 256, 256)] = acc
        return 0

    def attend_far(i, _):
        h, j = i // 2, i % 2
        top, den, acc = scores(h, j, 1 - y)
        top0 = R.stat[h, j, 2:3, :]
        most = jnp.maximum(top, top0)
        f, f0 = jnp.exp(top - most), jnp.exp(top0 - most)
        inv = 1.0 / (den * f + R.stat[h, j, 3:4, :] * f0)
        f, f0 = f * inv, f0 * inv
        R.stat[h, j, pl.ds(y, 1), :] = f0
        R.stat[h, j, pl.ds(1 - y, 1), :] = f
        qs = ds(j * 256, 256)
        R.half[h, :, qs] = acc * f + R.half[h, :, qs] * f0
        return 0

    lax.fori_loop(0, 6, attend_near, 0)
    for k in (0, 1, 2, 3):
        b = (1 - y) * 4 + zk[k]
        recv(R.tok.at[b], ct + 4 + k)
        block(b, False)
    lax.fori_loop(0, 6, attend_far, 0)
    for j in range(4):
        R.attcat[j] = jnp.concatenate([R.half[h, :, j * T:(j + 1) * T] for h in range(3)], axis=0).astype(BF)
    ca = chan(4)
    for k in (2, 1, 3):
        send(R.attcat.at[zk[k]], R.attg.at[z], ca + k, zdev[k])
    R.attg[z] = R.attcat[z]
    for n in "co12":
        loads[n].wait()
    for cp in tokens_out:
        cp.wait_send()
    for k in (1, 2, 3):
        recv(R.attg.at[zk[k]], ca + k)

    def slot(n, k):
        return ds(group[n].w[k] * T, T)

    def small(i):
        return R.small[i:i + 1, :]

    def colsum(v):
        return jnp.sum(v, axis=0, keepdims=True)

    def mean(v):
        return jnp.mean(v, axis=-1, keepdims=True)

    R.sm[...] = jnp.zeros((16, D), F32)
    cx = {n: chan(4) for n in ("first", "act", "att", "gs", "gi", "gb")}

    def share(n, ref):
        mine = ref.at[slot(n, 0), :]
        send(mine, mine, cx[n] + 2, group[n].dev[2])
        send(mine, mine, cx[n] + 1, group[n].dev[1])

    def pass_on(n, ref):
        theirs = ref.at[slot(n, 2), :]
        recv(theirs, cx[n] + 2)
        send(theirs, theirs, cx[n] + 3, group[n].dev[1])

    u = R.own[...] + dot(jnp.concatenate([R.attg[j] for j in range(4)], axis=0), R.Go[...], 0, 0) + small(2)
    u = u - mean(u)
    inv1 = lax.rsqrt(mean(u * u) + EPS)
    n1 = u * inv1
    first = n1 * small(3) + small(4)
    first_low = first.astype(BF)
    R.xfirst[slot("first", 0), :] = first_low
    share("first", R.xfirst)
    second = jnp.zeros((T, D), F32)
    for k in (2, 3, 1, 0):
        q = gx.w[k]
        cols = ds(q * D, D)
        inner = dot(first_low, R.G1[:, cols]) + R.small[pl.ds(8 + q, 1), :]
        phi = 0.5 * (1.0 + lax.erf(inner * 0.7071067811865476))
        R.gp[ds(q * T, T), :] = phi + inner * (0.3989422804014327 * jnp.exp(-0.5 * inner * inner))
        act = (inner * phi).astype(BF)
        if k:
            R.tok[k] = act
            send(R.tok.at[k], R.xact.at[slot("act", 0), :], cx["act"] + k, gx.dev[k])
        else:
            R.xact[slot("act", 0), :] = act
        second = second + dot(act, R.G2[cols, :])
    R.xatt[:, slot("att", 0)] = R.attg[gy.w[0]]
    u = first + second + small(5)
    u = u - mean(u)
    inv2 = lax.rsqrt(mean(u * u) + EPS)
    n2 = u * inv2
    R.layer[...] = (n2 * small(6) + small(7)).astype(BF)
    g = R.cot[...].astype(F32)
    R.sm[6:7, :] = colsum(g * n2)
    R.sm[7:8, :] = colsum(g)
    sc = g * small(6)
    gs = inv2 * (sc - mean(sc) - n2 * mean(sc * n2))
    gs_low = gs.astype(BF)
    R.xgs[slot("gs", 0), :] = gs_low
    share("gs", R.xgs)
    R.sm[5:6, :] = colsum(gs_low.astype(F32))
    pass_on("first", R.xfirst)
    for k in (2, 3, 1, 0):
        q = gy.w[k]
        cols = ds(q * D, D)
        gi = (dot(gs_low, R.G2[cols, :], 1, 1) * R.gp[ds(q * T, T), :]).astype(BF)
        if k:
            R.tok[4 + k] = gi
            send(R.tok.at[4 + k], R.xgi.at[slot("gi", 0), :], cx["gi"] + k, gy.dev[k])
        else:
            R.xgi[slot("gi", 0), :] = gi
        R.sm[pl.ds(8 + q, 1), :] = colsum(gi.astype(F32))
        gs = gs + dot(gi, R.G1[:, cols], 1, 1)
    R.sm[3:4, :] = colsum(gs * n1)
    R.sm[4:5, :] = colsum(gs)
    sc = gs * small(3)
    gfi = inv1 * (sc - mean(sc) - n1 * mean(sc * n1))
    R.own[...] = gfi
    gb = gfi.astype(BF)
    R.xgb[slot("gb", 0), :] = gb
    ga = dot(gb, R.Go[...], 1, 1).astype(BF)
    for j in range(4):
        R.gaout[j] = ga[:, 192 * j:192 * j + 192]
    cg = chan(4)
    for k in (2, 1, 3):
        send(R.gaout.at[zk[k]], R.gag.at[z], cg + k, zdev[k])
    R.gag[z] = R.gaout[z]
    R.sm[2:3, :] = colsum(gb.astype(F32))

    def two(h):
        lo = 384 * h
        return (lambda w, b: R.G2.at[ds(w * 768 + lo, 384), ds(b * 384, 384)],
                lambda w, b, zz: R.G2.at[ds(w * 768 + lo + zz * 96, 96), ds(b * 384, 384)])

    def one(h):
        lo = 384 * h
        return (lambda w, b: R.G1.at[lo:lo + 384, ds(w * 768 + b * 384, 384)],
                lambda w, b, zz: R.G1.at[ds(lo + zz * 96, 96), ds(w * 768 + b * 384, 384)])

    regions = {
        "2a": two(0), "2b": two(1), "1a": one(0), "1b": one(1),
        "o": (lambda w, b: R.Go.at[ds(w * 192, 192), ds(b * 384, 384)],
              lambda w, b, zz: R.Go.at[ds(w * 192 + zz * 48, 48), ds(b * 384, 384)]),
        "q": (lambda w, b: R.Gq.at[:, ds((w % 2) * 384 + (w // 2) * 192 + b * 96, 96), :],
              lambda w, b, zz: R.Gq.at[zz, ds((w % 2) * 384 + (w // 2) * 192 + b * 96, 96), :]),
        "t": (lambda w, b: R.Gt.at[ds((w % 2) * 256 + (w // 2) * 128, 128), ds(b * 384, 384)],
              lambda w, b, zz: R.Gt.at[ds((w % 2) * 256 + (w // 2) * 128 + zz * 32, 32), ds(b * 384, 384)]),
    }
    operands = {"2a": (R.xact, 0, R.xgs), "2b": (R.xact, 384, R.xgs), "1a": (R.xfirst, 0, R.xgi), "1b": (R.xfirst, 384, R.xgi)}
    cs = {n: chan(15) for n in STREAMS}
    arrived = set()

    def ready(n, ref, forwarded=True):
        if n not in arrived:
            arrived.add(n)
            for k in ((1, 3) if forwarded else (1, 2, 3)):
                recv(ref.at[:, slot(n, k)] if n == "att" else ref.at[slot(n, k), :], cx[n] + k)

    def stage1(n):
        acc, bs, br = getattr(R, "ac" + n), getattr(R, "bs" + n), getattr(R, "br" + n)
        b = group[n].b
        if n == "o":
            ready("att", R.xatt, False)
            ready("gb", R.xgb)
            bs[...] = dot(R.xatt[...], R.xgb[:, ds((1 - b) * 384, 384)]).astype(BF)
            send(bs, br, cs[n], group[n].bdev)
            acc[...] = dot(R.xatt[...], R.xgb[:, ds(b * 384, 384)])
            return
        if n[0] == "2":
            ready("act", R.xact, False)
            ready("gs", R.xgs)
        else:
            ready("gi", R.xgi, False)
            ready("first", R.xfirst)
        lhs, lo, rhs = operands[n]

        def other(i, _):
            bs[ds(i * 128, 128), :] = dot(lhs[:, ds(lo + i * 128, 128)], rhs[:, ds((1 - b) * 384, 384)], 0, 0).astype(BF)
            return 0

        def same(i, _):
            acc[ds(i * 128, 128), :] = dot(lhs[:, ds(lo + i * 128, 128)], rhs[:, ds(b * 384, 384)], 0, 0)
            return 0

        lax.fori_loop(0, 3, other, 0)
        send(bs, br, cs[n], group[n].bdev)
        lax.fori_loop(0, 3, same, 0)

    def stage2(n):
        acc, br, zr = (getattr(R, a + n) for a in ("ac", "br", "zr"))
        recv(br, cs[n])
        q = ROWS_OF[n] // 4
        for k in (3, 1, 2, 0):
            m = ds(zk[k] * q, q)
            v = acc[m, :] + br[m, :].astype(F32)
            if k % 2:
                br[m, :] = v.astype(BF)
                send(br.at[m, :], zr.at[k // 2], cs[n] + 1 + k // 2, zdev[1])
            else:
                acc[m, :] = v

    def stage2z(n):
        acc, br, zr = (getattr(R, a + n) for a in ("ac", "br", "zr"))
        recv(zr.at[1], cs[n] + 2)
        q = ROWS_OF[n] // 4
        m = ds(zk[2] * q, q)
        br[m, :] = (acc[m, :] + zr[1].astype(F32)).astype(BF)
        send(br.at[m, :], zr.at[2], cs[n] + 3, zdev[2])

    def stage3(n):
        acc, zr = getattr(R, "ac" + n), getattr(R, "zr" + n)
        q = ROWS_OF[n] // 4
        v = acc[ds(z * q, q), :]
        for i in (0, 2):
            recv(zr.at[i], cs[n] + 1 + i)
            v = v + zr[i].astype(F32)
        gatherA(n, v)

    def piece(n, zz):
        return regions[n][1](group[n].w[0], group[n].b, zz)

    def gatherA(n, v):
        p = piece(n, z)
        p[...] = v.astype(BF)
        send(p, p, cs[n] + 5, zdev[2])
        send(p, p, cs[n] + 4, zdev[1])

    def gatherZ(n):
        p = piece(n, zk[2])
        recv(p, cs[n] + 5)
        send(p, p, cs[n] + 6, zdev[1])

    def gatherB(n):
        for k in (1, 3):
            recv(piece(n, zk[k]), cs[n] + 3 + k)
        h = regions[n][0](group[n].w[0], group[n].b)
        send(h, h, cs[n] + 8, group[n].dev[2])
        send(h, h, cs[n] + 7, group[n].bdev)
        send(h, h, cs[n] + 9, group[n].dev[1])

    def gatherC(n):
        h = regions[n][0](group[n].w[0], 1 - group[n].b)
        recv(h, cs[n] + 7)
        send(h, h, cs[n] + 10, group[n].dev[2])
        send(h, h, cs[n] + 11, group[n].dev[1])

    def gatherD(n):
        h = regions[n][0](group[n].w[2], group[n].b)
        recv(h, cs[n] + 8)
        send(h, h, cs[n] + 12, group[n].dev[1])

    def gatherE(n):
        h = regions[n][0](group[n].w[2], 1 - group[n].b)
        recv(h, cs[n] + 10)
        send(h, h, cs[n] + 13, group[n].dev[1])

    def gatherF(n):
        g = group[n]
        recv(regions[n][0](g.w[1], g.b), cs[n] + 9)
        recv(regions[n][0](g.w[1], 1 - g.b), cs[n] + 11)
        recv(regions[n][0](g.w[3], g.b), cs[n] + 12)
        recv(regions[n][0](g.w[3], 1 - g.b), cs[n] + 13)

    def share_branch():
        for k in (1, 2, 3):
            send(R.attg.at[gy.w[k]], R.xatt.at[:, slot("att", 0)], cx["att"] + k, gy.dev[k])
        share("gb", R.xgb)

    def heads_in():
        for k in (1, 2, 3):
            recv(R.gag.at[zk[k]], cg + k)
        for h in range(3):
            R.ga3[h] = jnp.concatenate([R.gag[j, :, 64 * h:64 * h + 64] for j in range(4)], axis=0)

    def backward(h):
        def part(j, _):
            qs = ds(j * 256, 256)
            gah = R.ga3[h, qs, :]
            p = jnp.concatenate([R.pt[h, 512 * i:512 * i + 512, qs].astype(F32) * R.stat[h, j, i:i + 1, :]
                                 for i in range(2)], axis=0)
            pd = p * dot(R.v3[h], gah, 1, 1)
            gr = (pd - p * colsum(pd)).astype(BF)
            dk = dot(gr, R.q3[h, qs, :])
            dv = dot(p.astype(BF), gah)
            R.dk[...] = R.dk[...] + dk
            R.dv[...] = R.dv[...] + dv
            R.half[h, :, qs] = dot(R.k3[h], gr, 0, 0) * 0.125
            return 0

        R.dk[...] = jnp.zeros((L, HD), F32)
        R.dv[...] = jnp.zeros((L, HD), F32)
        lax.fori_loop(0, 2, part, 0)
        for ref, lo in ((R.dk, 64 * h), (R.dv, 192 + 64 * h)):
            R.kvs[:, lo:lo + 64] = ref[theirs, :].astype(BF)
            R.kvo[:, lo:lo + 64] = ref[ours, :]

    ck, cd, cq, ctb, csm, ctz = chan(1), chan(4), cs["q"], cs["t"], chan(6), chan(4)
    theirs, ours = ds((1 - y) * 512, 512), ds(y * 512, 512)

    def kv_out():
        send(R.kvs, R.kvr, ck, ydev)

    def kv_in():
        recv(R.kvr, ck)
        kv = (R.kvo[...] + R.kvr[...].astype(F32)).astype(BF)
        gq = jnp.concatenate([R.half[h] for h in range(3)], axis=0).T.astype(BF)
        R.gqkv[...] = jnp.concatenate([gq, kv], axis=1)
        for k in (2, 1, 3):
            send(R.gqkv.at[ds(zk[k] * T, T), :], R.dqin.at[z], cd + k, zdev[k])
        R.dqin[z] = R.gqkv[ds(z * T, T), :]

    def q0():
        def other(i, _):
            R.qs0[ds(i * 128, 128), :] = dot(R.elow[:, ds((1 - c) * 384 + i * 128, 128)], R.gqkv[...], 0, 0).astype(BF)
            return 0

        def same(i, _):
            R.qp[ds(i * 128, 128), :] = dot(R.elow[:, ds(c * 384 + i * 128, 128)], R.gqkv[...], 0, 0)
            return 0

        lax.fori_loop(0, 3, other, 0)
        send(R.qs0, R.qr0, cq, rdev[1])
        lax.fori_loop(0, 3, same, 0)

    def q1():
        recv(R.qr0, cq)
        R.qs1[...] = (R.qp[ds((1 - x) * 192, 192), :]
                      + R.qr0[ds((1 - x) * 192, 192), :].astype(F32)).astype(BF)
        send(R.qs1, R.qr1, cq + 1, rdev[2])

    def qsum(o):
        return (R.qp[ds(x * 192 + o, 96), :] + R.qr0[ds(x * 192 + o, 96), :].astype(F32)
                + R.qr1[ds(o, 96), :].astype(F32))

    def q2():
        recv(R.qr1, cq + 1)
        R.qs2[...] = qsum((1 - y) * 96).astype(BF)
        send(R.qs2, R.qr2, cq + 2, ydev)

    def q3():
        recv(R.qr2, cq + 2)
        gatherA("q", qsum(y * 96) + R.qr2[...].astype(F32))

    def entry():
        for k in (1, 2, 3):
            recv(R.dqin.at[zk[k]], cd + k)
        gq, gk, gv = (jnp.concatenate([R.dqin[j, :, 192 * i:192 * i + 192] for j in range(4)], axis=1) for i in range(3))
        R.sm[0:1, :] = colsum(gq.astype(F32))
        R.sm[1:2, :] = colsum(gv.astype(F32))
        ge = R.own[...] + dot(gq, R.Gwq[...], 1, 1) + dot(gk, R.Gwk[...], 1, 1) + dot(gv, R.Gwv[...], 1, 1)
        gel = ge.astype(BF)
        R.gtok[...] = gel
        R.gp[...] = dot(hot_of(me, 512, 0), gel)
        R.sm[12:14, :] = dot(hot_of(me, 16, 512), gel)[0:2, :]
        R.ts0[...] = R.gp[ds((1 - c) * 256, 256), :].astype(BF)
        send(R.ts0, R.tr0, ctb, rdev[1])
        R.sms[0] = R.sm[...]
        send(R.sms.at[0], R.smr.at[0], csm, rdev[1])

    gt = group["t"]

    def t1():
        recv(R.tr0, ctb)
        a = gt.w[0] // 2
        R.ts1[...] = (R.gp[ds(c * 256 + (1 - a) * 128, 128), :]
                      + R.tr0[ds((1 - a) * 128, 128), :].astype(F32)).astype(BF)
        send(R.ts1, R.tr1, ctb + 1, gt.dev[2])
        recv(R.smr.at[0], csm)
        R.sms[1] = R.sms[0] + R.smr[0]
        send(R.sms.at[1], R.smr.at[1], csm + 1, rdev[2])

    def tsum(b):
        lanes, a = ds(b * 384, 384), gt.w[0] // 2
        return (R.gp[ds(c * 256 + a * 128, 128), lanes] + R.tr0[ds(a * 128, 128), lanes].astype(F32)
                + R.tr1[:, lanes].astype(F32))

    def t2():
        recv(R.tr1, ctb + 1)
        R.ts2[...] = tsum(1 - gt.b).astype(BF)
        send(R.ts2, R.tr2, ctb + 2, gt.bdev)
        recv(R.smr.at[1], csm + 1)
        R.sms[2] = R.sms[1] + R.smr[1]
        send(R.sms.at[2], R.smr.at[2], csm + 2, ydev)

    def t3():
        recv(R.tr2, ctb + 2)
        tv = tsum(gt.b) + R.tr2[...].astype(F32)
        R.ts3[...] = tv.astype(BF)
        for k in (2, 1, 3):
            send(R.ts3.at[ds(zk[k] * 32, 32), :], R.tr3.at[k], ctz + k, zdev[k])
        R.gp[0:128, 0:384] = tv
        recv(R.smr.at[2], csm + 2)
        R.sms[3] = R.sms[2] + R.smr[2]
        for k in (2, 1, 3):
            send(R.sms.at[3], R.smr.at[2 + k], csm + 2 + k, zdev[k])

    def t4():
        fin = R.gp[ds(z * 32, 32), 0:384]
        for k in (1, 2, 3):
            recv(R.tr3.at[k], ctz + k)
            fin = fin + R.tr3[k].astype(F32)
        gatherA("t", fin)
        total = R.sms[3]
        for k in (1, 2, 3):
            recv(R.smr.at[2 + k], csm + 2 + k)
            total = total + R.smr[2 + k]
        R.Gs[...] = total

    def assemble():
        gatherF("q")

        def part(i, _):
            m = ds(i * 128, 128)
            for t, out in enumerate((R.Gwq, R.Gwk, R.Gwv)):
                out[m, :] = jnp.concatenate([R.Gq[j, m, 192 * t:192 * t + 192] for j in range(4)], axis=1)
            return 0

        lax.fori_loop(0, 6, part, 0)

    tasks = {"gs": lambda: pass_on("gs", R.xgs), "gb": lambda: pass_on("gb", R.xgb), "sb": share_branch, "in": heads_in, "kv": kv_out,
             "vk": kv_in, "q0": q0, "q1": q1, "q2": q2, "q3": q3, "en": entry, "t1": t1, "t2": t2, "t3": t3, "t4": t4,
             "as": assemble}
    for h in range(3):
        tasks["h%d" % h] = partial(backward, h)
    for n in STREAMS:
        for stage, f in zip("12z3ABCDEF", (stage1, stage2, stage2z, stage3, gatherZ, gatherB, gatherC, gatherD, gatherE, gatherF), strict=True):
            tasks[stage + n] = partial(f, n)
    for name in ORDER:
        tasks[name]()
    for cp in pending:
        cp.wait_send()


def mega(*args):
    any_, vm = pl.BlockSpec(memory_space=pltpu.HBM), pl.BlockSpec(memory_space=VMEM)
    square = VMEM((D, D), BF)
    return pl.pallas_call(
        kernel,
        out_shape=(VMEM((T, D), BF), VMEM((T, D), BF), VMEM((F, D), BF), VMEM((D, F), BF), square, square, square, square,
                   VMEM((512, D), BF), VMEM((16, D), F32)),
        in_specs=[any_, any_, vm, vm, any_, vm] + [any_] * 6,
        out_specs=(vm,) * 10,
        scratch_shapes=list(scratch().values()),
        compiler_params=pltpu.CompilerParams(collective_id=0, has_side_effects=True, vmem_limit_bytes=41 << 20),
    )(*args)


def finish_kernel(layer, gtok, g2, g1, go, gq, gk, gv, gt, gs, layer_o, gtok_o, t_o, q_o, k_o, v_o, o_o, o1, o2, tab, buf, wide, sem, sem2):
    whole = [pltpu.make_async_copy(a, b, sem2.at[i]) for i, (a, b) in enumerate(((layer, layer_o), (gtok, gtok_o)))]
    for cp in whole:
        cp.start()
    tab[0:512, :] = gt[...].astype(F32)
    tab[512:514, :] = gs[12:14, :]
    whole.append(pltpu.make_async_copy(tab, t_o, sem2.at[2]))
    whole[-1].start()
    chunks = [(g2, o2, buf, i) for i in range(12)] + [(g1, o1, wide, i) for i in range(12)]
    chunks += [(a, b, buf, i) for a, b in ((go, o_o), (gq, q_o), (gk, k_o), (gv, v_o)) for i in range(3)]
    flying = {}
    for n, (src, dst, stage, i) in enumerate(chunks):
        rows = 256 if stage is buf else 64
        slot = n % 4
        if n >= 4:
            flying[slot].wait()
        stage[slot] = src[i * rows:(i + 1) * rows, :].astype(F32)
        flying[slot] = pltpu.make_async_copy(stage.at[slot], dst.at[i * rows:(i + 1) * rows, :], sem.at[slot])
        flying[slot].start()
    for slot in range(4):
        flying[slot].wait()
    for cp in whole:
        cp.wait()


def finish(*args):
    S = jax.ShapeDtypeStruct
    square = S((D, D), F32)
    hbm, vm = pl.BlockSpec(memory_space=pltpu.HBM), pl.BlockSpec(memory_space=VMEM)
    return pl.pallas_call(
        finish_kernel,
        out_shape=(S((T, D), BF), S((T, D), BF), S((514, D), F32), square, square, square, square, S((D, F), F32), S((F, D), F32)),
        in_specs=[vm] * 10,
        out_specs=(hbm,) * 9,
        scratch_shapes=[VMEM((514, D), F32), VMEM((4, 256, D), F32), VMEM((4, 64, F), F32), pltpu.SemaphoreType.DMA((4,)),
                        pltpu.SemaphoreType.DMA((3,))],
        compiler_params=pltpu.CompilerParams(vmem_limit_bytes=20 << 20),
    )(*args)


def fast_device(tokens, cotangent, segment_ids, restarts, position_table, query_weight, query_bias, key_weight,
                value_weight, value_bias, out_weight, out_bias, first_gain, first_shift, inner_weight, inner_bias,
                outer_weight, outer_bias, second_gain, second_shift):
    vectors = (query_bias, value_bias, out_bias, first_gain, first_shift, outer_bias, second_gain, second_shift)
    small, at = jnp.zeros((16 * D,), F32), 0
    for v in vectors + (inner_bias,):
        small = small + jnp.pad(v.astype(F32), (at, 16 * D - at - v.shape[0]))
        at += v.shape[0]
    small = small.reshape(16, D)
    made = mega(
        tokens[0], cotangent[0], segment_ids, restarts, position_table, small, query_weight,
        key_weight, value_weight, out_weight, inner_weight, outer_weight)
    layer, gtok, table, gq, gk, gv, go, g1, g2 = finish(*made)
    gs = made[-1]
    return (layer[None], gtok[None], table, gq, gs[0], gk, gv, gs[1], go, gs[2], gs[3], gs[4], g1, gs[8:12].reshape(F), g2,
            gs[5], gs[6], gs[7])


HEADS = 12


epsilon = 1e-05


def carried_in(array, axis, combine, identity):
    count, place = (lax.axis_size(axis), lax.axis_index(axis))
    everything = lax.all_gather(array, axis)
    start = jnp.broadcast_to(jnp.asarray(identity, array.dtype), array.shape)

    def hop(k, before):
        reached = k < place
        new = combine(before, everything[k])
        return jnp.where(reached, new, before)

    return lax.fori_loop(0, count, hop, start)


def matmul(left, right):
    return jnp.dot(left, right, preferred_element_type=jnp.float32)


def matmul_t(left, right):
    return lax.dot_general(
        left, right, (((1,), (1,)), ((), ())), preferred_element_type=jnp.float32
    )


def outer_sum(left, right):
    return lax.dot_general(
        left, right, (((0,), (0,)), ((), ())), preferred_element_type=jnp.float32
    )


def norm_forward(value, gain, shift):
    centered = value - jnp.mean(value, axis=-1, keepdims=True)
    spread = jnp.mean(centered * centered, axis=-1, keepdims=True)
    inverse = lax.rsqrt(spread + epsilon)
    normal = centered * inverse
    return (normal * gain.astype(jnp.float32) + shift.astype(jnp.float32), normal, inverse)


def norm_backward(incoming, normal, inverse, gain):
    scaled = incoming * gain.astype(jnp.float32)
    centred = scaled - jnp.mean(scaled, axis=-1, keepdims=True)
    outgoing = inverse * (centred - normal * jnp.mean(scaled * normal, axis=-1, keepdims=True))
    return (outgoing, jnp.sum(incoming * normal, axis=0), jnp.sum(incoming, axis=0))


def block_size(key_count):
    for option in (1024, 512):
        return option
    return key_count


def make_forward(queries, query_segs, score_scale):
    rows_here, tok_count, head_count, head_depth = queries.shape

    def step(carry, piece, start):
        key_rows, value_rows, key_segs = piece
        key_count = key_rows.shape[1]
        size = block_size(key_count)

        def one_block(index, state):
            highest, denom, accum = state
            begin = index * size
            keys_blk = lax.dynamic_slice_in_dim(key_rows, begin, size, 1).reshape(
                rows_here, size, head_count, head_depth
            )
            values_blk = lax.dynamic_slice_in_dim(value_rows, begin, size, 1).reshape(
                rows_here, size, head_count, head_depth
            )
            segs_blk = lax.dynamic_slice_in_dim(key_segs, begin, size, 1)
            scores = (
                jnp.einsum("rqhd,rkhd->rhqk", queries, keys_blk, preferred_element_type=jnp.float32)
                * score_scale
            )
            allowed = query_segs[:, None, :, None] == segs_blk[:, None, None, :]
            scores = jnp.where(allowed, scores, -jnp.inf)
            newest = jnp.maximum(highest, jnp.max(scores, axis=-1))
            weights = jnp.exp(scores - newest[..., None])
            factor = jnp.exp(highest - newest)
            denom = denom * factor + jnp.sum(weights, axis=-1)
            update = jnp.einsum(
                "rhqk,rkhd->rqhd",
                weights.astype(jnp.bfloat16),
                values_blk,
                preferred_element_type=jnp.float32,
            )
            accum = accum * jnp.swapaxes(factor, 1, 2)[..., None] + update
            return (newest, denom, accum)

        return lax.fori_loop(0, key_count // size, one_block, carry)

    return step


def make_backward(queries, query_segs, grad_attend, delta, logsum, score_scale):
    rows_here, tok_count, head_count, head_depth = queries.shape

    def step(carry, piece, start):
        key_rows, value_rows, key_segs = piece
        key_count = key_rows.shape[1]
        size = block_size(key_count)

        def one_block(index, state):
            begin = index * size
            keys_blk = lax.dynamic_slice_in_dim(key_rows, begin, size, 1).reshape(
                rows_here, size, head_count, head_depth
            )
            values_blk = lax.dynamic_slice_in_dim(value_rows, begin, size, 1).reshape(
                rows_here, size, head_count, head_depth
            )
            segs_blk = lax.dynamic_slice_in_dim(key_segs, begin, size, 1)
            scores = (
                jnp.einsum("rqhd,rkhd->rhqk", queries, keys_blk, preferred_element_type=jnp.float32)
                * score_scale
            )
            allowed = query_segs[:, None, :, None] == segs_blk[:, None, None, :]
            scores = jnp.where(allowed, scores, -jnp.inf)
            probs = jnp.exp(scores - logsum[..., None])
            grad_p = jnp.einsum(
                "rqhd,rkhd->rhqk", grad_attend, values_blk, preferred_element_type=jnp.float32
            )
            grad_s = (probs * (grad_p - delta[..., None]) * score_scale).astype(jnp.bfloat16)
            grad_q = state[0] + jnp.einsum(
                "rhqk,rkhd->rqhd", grad_s, keys_blk, preferred_element_type=jnp.float32
            )
            grad_k, grad_v = (state[1], state[2])
            grad_v_blk = jnp.einsum(
                "rhqk,rqhd->rkhd",
                probs.astype(jnp.bfloat16),
                grad_attend,
                preferred_element_type=jnp.float32,
            )
            grad_k_blk = jnp.einsum(
                "rhqk,rqhd->rkhd", grad_s, queries, preferred_element_type=jnp.float32
            )
            grad_k = lax.dynamic_update_slice_in_dim(
                grad_k, grad_k_blk.reshape(rows_here, size, head_count * head_depth), begin, 1
            )
            grad_v = lax.dynamic_update_slice_in_dim(
                grad_v, grad_v_blk.reshape(rows_here, size, head_count * head_depth), begin, 1
            )
            return (grad_q, grad_k, grad_v)

        return lax.fori_loop(0, key_count // size, one_block, carry)

    return step


def per_device(
    tokens,
    cotangent,
    segment_ids,
    restarts,
    position_table,
    query_weight,
    query_bias,
    key_weight,
    value_weight,
    value_bias,
    out_weight,
    out_bias,
    first_gain,
    first_shift,
    inner_weight,
    inner_bias,
    outer_weight,
    outer_bias,
    second_gain,
    second_shift,
):
    rows_here, tok_count, model_width = tokens.shape
    head_count = HEADS
    head_depth = model_width // head_count
    score_scale = head_depth ** (-0.5)
    flat_count = rows_here * tok_count
    row_length = tok_count * lax.axis_size("seq")
    offset = lax.axis_index("seq") * tok_count
    places = offset + jnp.arange(tok_count, dtype=jnp.int32)[None, :]
    marked = jnp.where(restarts == 1, places, -1)
    earlier = carried_in(
        jnp.max(marked, axis=1), "seq", jnp.maximum, jnp.full((rows_here,), -1, jnp.int32)
    )
    latest = jnp.maximum(lax.cummax(marked, axis=1), earlier[:, None])
    positions = places - latest + 2
    onehot = (
        positions.reshape(flat_count, 1)
        == jnp.arange(position_table.shape[0], dtype=jnp.int32)[None, :]
    )
    entry = tokens.reshape(flat_count, model_width).astype(jnp.float32) + matmul(
        onehot.astype(jnp.bfloat16), position_table
    )
    entry_low = entry.astype(jnp.bfloat16)
    queries = (matmul(entry_low, query_weight) + query_bias.astype(jnp.float32)).astype(
        jnp.bfloat16
    )
    keys_low = matmul(entry_low, key_weight).astype(jnp.bfloat16)
    values_low = (matmul(entry_low, value_weight) + value_bias.astype(jnp.float32)).astype(
        jnp.bfloat16
    )
    query_heads = queries.reshape(rows_here, tok_count, head_count, head_depth)
    key_rows = keys_low.reshape(rows_here, tok_count, model_width)
    value_rows = values_low.reshape(rows_here, tok_count, model_width)
    start_state = (
        jnp.full((rows_here, head_count, tok_count), -1e30, jnp.float32),
        jnp.zeros((rows_here, head_count, tok_count), jnp.float32),
        jnp.zeros((rows_here, tok_count, head_count, head_depth), jnp.float32),
    )
    forward_step = make_forward(query_heads, segment_ids, score_scale)
    highest, denom, accum = forward_step(
        start_state,
        (
            lax.all_gather(key_rows, "seq", axis=1, tiled=True),
            lax.all_gather(value_rows, "seq", axis=1, tiled=True),
            lax.all_gather(segment_ids, "seq", axis=1, tiled=True),
        ),
        jnp.int32(0),
    )
    attend = accum / jnp.swapaxes(denom, 1, 2)[..., None]
    logsum = highest + jnp.log(denom)
    attended_low = attend.reshape(flat_count, model_width).astype(jnp.bfloat16)
    branch = matmul(attended_low, out_weight) + out_bias.astype(jnp.float32)
    first, first_normal, first_inverse = norm_forward(entry + branch, first_gain, first_shift)
    first_low = first.astype(jnp.bfloat16)
    inner = matmul(first_low, inner_weight) + inner_bias.astype(jnp.float32)
    activation, gelu_back = jax.vjp(partial(jax.nn.gelu, approximate=False), inner)
    active_low = activation.astype(jnp.bfloat16)
    second_in = first + matmul(active_low, outer_weight) + outer_bias.astype(jnp.float32)
    result, second_normal, second_inverse = norm_forward(second_in, second_gain, second_shift)
    layer_out = result.astype(jnp.bfloat16).reshape(rows_here, tok_count, model_width)
    incoming = cotangent.reshape(flat_count, model_width).astype(jnp.float32)
    grad_second, grad_gsecond, grad_ssecond = norm_backward(
        incoming, second_normal, second_inverse, second_gain
    )
    grad_second_low = grad_second.astype(jnp.bfloat16)
    grad_wouter = outer_sum(active_low, grad_second_low)
    grad_bouter = jnp.sum(grad_second_low.astype(jnp.float32), axis=0)
    grad_inner_low = gelu_back(matmul_t(grad_second_low, outer_weight))[0].astype(jnp.bfloat16)
    grad_winner = outer_sum(first_low, grad_inner_low)
    grad_binner = jnp.sum(grad_inner_low.astype(jnp.float32), axis=0)
    grad_first = grad_second + matmul_t(grad_inner_low, inner_weight)
    grad_first_in, grad_gfirst, grad_sfirst = norm_backward(
        grad_first, first_normal, first_inverse, first_gain
    )
    grad_branch_low = grad_first_in.astype(jnp.bfloat16)
    grad_wout = outer_sum(attended_low, grad_branch_low)
    grad_bout = jnp.sum(grad_branch_low.astype(jnp.float32), axis=0)
    grad_attend = (
        matmul_t(grad_branch_low, out_weight)
        .astype(jnp.bfloat16)
        .reshape(rows_here, tok_count, head_count, head_depth)
    )
    delta_rows = jnp.sum(grad_attend.astype(jnp.float32) * attend, axis=-1)
    delta = jnp.swapaxes(delta_rows, 1, 2)
    query_zero = jnp.zeros((rows_here, tok_count, head_count, head_depth), jnp.float32)
    back_state = (
        query_zero,
        jnp.zeros((rows_here, row_length, model_width), jnp.float32),
        jnp.zeros((rows_here, row_length, model_width), jnp.float32),
    )
    backward_step = make_backward(query_heads, segment_ids, grad_attend, delta, logsum, score_scale)
    back_out = backward_step(
        back_state,
        (
            lax.all_gather(key_rows, "seq", axis=1, tiled=True),
            lax.all_gather(value_rows, "seq", axis=1, tiled=True),
            lax.all_gather(segment_ids, "seq", axis=1, tiled=True),
        ),
        jnp.int32(0),
    )
    grad_q = back_out[0]
    grad_keys, grad_values = (
        lax.psum_scatter(back_out[1], "seq", scatter_dimension=1, tiled=True),
        lax.psum_scatter(back_out[2], "seq", scatter_dimension=1, tiled=True),
    )
    grad_query_low = grad_q.reshape(flat_count, model_width).astype(jnp.bfloat16)
    grad_key_low = grad_keys.reshape(flat_count, model_width).astype(jnp.bfloat16)
    grad_value_low = grad_values.reshape(flat_count, model_width).astype(jnp.bfloat16)
    grad_entry = (
        grad_first_in
        + matmul_t(grad_query_low, query_weight)
        + matmul_t(grad_key_low, key_weight)
        + matmul_t(grad_value_low, value_weight)
    )
    grad_wquery = outer_sum(entry_low, grad_query_low)
    grad_bquery = jnp.sum(grad_query_low.astype(jnp.float32), axis=0)
    grad_wkey = outer_sum(entry_low, grad_key_low)
    grad_wvalue = outer_sum(entry_low, grad_value_low)
    grad_bvalue = jnp.sum(grad_value_low.astype(jnp.float32), axis=0)
    grad_table = lax.dot_general(
        onehot.astype(jnp.float32),
        grad_entry,
        (((0,), (0,)), ((), ())),
        precision=lax.Precision.HIGHEST,
        preferred_element_type=jnp.float32,
    )
    grad_tokens = grad_entry.astype(jnp.bfloat16).reshape(rows_here, tok_count, model_width)
    pieces = (
        lax.psum_scatter(grad_wquery, "seq", scatter_dimension=0, tiled=True),
        lax.psum_scatter(grad_wkey, "seq", scatter_dimension=0, tiled=True),
        lax.psum_scatter(grad_wvalue, "seq", scatter_dimension=0, tiled=True),
        lax.psum_scatter(grad_wout, "seq", scatter_dimension=0, tiled=True),
        lax.psum_scatter(grad_winner, "seq", scatter_dimension=0, tiled=True),
        lax.psum_scatter(grad_wouter, "seq", scatter_dimension=0, tiled=True),
    )
    pieces = (
        lax.psum(pieces[0].astype(jnp.bfloat16), "rows").astype(jnp.float32),
        lax.psum(pieces[1].astype(jnp.bfloat16), "rows").astype(jnp.float32),
        lax.psum(pieces[2].astype(jnp.bfloat16), "rows").astype(jnp.float32),
        lax.psum(pieces[3].astype(jnp.bfloat16), "rows").astype(jnp.float32),
        lax.psum(pieces[4].astype(jnp.bfloat16), "rows").astype(jnp.float32),
        lax.psum(pieces[5].astype(jnp.bfloat16), "rows").astype(jnp.float32),
    )
    total_wquery, total_wkey, total_wvalue, total_wout, total_winner, total_wouter = (
        lax.all_gather(pieces[0].astype(jnp.bfloat16), "seq", axis=0, tiled=True).astype(
            jnp.float32
        ),
        lax.all_gather(pieces[1].astype(jnp.bfloat16), "seq", axis=0, tiled=True).astype(
            jnp.float32
        ),
        lax.all_gather(pieces[2].astype(jnp.bfloat16), "seq", axis=0, tiled=True).astype(
            jnp.float32
        ),
        lax.all_gather(pieces[3].astype(jnp.bfloat16), "seq", axis=0, tiled=True).astype(
            jnp.float32
        ),
        lax.all_gather(pieces[4].astype(jnp.bfloat16), "seq", axis=0, tiled=True).astype(
            jnp.float32
        ),
        lax.all_gather(pieces[5].astype(jnp.bfloat16), "seq", axis=0, tiled=True).astype(
            jnp.float32
        ),
    )
    smalls = lax.psum(
        (
            grad_table,
            grad_bquery,
            grad_bvalue,
            grad_bout,
            grad_gfirst,
            grad_sfirst,
            grad_binner,
            grad_bouter,
            grad_gsecond,
            grad_ssecond,
        ),
        ("seq", "rows"),
    )
    (
        total_table,
        total_bquery,
        total_bvalue,
        total_bout,
        total_gfirst,
        total_sfirst,
        total_binner,
        total_bouter,
        total_gsecond,
        total_ssecond,
    ) = smalls
    return (
        layer_out,
        grad_tokens,
        total_table,
        total_wquery,
        total_bquery,
        total_wkey,
        total_wvalue,
        total_bvalue,
        total_wout,
        total_bout,
        total_gfirst,
        total_sfirst,
        total_winner,
        total_binner,
        total_wouter,
        total_bouter,
        total_gsecond,
        total_ssecond,
    )


def solution(mesh):
    in_specs = (
        P("rows", "seq", None),
        P("rows", "seq", None),
        P("rows", "seq"),
        P("rows", "seq"),
        P(),
        P(),
        P(),
        P(),
        P(),
        P(),
        P(),
        P(),
        P(),
        P(),
        P(),
        P(),
        P(),
        P(),
        P(),
        P(),
    )
    out_specs = (
        P("rows", "seq", None),
        P("rows", "seq", None),
        P(),
        P(),
        P(),
        P(),
        P(),
        P(),
        P(),
        P(),
        P(),
        P(),
        P(),
        P(),
        P(),
        P(),
        P(),
        P(),
    )
    body = fast_device if mesh.shape["seq"] == 8 and mesh.shape["rows"] == 4 else per_device
    return jax.shard_map(
        body, mesh=mesh, in_specs=in_specs, out_specs=out_specs, check_vma=False
    )
```

```python
from functools import partial
from types import SimpleNamespace

import jax
import jax.numpy as jnp
from jax import lax
from jax.experimental import pallas as pl
from jax.experimental.pallas import tpu as pltpu
from jax.sharding import PartitionSpec as P

MESH = pl.DeviceIdType.MESH
VMEM = pltpu.VMEM
BF, F32, I32 = jnp.bfloat16, jnp.float32, jnp.int32
T, D, F, L, HD = 128, 768, 3072, 1024, 64
EPS = 1e-5
CHANNELS = 240
ROWS_OF = {"2a": 384, "2b": 384, "1a": 384, "1b": 384, "o": 192}
STREAMS = tuple(ROWS_OF) + ("q", "t")
ORDER = (
    "sb", "gs", "in", "11b", "12b", "11a", "h0", "h1", "12a", "21b", "gb", "h2", "22b", "z1b", "21a", "1o", "31b",
    "z2b", "kv", "z1a", "A1b", "32b", "2o", "B1b", "A2b", "vk", "q0", "q1", "B2b", "31a", "C2b", "D1b", "q2", "C1b",
    "en", "A1a", "zo", "q3", "t1", "B1a", "E1b", "Aq", "t2", "3o", "22a", "Bq", "Ao", "t3", "E2b", "Bo", "z2a", "Cq",
    "t4", "32a", "F1b", "C1a", "At", "A2a", "Do", "B2a", "D2b", "Eq", "Co", "Bt", "E1a", "C2a", "Dq", "Eo", "Ct",
    "Fo", "as", "Dt", "Et", "D2a", "D1a", "F2b", "E2a", "F1a", "Ft", "F2a",
)


def dot(a, b, ca=1, cb=0):
    return lax.dot_general(a, b, (((ca,), (cb,)), ((), ())), preferred_element_type=F32)


def ds(start, size, step=None):
    return pl.ds(pl.multiple_of(start, step or size), size)


def scratch():
    s = {}
    s["tok"] = VMEM((8, T, D), BF)
    s["meta"] = VMEM((8, 8, T), I32)
    s["tail"] = VMEM((16, D), BF)
    s["table"] = VMEM((514, D), BF)
    s["cot"] = VMEM((T, D), BF)
    s["pos"] = VMEM((8, 8, T), I32)
    s["segc"] = VMEM((L, T), F32)
    s["segq"] = VMEM((2, 8, 256), F32)
    s["elow"] = VMEM((4 * T, D), BF)
    s["q3"] = VMEM((3, 512, HD), BF)
    s["k3"] = VMEM((3, L, HD), BF)
    s["v3"] = VMEM((3, L, HD), BF)
    s["pt"] = VMEM((3, L, 512), BF)
    s["stat"] = VMEM((3, 2, 8, 256), F32)
    s["half"] = VMEM((3, HD, 512), F32)
    s["attcat"] = VMEM((4, 192, T), BF)
    s["attg"] = VMEM((4, 192, T), BF)
    s["own"] = VMEM((T, D), F32)
    for n in ("first", "act", "gs", "gi", "gb"):
        s["x" + n] = VMEM((4 * T, D), BF)
    s["xatt"] = VMEM((192, 4 * T), BF)
    s["gp"] = VMEM((4 * T, D), F32)
    s["gaout"] = VMEM((4, T, 192), BF)
    s["gag"] = VMEM((4, T, 192), BF)
    s["ga3"] = VMEM((3, 512, HD), BF)
    s["dk"] = VMEM((L, HD), F32)
    s["dv"] = VMEM((L, HD), F32)
    s["kvo"] = VMEM((512, 384), F32)
    s["kvs"] = VMEM((512, 384), BF)
    s["kvr"] = VMEM((512, 384), BF)
    s["gqkv"] = VMEM((512, 576), BF)
    s["dqin"] = VMEM((4, T, 576), BF)
    for n, m in ROWS_OF.items():
        s["bs" + n] = VMEM((m, 384), BF)
        s["br" + n] = VMEM((m, 384), BF)
        s["ac" + n] = VMEM((m, 384), F32)
        s["zr" + n] = VMEM((3, m // 4, 384), BF)
    s["qp"] = VMEM((384, 576), F32)
    for i, m in ((0, 384), (1, 192), (2, 96)):
        s["qs%d" % i] = VMEM((m, 576), BF)
        s["qr%d" % i] = VMEM((m, 576), BF)
    s["Gq"] = VMEM((4, D, 576), BF)
    for i, m in ((0, 256), (1, 128)):
        s["ts%d" % i] = VMEM((m, D), BF)
        s["tr%d" % i] = VMEM((m, D), BF)
    s["ts2"] = VMEM((128, 384), BF)
    s["tr2"] = VMEM((128, 384), BF)
    s["ts3"] = VMEM((128, 384), BF)
    s["tr3"] = VMEM((4, 32, 384), BF)
    s["sm"] = VMEM((16, D), F32)
    s["sms"] = VMEM((4, 16, D), F32)
    s["smr"] = VMEM((6, 16, D), F32)
    s["wsem"] = pltpu.SemaphoreType.DMA((9,))
    s["ss"] = pltpu.SemaphoreType.DMA((CHANNELS,))
    s["rs"] = pltpu.SemaphoreType.DMA((CHANNELS,))
    return s


INPUTS = ("tokens", "hcot", "segs", "rests", "htable", "small", "hq", "hk", "hv", "ho", "h1", "h2")
OUTPUTS = ("layer", "gtok", "G2", "G1", "Go", "Gwq", "Gwk", "Gwv", "Gt", "Gs")


def kernel(*refs):
    names = INPUTS + OUTPUTS + tuple(scratch())
    R = SimpleNamespace(**dict(zip(names, refs, strict=True)))
    seq, row = lax.axis_index("seq"), lax.axis_index("rows")
    z, y, x, c = seq // 2, seq % 2, row // 2, row % 2
    zk = [z, z + 1 - 2 * (z % 2), (z + 2) % 4, 3 - z]
    rk = [row, x * 2 + (1 - c), (1 - x) * 2 + c, (1 - x) * 2 + (1 - c)]
    zdev = [(zk[k] * 2 + y, row) for k in range(4)]
    ydev = (z * 2 + (1 - y), row)
    rdev = [(seq, rk[k]) for k in range(4)]
    counter = [0]
    pending = []

    def chan(n=1):
        counter[0] += n
        assert counter[0] <= CHANNELS
        return counter[0] - n

    def copy(src, dst, i, dev):
        return pltpu.make_async_remote_copy(src, dst, R.ss.at[i], R.rs.at[i], device_id=dev, device_id_type=MESH)

    def send(src, dst, i, dev):
        cp = copy(src, dst, i, dev)
        cp.start()
        pending.append(cp)

    def recv(dst, i):
        copy(dst, dst, i, ydev).wait_recv()

    yxdev = (z * 2 + (1 - y), x * 2 + (1 - c))
    gx = SimpleNamespace(w=[row, *rk[1:]], dev=rdev, b=y, bdev=ydev)
    wy = y * 2 + c
    gy = SimpleNamespace(w=[wy, y * 2 + (1 - c), (1 - y) * 2 + c, (1 - y) * 2 + (1 - c)],
                         dev=[(seq, row), rdev[1], ydev, yxdev], b=x, bdev=rdev[2])
    group = {n: gy if n[0] in "1ot" else gx for n in STREAMS}
    group.update(first=gy, gi=gy, att=gy, gb=gy, act=gx, gs=gx)

    seqpeers = [zdev[1], zdev[2], zdev[3]] + [(zk[k] * 2 + (1 - y), row) for k in range(4)]
    peers = seqpeers + rdev[1:] + [yxdev]
    bar = pltpu.get_barrier_semaphore()
    for p in peers:
        pl.semaphore_signal(bar, inc=1, device_id=p, device_id_type=MESH)

    loads = {}
    weights = (("n", R.tokens, R.tok.at[y * 4 + z]), ("t", R.htable, R.table), ("k", R.hk, R.Gwk), ("v", R.hv, R.Gwv), ("q", R.hq, R.Gwq), ("c", R.hcot, R.cot), ("o", R.ho, R.Go), ("1", R.h1, R.G1), ("2", R.h2, R.G2))

    def load(i):
        n, src, dst = weights[i]
        loads[n] = pltpu.make_async_copy(src, dst, R.wsem.at[i])
        loads[n].start()

    for i in range(5):
        load(i)

    me = y * 4 + z
    R.meta[me] = jnp.zeros((8, T), I32)
    R.meta[me, 0:1, :] = R.rests[...]
    R.meta[me, 1:2, :] = R.segs[...]
    pl.semaphore_wait(bar, len(peers))
    loads["n"].wait()
    cm = chan(7)
    metas = []
    for i, dev in enumerate(seqpeers):
        cp = copy(R.meta.at[me], R.meta.at[me], cm + i, dev)
        cp.start()
        metas.append(cp)
    ct = chan(16)
    tokens_out = []

    def half_of(b, h):
        return R.tok.at[b, 64 * h:64 * h + 64, :]

    def forward(b, i, h, dev):
        tokens_out.append(copy(half_of(b, h), half_of(b, h), ct + 2 * i + h, dev))
        tokens_out[-1].start()

    for h in range(2):
        forward(me, 1, h, zdev[1])
        forward(me, 4, h, ydev)
    for h in range(2):
        forward(me, 2, h, zdev[2])
    for i in range(5, 9):
        load(i)
    loads["t"].wait()
    R.tail[...] = jnp.zeros((16, D), BF)
    R.tail[0:2, :] = R.table[512:514, :]
    for cp in metas:
        cp.wait()
    lane = lax.broadcasted_iota(I32, (8, T), 1)
    spot = lax.broadcasted_iota(I32, (8, T), 0) * T + lane
    block_of = [(s % 2) * 4 + s // 2 for s in range(8)]
    flags = jnp.concatenate([R.meta[b, 0:1, :] for b in block_of], axis=0)
    mk = jnp.where(flags == 1, spot, -1)
    k = 1
    while k < T:
        mk = jnp.where(lane >= k, jnp.maximum(mk, pltpu.roll(mk, k, axis=1)), mk)
        k *= 2
    tot = jnp.max(mk, axis=1, keepdims=True)
    carry = jnp.full((1, 1), -1, I32)
    for s, b in enumerate(block_of):
        late = jnp.maximum(mk[s:s + 1, :], carry)
        R.pos[b, 0:1, :] = spot[s:s + 1, :] - late + 2
        carry = jnp.maximum(carry, tot[s:s + 1, :])
    for b in range(8):
        R.segc[b * T:(b + 1) * T, :] = jnp.broadcast_to(R.meta[b, 1:2, :], (T, T)).astype(F32).T
    for j in range(2):
        R.segq[j, 0:1, :] = jnp.concatenate([R.meta[y * 4 + 2 * j + i, 1:2, :] for i in range(2)], axis=1).astype(F32)

    off = pl.multiple_of(128 * ((3 * z) // 2), 128)
    odd = (z % 2) == 1

    def window(v):
        return jnp.where(odd, v[:, 64:256], v[:, 0:192])

    bq = R.small[0:1, pl.ds(off, 256)]
    bv = R.small[1:2, pl.ds(off, 256)]
    for n in "kvq":
        loads[n].wait()

    def hot_of(b, size, start):
        return (lax.broadcasted_iota(I32, (size, T), 0) + start == R.pos[b, 0:1, :]).astype(BF)

    def block(b, with_q):
        e = dot(hot_of(b, 512, 0), R.table[0:512, :], 0, 0) + dot(hot_of(b, 16, 512), R.tail[...], 0, 0)
        e = e + R.tok[b].astype(F32)
        el = e.astype(BF)
        here = ds(b * T, T)
        kk = window(dot(el, R.Gwk[:, pl.ds(off, 256)])).astype(BF)
        vv = window(dot(el, R.Gwv[:, pl.ds(off, 256)]) + bv).astype(BF)
        for h in range(3):
            R.k3[h, here, :] = kk[:, 64 * h:64 * h + 64]
            R.v3[h, here, :] = vv[:, 64 * h:64 * h + 64]
        if with_q:
            qq = (window(dot(el, R.Gwq[:, pl.ds(off, 256)]) + bq) * 0.125).astype(BF)
            there = ds((b - y * 4) * T, T)
            R.elow[there, :] = el
            for h in range(3):
                R.q3[h, there, :] = qq[:, 64 * h:64 * h + 64]
        return e

    R.own[...] = block(me, True)

    for k in (1, 2, 3):
        b = y * 4 + zk[k]
        for h in range(2):
            recv(half_of(b, h), ct + 2 * k + h)
            if k == 2:
                forward(b, 3, h, zdev[1])
            forward(b, 4 + k, h, ydev)
        block(b, True)

    def scores(h, j, parity):
        rows, qs = ds(parity * 512, 512), ds(j * 256, 256)
        s = dot(R.k3[h, rows, :], R.q3[h, qs, :], 1, 1)
        sc = R.segc[rows, :]
        s = jnp.where(jnp.concatenate([sc, sc], axis=1) == R.segq[j, 0:1, :], s, -1e30)
        top = jnp.max(s, axis=0, keepdims=True)
        p = jnp.exp(s - top)
        low = p.astype(BF)
        R.pt[h, rows, qs] = low
        return top, jnp.sum(p, axis=0, keepdims=True), dot(R.v3[h, rows, :], low, 0, 0)

    def attend_near(i, _):
        h, j = i // 2, i % 2
        top, den, acc = scores(h, j, y)
        R.stat[h, j, 2:3, :] = top
        R.stat[h, j, 3:4, :] = den
        R.half[h, :, ds(j * 256, 256)] = acc
        return 0

    def attend_far(i, _):
        h, j = i // 2, i % 2
        top, den, acc = scores(h, j, 1 - y)
        top0 = R.stat[h, j, 2:3, :]
        most = jnp.maximum(top, top0)
        f, f0 = jnp.exp(top - most), jnp.exp(top0 - most)
        inv = 1.0 / (den * f + R.stat[h, j, 3:4, :] * f0)
        f, f0 = f * inv, f0 * inv
        R.stat[h, j, pl.ds(y, 1), :] = f0
        R.stat[h, j, pl.ds(1 - y, 1), :] = f
        qs = ds(j * 256, 256)
        R.half[h, :, qs] = acc * f + R.half[h, :, qs] * f0
        return 0

    lax.fori_loop(0, 6, attend_near, 0)
    for k in (0, 1, 2, 3):
        b = (1 - y) * 4 + zk[k]
        for h in range(2):
            recv(half_of(b, h), ct + 8 + 2 * k + h)
        block(b, False)
    ca = chan(12)

    def head_of(ref, j, h):
        return ref.at[j, 64 * h:64 * h + 64, :]

    for h in range(3):
        lax.fori_loop(2 * h, 2 * h + 2, attend_far, 0)
        for j in range(4):
            R.attcat[j, 64 * h:64 * h + 64, :] = R.half[h, :, j * T:(j + 1) * T].astype(BF)
        for k in (2, 1, 3):
            send(head_of(R.attcat, zk[k], h), head_of(R.attg, z, h), ca + 3 * k + h, zdev[k])
    R.attg[z] = R.attcat[z]
    for n in "co12":
        loads[n].wait()
    for cp in tokens_out:
        cp.wait_send()
    for k in (1, 2, 3):
        for h in range(3):
            recv(head_of(R.attg, zk[k], h), ca + 3 * k + h)

    def slot(n, k):
        return ds(group[n].w[k] * T, T)

    def small(i):
        return R.small[i:i + 1, :]

    def colsum(v):
        return jnp.sum(v, axis=0, keepdims=True)

    def mean(v):
        return jnp.mean(v, axis=-1, keepdims=True)

    R.sm[...] = jnp.zeros((16, D), F32)
    cx = {n: chan(4) for n in ("first", "act", "att", "gs", "gi", "gb")}

    def share(n, ref):
        mine = ref.at[slot(n, 0), :]
        send(mine, mine, cx[n] + 2, group[n].dev[2])
        send(mine, mine, cx[n] + 1, group[n].dev[1])

    def pass_on(n, ref):
        theirs = ref.at[slot(n, 2), :]
        recv(theirs, cx[n] + 2)
        send(theirs, theirs, cx[n] + 3, group[n].dev[1])

    u = R.own[...] + dot(jnp.concatenate([R.attg[j] for j in range(4)], axis=0), R.Go[...], 0, 0) + small(2)
    u = u - mean(u)
    inv1 = lax.rsqrt(mean(u * u) + EPS)
    n1 = u * inv1
    first = n1 * small(3) + small(4)
    first_low = first.astype(BF)
    R.xfirst[slot("first", 0), :] = first_low
    share("first", R.xfirst)
    second = jnp.zeros((T, D), F32)
    for k in (2, 3, 1, 0):
        q = gx.w[k]
        cols = ds(q * D, D)
        inner = dot(first_low, R.G1[:, cols]) + R.small[pl.ds(8 + q, 1), :]
        phi = 0.5 * (1.0 + lax.erf(inner * 0.7071067811865476))
        R.gp[ds(q * T, T), :] = phi + inner * (0.3989422804014327 * jnp.exp(-0.5 * inner * inner))
        act = (inner * phi).astype(BF)
        if k:
            R.tok[k] = act
            send(R.tok.at[k], R.xact.at[slot("act", 0), :], cx["act"] + k, gx.dev[k])
        else:
            R.xact[slot("act", 0), :] = act
        second = second + dot(act, R.G2[cols, :])
    R.xatt[:, slot("att", 0)] = R.attg[gy.w[0]]
    u = first + second + small(5)
    u = u - mean(u)
    inv2 = lax.rsqrt(mean(u * u) + EPS)
    n2 = u * inv2
    R.layer[...] = (n2 * small(6) + small(7)).astype(BF)
    g = R.cot[...].astype(F32)
    R.sm[6:7, :] = colsum(g * n2)
    R.sm[7:8, :] = colsum(g)
    sc = g * small(6)
    gs = inv2 * (sc - mean(sc) - n2 * mean(sc * n2))
    gs_low = gs.astype(BF)
    R.xgs[slot("gs", 0), :] = gs_low
    share("gs", R.xgs)
    R.sm[5:6, :] = colsum(gs_low.astype(F32))
    pass_on("first", R.xfirst)
    for k in (2, 3, 1, 0):
        q = gy.w[k]
        cols = ds(q * D, D)
        gi = (dot(gs_low, R.G2[cols, :], 1, 1) * R.gp[ds(q * T, T), :]).astype(BF)
        if k:
            R.tok[4 + k] = gi
            send(R.tok.at[4 + k], R.xgi.at[slot("gi", 0), :], cx["gi"] + k, gy.dev[k])
        else:
            R.xgi[slot("gi", 0), :] = gi
        R.sm[pl.ds(8 + q, 1), :] = colsum(gi.astype(F32))
        gs = gs + dot(gi, R.G1[:, cols], 1, 1)
    R.sm[3:4, :] = colsum(gs * n1)
    R.sm[4:5, :] = colsum(gs)
    sc = gs * small(3)
    gfi = inv1 * (sc - mean(sc) - n1 * mean(sc * n1))
    R.own[...] = gfi
    gb = gfi.astype(BF)
    R.xgb[slot("gb", 0), :] = gb
    ga = dot(gb, R.Go[...], 1, 1).astype(BF)
    for j in range(4):
        R.gaout[j] = ga[:, 192 * j:192 * j + 192]
    cg = chan(4)
    for k in (2, 1, 3):
        send(R.gaout.at[zk[k]], R.gag.at[z], cg + k, zdev[k])
    R.gag[z] = R.gaout[z]
    R.sm[2:3, :] = colsum(gb.astype(F32))

    def two(h):
        lo = 384 * h
        return (lambda w, b: R.G2.at[ds(w * 768 + lo, 384), ds(b * 384, 384)],
                lambda w, b, zz: R.G2.at[ds(w * 768 + lo + zz * 96, 96), ds(b * 384, 384)])

    def one(h):
        lo = 384 * h
        return (lambda w, b: R.G1.at[lo:lo + 384, ds(w * 768 + b * 384, 384)],
                lambda w, b, zz: R.G1.at[ds(lo + zz * 96, 96), ds(w * 768 + b * 384, 384)])

    regions = {
        "2a": two(0), "2b": two(1), "1a": one(0), "1b": one(1),
        "o": (lambda w, b: R.Go.at[ds(w * 192, 192), ds(b * 384, 384)],
              lambda w, b, zz: R.Go.at[ds(w * 192 + zz * 48, 48), ds(b * 384, 384)]),
        "q": (lambda w, b: R.Gq.at[:, ds((w % 2) * 384 + (w // 2) * 192 + b * 96, 96), :],
              lambda w, b, zz: R.Gq.at[zz, ds((w % 2) * 384 + (w // 2) * 192 + b * 96, 96), :]),
        "t": (lambda w, b: R.Gt.at[ds((w % 2) * 256 + (w // 2) * 128, 128), ds(b * 384, 384)],
              lambda w, b, zz: R.Gt.at[ds((w % 2) * 256 + (w // 2) * 128 + zz * 32, 32), ds(b * 384, 384)]),
    }
    operands = {"2a": (R.xact, 0, R.xgs), "2b": (R.xact, 384, R.xgs), "1a": (R.xfirst, 0, R.xgi), "1b": (R.xfirst, 384, R.xgi)}
    cs = {n: chan(15) for n in STREAMS}
    arrived = set()

    def ready(n, ref, forwarded=True):
        if n not in arrived:
            arrived.add(n)
            for k in ((1, 3) if forwarded else (1, 2, 3)):
                recv(ref.at[:, slot(n, k)] if n == "att" else ref.at[slot(n, k), :], cx[n] + k)

    def stage1(n):
        acc, bs, br = getattr(R, "ac" + n), getattr(R, "bs" + n), getattr(R, "br" + n)
        b = group[n].b
        if n == "o":
            ready("att", R.xatt, False)
            ready("gb", R.xgb)
            bs[...] = dot(R.xatt[...], R.xgb[:, ds((1 - b) * 384, 384)]).astype(BF)
            send(bs, br, cs[n], group[n].bdev)
            acc[...] = dot(R.xatt[...], R.xgb[:, ds(b * 384, 384)])
            return
        if n[0] == "2":
            ready("act", R.xact, False)
            ready("gs", R.xgs)
        else:
            ready("gi", R.xgi, False)
            ready("first", R.xfirst)
        lhs, lo, rhs = operands[n]

        def other(i, _):
            bs[ds(i * 128, 128), :] = dot(lhs[:, ds(lo + i * 128, 128)], rhs[:, ds((1 - b) * 384, 384)], 0, 0).astype(BF)
            return 0

        def same(i, _):
            acc[ds(i * 128, 128), :] = dot(lhs[:, ds(lo + i * 128, 128)], rhs[:, ds(b * 384, 384)], 0, 0)
            return 0

        lax.fori_loop(0, 3, other, 0)
        send(bs, br, cs[n], group[n].bdev)
        lax.fori_loop(0, 3, same, 0)

    def stage2(n):
        acc, br, zr = (getattr(R, a + n) for a in ("ac", "br", "zr"))
        recv(br, cs[n])
        q = ROWS_OF[n] // 4
        for k in (3, 1, 2, 0):
            m = ds(zk[k] * q, q)
            v = acc[m, :] + br[m, :].astype(F32)
            if k % 2:
                br[m, :] = v.astype(BF)
                send(br.at[m, :], zr.at[k // 2], cs[n] + 1 + k // 2, zdev[1])
            else:
                acc[m, :] = v

    def stage2z(n):
        acc, br, zr = (getattr(R, a + n) for a in ("ac", "br", "zr"))
        recv(zr.at[1], cs[n] + 2)
        q = ROWS_OF[n] // 4
        m = ds(zk[2] * q, q)
        br[m, :] = (acc[m, :] + zr[1].astype(F32)).astype(BF)
        send(br.at[m, :], zr.at[2], cs[n] + 3, zdev[2])

    def stage3(n):
        acc, zr = getattr(R, "ac" + n), getattr(R, "zr" + n)
        q = ROWS_OF[n] // 4
        v = acc[ds(z * q, q), :]
        for i in (0, 2):
            recv(zr.at[i], cs[n] + 1 + i)
            v = v + zr[i].astype(F32)
        gatherA(n, v)

    def piece(n, zz):
        return regions[n][1](group[n].w[0], group[n].b, zz)

    def gatherA(n, v):
        p = piece(n, z)
        p[...] = v.astype(BF)
        send(p, p, cs[n] + 5, zdev[2])
        send(p, p, cs[n] + 4, zdev[1])

    def gatherZ(n):
        p = piece(n, zk[2])
        recv(p, cs[n] + 5)
        send(p, p, cs[n] + 6, zdev[1])

    def gatherB(n):
        for k in (1, 3):
            recv(piece(n, zk[k]), cs[n] + 3 + k)
        h = regions[n][0](group[n].w[0], group[n].b)
        send(h, h, cs[n] + 8, group[n].dev[2])
        send(h, h, cs[n] + 7, group[n].bdev)
        send(h, h, cs[n] + 9, group[n].dev[1])

    def gatherC(n):
        h = regions[n][0](group[n].w[0], 1 - group[n].b)
        recv(h, cs[n] + 7)
        send(h, h, cs[n] + 10, group[n].dev[2])
        send(h, h, cs[n] + 11, group[n].dev[1])

    def gatherD(n):
        h = regions[n][0](group[n].w[2], group[n].b)
        recv(h, cs[n] + 8)
        send(h, h, cs[n] + 12, group[n].dev[1])

    def gatherE(n):
        h = regions[n][0](group[n].w[2], 1 - group[n].b)
        recv(h, cs[n] + 10)
        send(h, h, cs[n] + 13, group[n].dev[1])

    def gatherF(n):
        g = group[n]
        recv(regions[n][0](g.w[1], g.b), cs[n] + 9)
        recv(regions[n][0](g.w[1], 1 - g.b), cs[n] + 11)
        recv(regions[n][0](g.w[3], g.b), cs[n] + 12)
        recv(regions[n][0](g.w[3], 1 - g.b), cs[n] + 13)

    def share_branch():
        for k in (1, 2, 3):
            send(R.attg.at[gy.w[k]], R.xatt.at[:, slot("att", 0)], cx["att"] + k, gy.dev[k])
        share("gb", R.xgb)

    def heads_in():
        for k in (1, 2, 3):
            recv(R.gag.at[zk[k]], cg + k)
        for h in range(3):
            R.ga3[h] = jnp.concatenate([R.gag[j, :, 64 * h:64 * h + 64] for j in range(4)], axis=0)

    def backward(h):
        def part(j, _):
            qs = ds(j * 256, 256)
            gah = R.ga3[h, qs, :]
            p = jnp.concatenate([R.pt[h, 512 * i:512 * i + 512, qs].astype(F32) * R.stat[h, j, i:i + 1, :]
                                 for i in range(2)], axis=0)
            pd = p * dot(R.v3[h], gah, 1, 1)
            gr = (pd - p * colsum(pd)).astype(BF)
            dk = dot(gr, R.q3[h, qs, :])
            dv = dot(p.astype(BF), gah)
            R.dk[...] = R.dk[...] + dk
            R.dv[...] = R.dv[...] + dv
            R.half[h, :, qs] = dot(R.k3[h], gr, 0, 0) * 0.125
            return 0

        R.dk[...] = jnp.zeros((L, HD), F32)
        R.dv[...] = jnp.zeros((L, HD), F32)
        lax.fori_loop(0, 2, part, 0)
        for ref, lo in ((R.dk, 64 * h), (R.dv, 192 + 64 * h)):
            R.kvs[:, lo:lo + 64] = ref[theirs, :].astype(BF)
            R.kvo[:, lo:lo + 64] = ref[ours, :]

    ck, cd, cq, ctb, csm, ctz = chan(1), chan(4), cs["q"], cs["t"], chan(6), chan(4)
    theirs, ours = ds((1 - y) * 512, 512), ds(y * 512, 512)

    def kv_out():
        send(R.kvs, R.kvr, ck, ydev)

    def kv_in():
        recv(R.kvr, ck)
        kv = (R.kvo[...] + R.kvr[...].astype(F32)).astype(BF)
        gq = jnp.concatenate([R.half[h] for h in range(3)], axis=0).T.astype(BF)
        R.gqkv[...] = jnp.concatenate([gq, kv], axis=1)
        for k in (2, 1, 3):
            send(R.gqkv.at[ds(zk[k] * T, T), :], R.dqin.at[z], cd + k, zdev[k])
        R.dqin[z] = R.gqkv[ds(z * T, T), :]

    def q0():
        def other(i, _):
            R.qs0[ds(i * 128, 128), :] = dot(R.elow[:, ds((1 - c) * 384 + i * 128, 128)], R.gqkv[...], 0, 0).astype(BF)
            return 0

        def same(i, _):
            R.qp[ds(i * 128, 128), :] = dot(R.elow[:, ds(c * 384 + i * 128, 128)], R.gqkv[...], 0, 0)
            return 0

        lax.fori_loop(0, 3, other, 0)
        send(R.qs0, R.qr0, cq, rdev[1])
        lax.fori_loop(0, 3, same, 0)

    def q1():
        recv(R.qr0, cq)
        R.qs1[...] = (R.qp[ds((1 - x) * 192, 192), :]
                      + R.qr0[ds((1 - x) * 192, 192), :].astype(F32)).astype(BF)
        send(R.qs1, R.qr1, cq + 1, rdev[2])

    def qsum(o):
        return (R.qp[ds(x * 192 + o, 96), :] + R.qr0[ds(x * 192 + o, 96), :].astype(F32)
                + R.qr1[ds(o, 96), :].astype(F32))

    def q2():
        recv(R.qr1, cq + 1)
        R.qs2[...] = qsum((1 - y) * 96).astype(BF)
        send(R.qs2, R.qr2, cq + 2, ydev)

    def q3():
        recv(R.qr2, cq + 2)
        gatherA("q", qsum(y * 96) + R.qr2[...].astype(F32))

    def entry():
        for k in (1, 2, 3):
            recv(R.dqin.at[zk[k]], cd + k)
        gq, gk, gv = (jnp.concatenate([R.dqin[j, :, 192 * i:192 * i + 192] for j in range(4)], axis=1) for i in range(3))
        R.sm[0:1, :] = colsum(gq.astype(F32))
        R.sm[1:2, :] = colsum(gv.astype(F32))
        ge = R.own[...] + dot(gq, R.Gwq[...], 1, 1) + dot(gk, R.Gwk[...], 1, 1) + dot(gv, R.Gwv[...], 1, 1)
        gel = ge.astype(BF)
        R.gtok[...] = gel
        R.gp[...] = dot(hot_of(me, 512, 0), gel)
        R.sm[12:14, :] = dot(hot_of(me, 16, 512), gel)[0:2, :]
        R.ts0[...] = R.gp[ds((1 - c) * 256, 256), :].astype(BF)
        send(R.ts0, R.tr0, ctb, rdev[1])
        R.sms[0] = R.sm[...]
        send(R.sms.at[0], R.smr.at[0], csm, rdev[1])

    gt = group["t"]

    def t1():
        recv(R.tr0, ctb)
        a = gt.w[0] // 2
        R.ts1[...] = (R.gp[ds(c * 256 + (1 - a) * 128, 128), :]
                      + R.tr0[ds((1 - a) * 128, 128), :].astype(F32)).astype(BF)
        send(R.ts1, R.tr1, ctb + 1, gt.dev[2])
        recv(R.smr.at[0], csm)
        R.sms[1] = R.sms[0] + R.smr[0]
        send(R.sms.at[1], R.smr.at[1], csm + 1, rdev[2])

    def tsum(b):
        lanes, a = ds(b * 384, 384), gt.w[0] // 2
        return (R.gp[ds(c * 256 + a * 128, 128), lanes] + R.tr0[ds(a * 128, 128), lanes].astype(F32)
                + R.tr1[:, lanes].astype(F32))

    def t2():
        recv(R.tr1, ctb + 1)
        R.ts2[...] = tsum(1 - gt.b).astype(BF)
        send(R.ts2, R.tr2, ctb + 2, gt.bdev)
        recv(R.smr.at[1], csm + 1)
        R.sms[2] = R.sms[1] + R.smr[1]
        send(R.sms.at[2], R.smr.at[2], csm + 2, ydev)

    def t3():
        recv(R.tr2, ctb + 2)
        tv = tsum(gt.b) + R.tr2[...].astype(F32)
        R.ts3[...] = tv.astype(BF)
        for k in (2, 1, 3):
            send(R.ts3.at[ds(zk[k] * 32, 32), :], R.tr3.at[k], ctz + k, zdev[k])
        R.gp[0:128, 0:384] = tv
        recv(R.smr.at[2], csm + 2)
        R.sms[3] = R.sms[2] + R.smr[2]
        for k in (2, 1, 3):
            send(R.sms.at[3], R.smr.at[2 + k], csm + 2 + k, zdev[k])

    def t4():
        fin = R.gp[ds(z * 32, 32), 0:384]
        for k in (1, 2, 3):
            recv(R.tr3.at[k], ctz + k)
            fin = fin + R.tr3[k].astype(F32)
        gatherA("t", fin)
        total = R.sms[3]
        for k in (1, 2, 3):
            recv(R.smr.at[2 + k], csm + 2 + k)
            total = total + R.smr[2 + k]
        R.Gs[...] = total

    def assemble():
        gatherF("q")

        def part(i, _):
            m = ds(i * 128, 128)
            for t, out in enumerate((R.Gwq, R.Gwk, R.Gwv)):
                out[m, :] = jnp.concatenate([R.Gq[j, m, 192 * t:192 * t + 192] for j in range(4)], axis=1)
            return 0

        lax.fori_loop(0, 6, part, 0)

    tasks = {"gs": lambda: pass_on("gs", R.xgs), "gb": lambda: pass_on("gb", R.xgb), "sb": share_branch, "in": heads_in, "kv": kv_out,
             "vk": kv_in, "q0": q0, "q1": q1, "q2": q2, "q3": q3, "en": entry, "t1": t1, "t2": t2, "t3": t3, "t4": t4,
             "as": assemble}
    for h in range(3):
        tasks["h%d" % h] = partial(backward, h)
    for n in STREAMS:
        for stage, f in zip("12z3ABCDEF", (stage1, stage2, stage2z, stage3, gatherZ, gatherB, gatherC, gatherD, gatherE, gatherF), strict=True):
            tasks[stage + n] = partial(f, n)
    for name in ORDER:
        tasks[name]()
    for cp in pending:
        cp.wait_send()


def mega(*args):
    any_, vm = pl.BlockSpec(memory_space=pltpu.HBM), pl.BlockSpec(memory_space=VMEM)
    square = VMEM((D, D), BF)
    return pl.pallas_call(
        kernel,
        out_shape=(VMEM((T, D), BF), VMEM((T, D), BF), VMEM((F, D), BF), VMEM((D, F), BF), square, square, square, square,
                   VMEM((512, D), BF), VMEM((16, D), F32)),
        in_specs=[any_, any_, vm, vm, any_, vm] + [any_] * 6,
        out_specs=(vm,) * 10,
        scratch_shapes=list(scratch().values()),
        compiler_params=pltpu.CompilerParams(collective_id=0, has_side_effects=True, vmem_limit_bytes=41 << 20),
    )(*args)


def finish_kernel(layer, gtok, g2, g1, go, gq, gk, gv, gt, gs, layer_o, gtok_o, t_o, q_o, k_o, v_o, o_o, o1, o2, tab, buf, wide, sem, sem2):
    whole = [pltpu.make_async_copy(a, b, sem2.at[i]) for i, (a, b) in enumerate(((layer, layer_o), (gtok, gtok_o)))]
    for cp in whole:
        cp.start()
    tab[0:512, :] = gt[...].astype(F32)
    tab[512:514, :] = gs[12:14, :]
    whole.append(pltpu.make_async_copy(tab, t_o, sem2.at[2]))
    whole[-1].start()
    chunks = [(g2, o2, buf, i) for i in range(12)] + [(g1, o1, wide, i) for i in range(12)]
    chunks += [(a, b, buf, i) for a, b in ((go, o_o), (gq, q_o), (gk, k_o), (gv, v_o)) for i in range(3)]
    flying = {}
    for n, (src, dst, stage, i) in enumerate(chunks):
        rows = 256 if stage is buf else 64
        slot = n % 4
        if n >= 4:
            flying[slot].wait()
        stage[slot] = src[i * rows:(i + 1) * rows, :].astype(F32)
        flying[slot] = pltpu.make_async_copy(stage.at[slot], dst.at[i * rows:(i + 1) * rows, :], sem.at[slot])
        flying[slot].start()
    for slot in range(4):
        flying[slot].wait()
    for cp in whole:
        cp.wait()


def finish(*args):
    S = jax.ShapeDtypeStruct
    square = S((D, D), F32)
    hbm, vm = pl.BlockSpec(memory_space=pltpu.HBM), pl.BlockSpec(memory_space=VMEM)
    return pl.pallas_call(
        finish_kernel,
        out_shape=(S((T, D), BF), S((T, D), BF), S((514, D), F32), square, square, square, square, S((D, F), F32), S((F, D), F32)),
        in_specs=[vm] * 10,
        out_specs=(hbm,) * 9,
        scratch_shapes=[VMEM((514, D), F32), VMEM((4, 256, D), F32), VMEM((4, 64, F), F32), pltpu.SemaphoreType.DMA((4,)),
                        pltpu.SemaphoreType.DMA((3,))],
        compiler_params=pltpu.CompilerParams(vmem_limit_bytes=20 << 20),
    )(*args)


def fast_device(tokens, cotangent, segment_ids, restarts, position_table, query_weight, query_bias, key_weight,
                value_weight, value_bias, out_weight, out_bias, first_gain, first_shift, inner_weight, inner_bias,
                outer_weight, outer_bias, second_gain, second_shift):
    vectors = (query_bias, value_bias, out_bias, first_gain, first_shift, outer_bias, second_gain, second_shift)
    small, at = jnp.zeros((16 * D,), F32), 0
    for v in vectors + (inner_bias,):
        small = small + jnp.pad(v.astype(F32), (at, 16 * D - at - v.shape[0]))
        at += v.shape[0]
    small = small.reshape(16, D)
    made = mega(
        tokens[0], cotangent[0], segment_ids, restarts, position_table, small, query_weight,
        key_weight, value_weight, out_weight, inner_weight, outer_weight)
    layer, gtok, table, gq, gk, gv, go, g1, g2 = finish(*made)
    gs = made[-1]
    return (layer[None], gtok[None], table, gq, gs[0], gk, gv, gs[1], go, gs[2], gs[3], gs[4], g1, gs[8:12].reshape(F), g2,
            gs[5], gs[6], gs[7])


HEADS = 12


epsilon = 1e-05


def carried_in(array, axis, combine, identity):
    count, place = (lax.axis_size(axis), lax.axis_index(axis))
    everything = lax.all_gather(array, axis)
    start = jnp.broadcast_to(jnp.asarray(identity, array.dtype), array.shape)

    def hop(k, before):
        reached = k < place
        new = combine(before, everything[k])
        return jnp.where(reached, new, before)

    return lax.fori_loop(0, count, hop, start)


def matmul(left, right):
    return jnp.dot(left, right, preferred_element_type=jnp.float32)


def matmul_t(left, right):
    return lax.dot_general(
        left, right, (((1,), (1,)), ((), ())), preferred_element_type=jnp.float32
    )


def outer_sum(left, right):
    return lax.dot_general(
        left, right, (((0,), (0,)), ((), ())), preferred_element_type=jnp.float32
    )


def norm_forward(value, gain, shift):
    centered = value - jnp.mean(value, axis=-1, keepdims=True)
    spread = jnp.mean(centered * centered, axis=-1, keepdims=True)
    inverse = lax.rsqrt(spread + epsilon)
    normal = centered * inverse
    return (normal * gain.astype(jnp.float32) + shift.astype(jnp.float32), normal, inverse)


def norm_backward(incoming, normal, inverse, gain):
    scaled = incoming * gain.astype(jnp.float32)
    centred = scaled - jnp.mean(scaled, axis=-1, keepdims=True)
    outgoing = inverse * (centred - normal * jnp.mean(scaled * normal, axis=-1, keepdims=True))
    return (outgoing, jnp.sum(incoming * normal, axis=0), jnp.sum(incoming, axis=0))


def block_size(key_count):
    for option in (1024, 512):
        return option
    return key_count


def make_forward(queries, query_segs, score_scale):
    rows_here, tok_count, head_count, head_depth = queries.shape

    def step(carry, piece, start):
        key_rows, value_rows, key_segs = piece
        key_count = key_rows.shape[1]
        size = block_size(key_count)

        def one_block(index, state):
            highest, denom, accum = state
            begin = index * size
            keys_blk = lax.dynamic_slice_in_dim(key_rows, begin, size, 1).reshape(
                rows_here, size, head_count, head_depth
            )
            values_blk = lax.dynamic_slice_in_dim(value_rows, begin, size, 1).reshape(
                rows_here, size, head_count, head_depth
            )
            segs_blk = lax.dynamic_slice_in_dim(key_segs, begin, size, 1)
            scores = (
                jnp.einsum("rqhd,rkhd->rhqk", queries, keys_blk, preferred_element_type=jnp.float32)
                * score_scale
            )
            allowed = query_segs[:, None, :, None] == segs_blk[:, None, None, :]
            scores = jnp.where(allowed, scores, -jnp.inf)
            newest = jnp.maximum(highest, jnp.max(scores, axis=-1))
            weights = jnp.exp(scores - newest[..., None])
            factor = jnp.exp(highest - newest)
            denom = denom * factor + jnp.sum(weights, axis=-1)
            update = jnp.einsum(
                "rhqk,rkhd->rqhd",
                weights.astype(jnp.bfloat16),
                values_blk,
                preferred_element_type=jnp.float32,
            )
            accum = accum * jnp.swapaxes(factor, 1, 2)[..., None] + update
            return (newest, denom, accum)

        return lax.fori_loop(0, key_count // size, one_block, carry)

    return step


def make_backward(queries, query_segs, grad_attend, delta, logsum, score_scale):
    rows_here, tok_count, head_count, head_depth = queries.shape

    def step(carry, piece, start):
        key_rows, value_rows, key_segs = piece
        key_count = key_rows.shape[1]
        size = block_size(key_count)

        def one_block(index, state):
            begin = index * size
            keys_blk = lax.dynamic_slice_in_dim(key_rows, begin, size, 1).reshape(
                rows_here, size, head_count, head_depth
            )
            values_blk = lax.dynamic_slice_in_dim(value_rows, begin, size, 1).reshape(
                rows_here, size, head_count, head_depth
            )
            segs_blk = lax.dynamic_slice_in_dim(key_segs, begin, size, 1)
            scores = (
                jnp.einsum("rqhd,rkhd->rhqk", queries, keys_blk, preferred_element_type=jnp.float32)
                * score_scale
            )
            allowed = query_segs[:, None, :, None] == segs_blk[:, None, None, :]
            scores = jnp.where(allowed, scores, -jnp.inf)
            probs = jnp.exp(scores - logsum[..., None])
            grad_p = jnp.einsum(
                "rqhd,rkhd->rhqk", grad_attend, values_blk, preferred_element_type=jnp.float32
            )
            grad_s = (probs * (grad_p - delta[..., None]) * score_scale).astype(jnp.bfloat16)
            grad_q = state[0] + jnp.einsum(
                "rhqk,rkhd->rqhd", grad_s, keys_blk, preferred_element_type=jnp.float32
            )
            grad_k, grad_v = (state[1], state[2])
            grad_v_blk = jnp.einsum(
                "rhqk,rqhd->rkhd",
                probs.astype(jnp.bfloat16),
                grad_attend,
                preferred_element_type=jnp.float32,
            )
            grad_k_blk = jnp.einsum(
                "rhqk,rqhd->rkhd", grad_s, queries, preferred_element_type=jnp.float32
            )
            grad_k = lax.dynamic_update_slice_in_dim(
                grad_k, grad_k_blk.reshape(rows_here, size, head_count * head_depth), begin, 1
            )
            grad_v = lax.dynamic_update_slice_in_dim(
                grad_v, grad_v_blk.reshape(rows_here, size, head_count * head_depth), begin, 1
            )
            return (grad_q, grad_k, grad_v)

        return lax.fori_loop(0, key_count // size, one_block, carry)

    return step


def per_device(
    tokens,
    cotangent,
    segment_ids,
    restarts,
    position_table,
    query_weight,
    query_bias,
    key_weight,
    value_weight,
    value_bias,
    out_weight,
    out_bias,
    first_gain,
    first_shift,
    inner_weight,
    inner_bias,
    outer_weight,
    outer_bias,
    second_gain,
    second_shift,
):
    rows_here, tok_count, model_width = tokens.shape
    head_count = HEADS
    head_depth = model_width // head_count
    score_scale = head_depth ** (-0.5)
    flat_count = rows_here * tok_count
    row_length = tok_count * lax.axis_size("seq")
    offset = lax.axis_index("seq") * tok_count
    places = offset + jnp.arange(tok_count, dtype=jnp.int32)[None, :]
    marked = jnp.where(restarts == 1, places, -1)
    earlier = carried_in(
        jnp.max(marked, axis=1), "seq", jnp.maximum, jnp.full((rows_here,), -1, jnp.int32)
    )
    latest = jnp.maximum(lax.cummax(marked, axis=1), earlier[:, None])
    positions = places - latest + 2
    onehot = (
        positions.reshape(flat_count, 1)
        == jnp.arange(position_table.shape[0], dtype=jnp.int32)[None, :]
    )
    entry = tokens.reshape(flat_count, model_width).astype(jnp.float32) + matmul(
        onehot.astype(jnp.bfloat16), position_table
    )
    entry_low = entry.astype(jnp.bfloat16)
    queries = (matmul(entry_low, query_weight) + query_bias.astype(jnp.float32)).astype(
        jnp.bfloat16
    )
    keys_low = matmul(entry_low, key_weight).astype(jnp.bfloat16)
    values_low = (matmul(entry_low, value_weight) + value_bias.astype(jnp.float32)).astype(
        jnp.bfloat16
    )
    query_heads = queries.reshape(rows_here, tok_count, head_count, head_depth)
    key_rows = keys_low.reshape(rows_here, tok_count, model_width)
    value_rows = values_low.reshape(rows_here, tok_count, model_width)
    start_state = (
        jnp.full((rows_here, head_count, tok_count), -1e30, jnp.float32),
        jnp.zeros((rows_here, head_count, tok_count), jnp.float32),
        jnp.zeros((rows_here, tok_count, head_count, head_depth), jnp.float32),
    )
    forward_step = make_forward(query_heads, segment_ids, score_scale)
    highest, denom, accum = forward_step(
        start_state,
        (
            lax.all_gather(key_rows, "seq", axis=1, tiled=True),
            lax.all_gather(value_rows, "seq", axis=1, tiled=True),
            lax.all_gather(segment_ids, "seq", axis=1, tiled=True),
        ),
        jnp.int32(0),
    )
    attend = accum / jnp.swapaxes(denom, 1, 2)[..., None]
    logsum = highest + jnp.log(denom)
    attended_low = attend.reshape(flat_count, model_width).astype(jnp.bfloat16)
    branch = matmul(attended_low, out_weight) + out_bias.astype(jnp.float32)
    first, first_normal, first_inverse = norm_forward(entry + branch, first_gain, first_shift)
    first_low = first.astype(jnp.bfloat16)
    inner = matmul(first_low, inner_weight) + inner_bias.astype(jnp.float32)
    activation, gelu_back = jax.vjp(partial(jax.nn.gelu, approximate=False), inner)
    active_low = activation.astype(jnp.bfloat16)
    second_in = first + matmul(active_low, outer_weight) + outer_bias.astype(jnp.float32)
    result, second_normal, second_inverse = norm_forward(second_in, second_gain, second_shift)
    layer_out = result.astype(jnp.bfloat16).reshape(rows_here, tok_count, model_width)
    incoming = cotangent.reshape(flat_count, model_width).astype(jnp.float32)
    grad_second, grad_gsecond, grad_ssecond = norm_backward(
        incoming, second_normal, second_inverse, second_gain
    )
    grad_second_low = grad_second.astype(jnp.bfloat16)
    grad_wouter = outer_sum(active_low, grad_second_low)
    grad_bouter = jnp.sum(grad_second_low.astype(jnp.float32), axis=0)
    grad_inner_low = gelu_back(matmul_t(grad_second_low, outer_weight))[0].astype(jnp.bfloat16)
    grad_winner = outer_sum(first_low, grad_inner_low)
    grad_binner = jnp.sum(grad_inner_low.astype(jnp.float32), axis=0)
    grad_first = grad_second + matmul_t(grad_inner_low, inner_weight)
    grad_first_in, grad_gfirst, grad_sfirst = norm_backward(
        grad_first, first_normal, first_inverse, first_gain
    )
    grad_branch_low = grad_first_in.astype(jnp.bfloat16)
    grad_wout = outer_sum(attended_low, grad_branch_low)
    grad_bout = jnp.sum(grad_branch_low.astype(jnp.float32), axis=0)
    grad_attend = (
        matmul_t(grad_branch_low, out_weight)
        .astype(jnp.bfloat16)
        .reshape(rows_here, tok_count, head_count, head_depth)
    )
    delta_rows = jnp.sum(grad_attend.astype(jnp.float32) * attend, axis=-1)
    delta = jnp.swapaxes(delta_rows, 1, 2)
    query_zero = jnp.zeros((rows_here, tok_count, head_count, head_depth), jnp.float32)
    back_state = (
        query_zero,
        jnp.zeros((rows_here, row_length, model_width), jnp.float32),
        jnp.zeros((rows_here, row_length, model_width), jnp.float32),
    )
    backward_step = make_backward(query_heads, segment_ids, grad_attend, delta, logsum, score_scale)
    back_out = backward_step(
        back_state,
        (
            lax.all_gather(key_rows, "seq", axis=1, tiled=True),
            lax.all_gather(value_rows, "seq", axis=1, tiled=True),
            lax.all_gather(segment_ids, "seq", axis=1, tiled=True),
        ),
        jnp.int32(0),
    )
    grad_q = back_out[0]
    grad_keys, grad_values = (
        lax.psum_scatter(back_out[1], "seq", scatter_dimension=1, tiled=True),
        lax.psum_scatter(back_out[2], "seq", scatter_dimension=1, tiled=True),
    )
    grad_query_low = grad_q.reshape(flat_count, model_width).astype(jnp.bfloat16)
    grad_key_low = grad_keys.reshape(flat_count, model_width).astype(jnp.bfloat16)
    grad_value_low = grad_values.reshape(flat_count, model_width).astype(jnp.bfloat16)
    grad_entry = (
        grad_first_in
        + matmul_t(grad_query_low, query_weight)
        + matmul_t(grad_key_low, key_weight)
        + matmul_t(grad_value_low, value_weight)
    )
    grad_wquery = outer_sum(entry_low, grad_query_low)
    grad_bquery = jnp.sum(grad_query_low.astype(jnp.float32), axis=0)
    grad_wkey = outer_sum(entry_low, grad_key_low)
    grad_wvalue = outer_sum(entry_low, grad_value_low)
    grad_bvalue = jnp.sum(grad_value_low.astype(jnp.float32), axis=0)
    grad_table = lax.dot_general(
        onehot.astype(jnp.float32),
        grad_entry,
        (((0,), (0,)), ((), ())),
        precision=lax.Precision.HIGHEST,
        preferred_element_type=jnp.float32,
    )
    grad_tokens = grad_entry.astype(jnp.bfloat16).reshape(rows_here, tok_count, model_width)
    pieces = (
        lax.psum_scatter(grad_wquery, "seq", scatter_dimension=0, tiled=True),
        lax.psum_scatter(grad_wkey, "seq", scatter_dimension=0, tiled=True),
        lax.psum_scatter(grad_wvalue, "seq", scatter_dimension=0, tiled=True),
        lax.psum_scatter(grad_wout, "seq", scatter_dimension=0, tiled=True),
        lax.psum_scatter(grad_winner, "seq", scatter_dimension=0, tiled=True),
        lax.psum_scatter(grad_wouter, "seq", scatter_dimension=0, tiled=True),
    )
    pieces = (
        lax.psum(pieces[0].astype(jnp.bfloat16), "rows").astype(jnp.float32),
        lax.psum(pieces[1].astype(jnp.bfloat16), "rows").astype(jnp.float32),
        lax.psum(pieces[2].astype(jnp.bfloat16), "rows").astype(jnp.float32),
        lax.psum(pieces[3].astype(jnp.bfloat16), "rows").astype(jnp.float32),
        lax.psum(pieces[4].astype(jnp.bfloat16), "rows").astype(jnp.float32),
        lax.psum(pieces[5].astype(jnp.bfloat16), "rows").astype(jnp.float32),
    )
    total_wquery, total_wkey, total_wvalue, total_wout, total_winner, total_wouter = (
        lax.all_gather(pieces[0].astype(jnp.bfloat16), "seq", axis=0, tiled=True).astype(
            jnp.float32
        ),
        lax.all_gather(pieces[1].astype(jnp.bfloat16), "seq", axis=0, tiled=True).astype(
            jnp.float32
        ),
        lax.all_gather(pieces[2].astype(jnp.bfloat16), "seq", axis=0, tiled=True).astype(
            jnp.float32
        ),
        lax.all_gather(pieces[3].astype(jnp.bfloat16), "seq", axis=0, tiled=True).astype(
            jnp.float32
        ),
        lax.all_gather(pieces[4].astype(jnp.bfloat16), "seq", axis=0, tiled=True).astype(
            jnp.float32
        ),
        lax.all_gather(pieces[5].astype(jnp.bfloat16), "seq", axis=0, tiled=True).astype(
            jnp.float32
        ),
    )
    smalls = lax.psum(
        (
            grad_table,
            grad_bquery,
            grad_bvalue,
            grad_bout,
            grad_gfirst,
            grad_sfirst,
            grad_binner,
            grad_bouter,
            grad_gsecond,
            grad_ssecond,
        ),
        ("seq", "rows"),
    )
    (
        total_table,
        total_bquery,
        total_bvalue,
        total_bout,
        total_gfirst,
        total_sfirst,
        total_binner,
        total_bouter,
        total_gsecond,
        total_ssecond,
    ) = smalls
    return (
        layer_out,
        grad_tokens,
        total_table,
        total_wquery,
        total_bquery,
        total_wkey,
        total_wvalue,
        total_bvalue,
        total_wout,
        total_bout,
        total_gfirst,
        total_sfirst,
        total_winner,
        total_binner,
        total_wouter,
        total_bouter,
        total_gsecond,
        total_ssecond,
    )


def solution(mesh):
    in_specs = (
        P("rows", "seq", None),
        P("rows", "seq", None),
        P("rows", "seq"),
        P("rows", "seq"),
        P(),
        P(),
        P(),
        P(),
        P(),
        P(),
        P(),
        P(),
        P(),
        P(),
        P(),
        P(),
        P(),
        P(),
        P(),
        P(),
    )
    out_specs = (
        P("rows", "seq", None),
        P("rows", "seq", None),
        P(),
        P(),
        P(),
        P(),
        P(),
        P(),
        P(),
        P(),
        P(),
        P(),
        P(),
        P(),
        P(),
        P(),
        P(),
        P(),
    )
    body = fast_device if mesh.shape["seq"] == 8 and mesh.shape["rows"] == 4 else per_device
    return jax.shard_map(
        body, mesh=mesh, in_specs=in_specs, out_specs=out_specs, check_vma=False
    )
```

```python
from functools import partial
from types import SimpleNamespace

import jax
import jax.numpy as jnp
from jax import lax
from jax.experimental import pallas as pl
from jax.experimental.pallas import tpu as pltpu
from jax.sharding import PartitionSpec as P

MESH = pl.DeviceIdType.MESH
VMEM = pltpu.VMEM
BF, F32, I32 = jnp.bfloat16, jnp.float32, jnp.int32
T, D, F, L, HD = 128, 768, 3072, 1024, 64
EPS = 1e-5
CHANNELS = 240
ROWS_OF = {"2a": 384, "2b": 384, "1a": 384, "1b": 384, "o": 192}
STREAMS = tuple(ROWS_OF) + ("q", "t")
ORDER = (
    "sb", "gs", "11a", "in", "12a", "h0", "h1", "gb", "11b", "21a", "22a", "h2", "z1a", "21b", "kv", "12b", "1o",
    "z2a", "31a", "A1a", "32a", "B1a", "z1b", "A2a", "vk", "q0", "q1", "B2a", "31b", "C2a", "2o", "q2", "C1a", "en",
    "A1b", "q3", "t1", "B1b", "Aq", "E2a", "22b", "zo", "t2", "Bq", "3o", "z2b", "Ao", "32b", "D2a", "D1b", "C1b",
    "t3", "Bo", "Cq", "A2b", "Co", "B2b", "t4", "E1b", "Dq", "Eo", "At", "F2a", "Do", "Eq", "Bt", "C2b", "D1a", "Dt",
    "Ct", "as", "D2b", "E1a", "F1b", "Et", "Fo", "Ft", "E2b", "F1a", "F2b",
)


def dot(a, b, ca=1, cb=0):
    return lax.dot_general(a, b, (((ca,), (cb,)), ((), ())), preferred_element_type=F32)


def ds(start, size, step=None):
    return pl.ds(pl.multiple_of(start, step or size), size)


def scratch():
    s = {}
    s["tok"] = VMEM((8, T, D), BF)
    s["meta"] = VMEM((8, 8, T), I32)
    s["tail"] = VMEM((16, D), BF)
    s["table"] = VMEM((514, D), BF)
    s["cot"] = VMEM((T, D), BF)
    s["pos"] = VMEM((8, 8, T), I32)
    s["segc"] = VMEM((L, T), F32)
    s["segq"] = VMEM((2, 8, 256), F32)
    s["elow"] = VMEM((4 * T, D), BF)
    s["q3"] = VMEM((3, 512, HD), BF)
    s["k3"] = VMEM((3, L, HD), BF)
    s["v3"] = VMEM((3, L, HD), BF)
    s["pt"] = VMEM((3, L, 512), BF)
    s["stat"] = VMEM((3, 2, 8, 256), F32)
    s["half"] = VMEM((3, HD, 512), F32)
    s["attcat"] = VMEM((4, 192, T), BF)
    s["attg"] = VMEM((4, 192, T), BF)
    s["own"] = VMEM((T, D), F32)
    for n in ("first", "act", "gs", "gi", "gb"):
        s["x" + n] = VMEM((4 * T, D), BF)
    s["xatt"] = VMEM((192, 4 * T), BF)
    s["gp"] = VMEM((4 * T, D), F32)
    s["gaout"] = VMEM((4, T, 192), BF)
    s["gag"] = VMEM((4, T, 192), BF)
    s["ga3"] = VMEM((3, 512, HD), BF)
    s["dk"] = VMEM((L, HD), F32)
    s["dv"] = VMEM((L, HD), F32)
    s["kvo"] = VMEM((512, 384), F32)
    s["kvs"] = VMEM((512, 384), BF)
    s["kvr"] = VMEM((512, 384), BF)
    s["gqkv"] = VMEM((512, 576), BF)
    s["dqin"] = VMEM((4, T, 576), BF)
    for n, m in ROWS_OF.items():
        s["bs" + n] = VMEM((m, 384), BF)
        s["br" + n] = VMEM((m, 384), BF)
        s["ac" + n] = VMEM((m, 384), F32)
        s["zr" + n] = VMEM((3, m // 4, 384), BF)
    s["qp"] = VMEM((384, 576), F32)
    for i, m in ((0, 384), (1, 192), (2, 96)):
        s["qs%d" % i] = VMEM((m, 576), BF)
        s["qr%d" % i] = VMEM((m, 576), BF)
    s["Gq"] = VMEM((4, D, 576), BF)
    for i, m in ((0, 256), (1, 128)):
        s["ts%d" % i] = VMEM((m, D), BF)
        s["tr%d" % i] = VMEM((m, D), BF)
    s["ts2"] = VMEM((128, 384), BF)
    s["tr2"] = VMEM((128, 384), BF)
    s["ts3"] = VMEM((128, 384), BF)
    s["tr3"] = VMEM((4, 32, 384), BF)
    s["sm"] = VMEM((16, D), F32)
    s["sms"] = VMEM((4, 16, D), F32)
    s["smr"] = VMEM((6, 16, D), F32)
    s["wsem"] = pltpu.SemaphoreType.DMA((9,))
    s["ss"] = pltpu.SemaphoreType.DMA((CHANNELS,))
    s["rs"] = pltpu.SemaphoreType.DMA((CHANNELS,))
    return s


INPUTS = ("tokens", "hcot", "segs", "rests", "htable", "small", "hq", "hk", "hv", "ho", "h1", "h2")
OUTPUTS = ("layer", "gtok", "G2", "G1", "Go", "Gwq", "Gwk", "Gwv", "Gt", "Gs")


def kernel(*refs):
    names = INPUTS + OUTPUTS + tuple(scratch())
    R = SimpleNamespace(**dict(zip(names, refs, strict=True)))
    seq, row = lax.axis_index("seq"), lax.axis_index("rows")
    z, y, x, c = seq // 2, seq % 2, row // 2, row % 2
    zk = [z, z + 1 - 2 * (z % 2), (z + 2) % 4, 3 - z]
    rk = [row, x * 2 + (1 - c), (1 - x) * 2 + c, (1 - x) * 2 + (1 - c)]
    zdev = [(zk[k] * 2 + y, row) for k in range(4)]
    ydev = (z * 2 + (1 - y), row)
    rdev = [(seq, rk[k]) for k in range(4)]
    counter = [0]
    pending = []

    def chan(n=1):
        counter[0] += n
        assert counter[0] <= CHANNELS
        return counter[0] - n

    def copy(src, dst, i, dev):
        return pltpu.make_async_remote_copy(src, dst, R.ss.at[i], R.rs.at[i], device_id=dev, device_id_type=MESH)

    def send(src, dst, i, dev):
        cp = copy(src, dst, i, dev)
        cp.start()
        pending.append(cp)

    def recv(dst, i):
        copy(dst, dst, i, ydev).wait_recv()

    yxdev = (z * 2 + (1 - y), x * 2 + (1 - c))
    gx = SimpleNamespace(w=[row, *rk[1:]], dev=rdev, b=y, bdev=ydev)
    wy = y * 2 + c
    gy = SimpleNamespace(w=[wy, y * 2 + (1 - c), (1 - y) * 2 + c, (1 - y) * 2 + (1 - c)],
                         dev=[(seq, row), rdev[1], ydev, yxdev], b=x, bdev=rdev[2])
    group = {n: gy if n[0] in "1ot" else gx for n in STREAMS}
    group.update(first=gy, gi=gy, att=gy, gb=gy, act=gx, gs=gx)

    seqpeers = [zdev[1], zdev[2], zdev[3]] + [(zk[k] * 2 + (1 - y), row) for k in range(4)]
    peers = seqpeers + rdev[1:] + [yxdev]
    bar = pltpu.get_barrier_semaphore()
    for p in peers:
        pl.semaphore_signal(bar, inc=1, device_id=p, device_id_type=MESH)

    loads = {}
    weights = (("n", R.tokens, R.tok.at[y * 4 + z]), ("t", R.htable, R.table), ("k", R.hk, R.Gwk), ("v", R.hv, R.Gwv), ("q", R.hq, R.Gwq), ("c", R.hcot, R.cot), ("o", R.ho, R.Go), ("1", R.h1, R.G1), ("2", R.h2, R.G2))

    def load(i):
        n, src, dst = weights[i]
        loads[n] = pltpu.make_async_copy(src, dst, R.wsem.at[i])
        loads[n].start()

    for i in range(5):
        load(i)

    me = y * 4 + z
    R.meta[me] = jnp.zeros((8, T), I32)
    R.meta[me, 0:1, :] = R.rests[...]
    R.meta[me, 1:2, :] = R.segs[...]
    pl.semaphore_wait(bar, len(peers))
    loads["n"].wait()
    cm = chan(7)
    metas = []
    for i, dev in enumerate(seqpeers):
        cp = copy(R.meta.at[me], R.meta.at[me], cm + i, dev)
        cp.start()
        metas.append(cp)
    ct = chan(16)
    tokens_out = []

    def half_of(b, h):
        return R.tok.at[b, 64 * h:64 * h + 64, :]

    def forward(b, i, h, dev):
        tokens_out.append(copy(half_of(b, h), half_of(b, h), ct + 2 * i + h, dev))
        tokens_out[-1].start()

    for h in range(2):
        forward(me, 1, h, zdev[1])
        forward(me, 4, h, ydev)
    for h in range(2):
        forward(me, 2, h, zdev[2])
    for i in range(5, 9):
        load(i)
    loads["t"].wait()
    R.tail[...] = jnp.zeros((16, D), BF)
    R.tail[0:2, :] = R.table[512:514, :]
    for cp in metas:
        cp.wait()
    lane = lax.broadcasted_iota(I32, (8, T), 1)
    spot = lax.broadcasted_iota(I32, (8, T), 0) * T + lane
    block_of = [(s % 2) * 4 + s // 2 for s in range(8)]
    flags = jnp.concatenate([R.meta[b, 0:1, :] for b in block_of], axis=0)
    mk = jnp.where(flags == 1, spot, -1)
    k = 1
    while k < T:
        mk = jnp.where(lane >= k, jnp.maximum(mk, pltpu.roll(mk, k, axis=1)), mk)
        k *= 2
    tot = jnp.max(mk, axis=1, keepdims=True)
    carry = jnp.full((1, 1), -1, I32)
    for s, b in enumerate(block_of):
        late = jnp.maximum(mk[s:s + 1, :], carry)
        R.pos[b, 0:1, :] = spot[s:s + 1, :] - late + 2
        carry = jnp.maximum(carry, tot[s:s + 1, :])
    for b in range(8):
        R.segc[b * T:(b + 1) * T, :] = jnp.broadcast_to(R.meta[b, 1:2, :], (T, T)).astype(F32).T
    for j in range(2):
        R.segq[j, 0:1, :] = jnp.concatenate([R.meta[y * 4 + 2 * j + i, 1:2, :] for i in range(2)], axis=1).astype(F32)

    off = pl.multiple_of(128 * ((3 * z) // 2), 128)
    odd = (z % 2) == 1

    def window(v):
        return jnp.where(odd, v[:, 64:256], v[:, 0:192])

    bq = R.small[0:1, pl.ds(off, 256)]
    bv = R.small[1:2, pl.ds(off, 256)]
    for n in "kvq":
        loads[n].wait()

    def hot_of(b, size, start):
        return (lax.broadcasted_iota(I32, (size, T), 0) + start == R.pos[b, 0:1, :]).astype(BF)

    def block(b, with_q):
        e = dot(hot_of(b, 512, 0), R.table[0:512, :], 0, 0) + dot(hot_of(b, 16, 512), R.tail[...], 0, 0)
        e = e + R.tok[b].astype(F32)
        el = e.astype(BF)
        here = ds(b * T, T)
        kk = window(dot(el, R.Gwk[:, pl.ds(off, 256)])).astype(BF)
        vv = window(dot(el, R.Gwv[:, pl.ds(off, 256)]) + bv).astype(BF)
        for h in range(3):
            R.k3[h, here, :] = kk[:, 64 * h:64 * h + 64]
            R.v3[h, here, :] = vv[:, 64 * h:64 * h + 64]
        if with_q:
            qq = (window(dot(el, R.Gwq[:, pl.ds(off, 256)]) + bq) * 0.125).astype(BF)
            there = ds((b - y * 4) * T, T)
            R.elow[there, :] = el
            for h in range(3):
                R.q3[h, there, :] = qq[:, 64 * h:64 * h + 64]
        return e

    R.own[...] = block(me, True)

    for k in (1, 2, 3):
        b = y * 4 + zk[k]
        for h in range(2):
            recv(half_of(b, h), ct + 2 * k + h)
            if k == 2:
                forward(b, 3, h, zdev[1])
            forward(b, 4 + k, h, ydev)
        block(b, True)

    def scores(h, j, parity):
        rows, qs = ds(parity * 512, 512), ds(j * 256, 256)
        s = dot(R.k3[h, rows, :], R.q3[h, qs, :], 1, 1)
        sc = R.segc[rows, :]
        s = jnp.where(jnp.concatenate([sc, sc], axis=1) == R.segq[j, 0:1, :], s, -1e30)
        top = jnp.max(s, axis=0, keepdims=True)
        p = jnp.exp(s - top)
        low = p.astype(BF)
        R.pt[h, rows, qs] = low
        return top, jnp.sum(p, axis=0, keepdims=True), dot(R.v3[h, rows, :], low, 0, 0)

    def attend_near(i, _):
        h, j = i // 2, i % 2
        top, den, acc = scores(h, j, y)
        R.stat[h, j, 2:3, :] = top
        R.stat[h, j, 3:4, :] = den
        R.half[h, :, ds(j * 256, 256)] = acc
        return 0

    def attend_far(i, _):
        h, j = i // 2, i % 2
        top, den, acc = scores(h, j, 1 - y)
        top0 = R.stat[h, j, 2:3, :]
        most = jnp.maximum(top, top0)
        f, f0 = jnp.exp(top - most), jnp.exp(top0 - most)
        inv = 1.0 / (den * f + R.stat[h, j, 3:4, :] * f0)
        f, f0 = f * inv, f0 * inv
        R.stat[h, j, pl.ds(y, 1), :] = f0
        R.stat[h, j, pl.ds(1 - y, 1), :] = f
        qs = ds(j * 256, 256)
        R.half[h, :, qs] = acc * f + R.half[h, :, qs] * f0
        return 0

    lax.fori_loop(0, 6, attend_near, 0)
    for k in (0, 1, 2, 3):
        b = (1 - y) * 4 + zk[k]
        for h in range(2):
            recv(half_of(b, h), ct + 8 + 2 * k + h)
        block(b, False)
    ca = chan(12)

    def head_of(ref, j, h):
        return ref.at[j, 64 * h:64 * h + 64, :]

    for h in range(3):
        lax.fori_loop(2 * h, 2 * h + 2, attend_far, 0)
        for j in range(4):
            R.attcat[j, 64 * h:64 * h + 64, :] = R.half[h, :, j * T:(j + 1) * T].astype(BF)
        for k in (2, 1, 3):
            send(head_of(R.attcat, zk[k], h), head_of(R.attg, z, h), ca + 3 * k + h, zdev[k])
    R.attg[z] = R.attcat[z]
    for n in "co12":
        loads[n].wait()
    for cp in tokens_out:
        cp.wait_send()
    for k in (1, 2, 3):
        for h in range(3):
            recv(head_of(R.attg, zk[k], h), ca + 3 * k + h)

    def slot(n, k):
        return ds(group[n].w[k] * T, T)

    def small(i):
        return R.small[i:i + 1, :]

    def colsum(v):
        return jnp.sum(v, axis=0, keepdims=True)

    def mean(v):
        return jnp.mean(v, axis=-1, keepdims=True)

    R.sm[...] = jnp.zeros((16, D), F32)
    cx = {n: chan(4) for n in ("first", "act", "att", "gs", "gi", "gb")}

    def share(n, ref):
        mine = ref.at[slot(n, 0), :]
        send(mine, mine, cx[n] + 2, group[n].dev[2])
        send(mine, mine, cx[n] + 1, group[n].dev[1])

    def pass_on(n, ref):
        theirs = ref.at[slot(n, 2), :]
        recv(theirs, cx[n] + 2)
        send(theirs, theirs, cx[n] + 3, group[n].dev[1])

    u = R.own[...] + dot(jnp.concatenate([R.attg[j] for j in range(4)], axis=0), R.Go[...], 0, 0) + small(2)
    u = u - mean(u)
    inv1 = lax.rsqrt(mean(u * u) + EPS)
    n1 = u * inv1
    first = n1 * small(3) + small(4)
    first_low = first.astype(BF)
    R.xfirst[slot("first", 0), :] = first_low
    share("first", R.xfirst)
    second = jnp.zeros((T, D), F32)
    for k in (2, 3, 1, 0):
        q = gx.w[k]
        cols = ds(q * D, D)
        inner = dot(first_low, R.G1[:, cols]) + R.small[pl.ds(8 + q, 1), :]
        phi = 0.5 * (1.0 + lax.erf(inner * 0.7071067811865476))
        R.gp[ds(q * T, T), :] = phi + inner * (0.3989422804014327 * jnp.exp(-0.5 * inner * inner))
        act = (inner * phi).astype(BF)
        if k:
            R.tok[k] = act
            send(R.tok.at[k], R.xact.at[slot("act", 0), :], cx["act"] + k, gx.dev[k])
        else:
            R.xact[slot("act", 0), :] = act
        second = second + dot(act, R.G2[cols, :])
    R.xatt[:, slot("att", 0)] = R.attg[gy.w[0]]
    u = first + second + small(5)
    u = u - mean(u)
    inv2 = lax.rsqrt(mean(u * u) + EPS)
    n2 = u * inv2
    R.layer[...] = (n2 * small(6) + small(7)).astype(BF)
    g = R.cot[...].astype(F32)
    R.sm[6:7, :] = colsum(g * n2)
    R.sm[7:8, :] = colsum(g)
    sc = g * small(6)
    gs = inv2 * (sc - mean(sc) - n2 * mean(sc * n2))
    gs_low = gs.astype(BF)
    R.xgs[slot("gs", 0), :] = gs_low
    share("gs", R.xgs)
    R.sm[5:6, :] = colsum(gs_low.astype(F32))
    pass_on("first", R.xfirst)
    for k in (2, 3, 1, 0):
        q = gy.w[k]
        cols = ds(q * D, D)
        gi = (dot(gs_low, R.G2[cols, :], 1, 1) * R.gp[ds(q * T, T), :]).astype(BF)
        if k:
            R.tok[4 + k] = gi
            send(R.tok.at[4 + k], R.xgi.at[slot("gi", 0), :], cx["gi"] + k, gy.dev[k])
        else:
            R.xgi[slot("gi", 0), :] = gi
        R.sm[pl.ds(8 + q, 1), :] = colsum(gi.astype(F32))
        gs = gs + dot(gi, R.G1[:, cols], 1, 1)
    R.sm[3:4, :] = colsum(gs * n1)
    R.sm[4:5, :] = colsum(gs)
    sc = gs * small(3)
    gfi = inv1 * (sc - mean(sc) - n1 * mean(sc * n1))
    R.own[...] = gfi
    gb = gfi.astype(BF)
    R.xgb[slot("gb", 0), :] = gb
    ga = dot(gb, R.Go[...], 1, 1).astype(BF)
    for j in range(4):
        R.gaout[j] = ga[:, 192 * j:192 * j + 192]
    cg = chan(4)
    for k in (2, 1, 3):
        send(R.gaout.at[zk[k]], R.gag.at[z], cg + k, zdev[k])
    R.gag[z] = R.gaout[z]
    R.sm[2:3, :] = colsum(gb.astype(F32))

    def two(h):
        lo = 384 * h
        return (lambda w, b: R.G2.at[ds(w * 768 + lo, 384), ds(b * 384, 384)],
                lambda w, b, zz: R.G2.at[ds(w * 768 + lo + zz * 96, 96), ds(b * 384, 384)])

    def one(h):
        lo = 384 * h
        return (lambda w, b: R.G1.at[lo:lo + 384, ds(w * 768 + b * 384, 384)],
                lambda w, b, zz: R.G1.at[ds(lo + zz * 96, 96), ds(w * 768 + b * 384, 384)])

    regions = {
        "2a": two(0), "2b": two(1), "1a": one(0), "1b": one(1),
        "o": (lambda w, b: R.Go.at[ds(w * 192, 192), ds(b * 384, 384)],
              lambda w, b, zz: R.Go.at[ds(w * 192 + zz * 48, 48), ds(b * 384, 384)]),
        "q": (lambda w, b: R.Gq.at[:, ds((w % 2) * 384 + (w // 2) * 192 + b * 96, 96), :],
              lambda w, b, zz: R.Gq.at[zz, ds((w % 2) * 384 + (w // 2) * 192 + b * 96, 96), :]),
        "t": (lambda w, b: R.Gt.at[ds((w % 2) * 256 + (w // 2) * 128, 128), ds(b * 384, 384)],
              lambda w, b, zz: R.Gt.at[ds((w % 2) * 256 + (w // 2) * 128 + zz * 32, 32), ds(b * 384, 384)]),
    }
    operands = {"2a": (R.xact, 0, R.xgs), "2b": (R.xact, 384, R.xgs), "1a": (R.xfirst, 0, R.xgi), "1b": (R.xfirst, 384, R.xgi)}
    cs = {n: chan(15) for n in STREAMS}
    arrived = set()

    def ready(n, ref, forwarded=True):
        if n not in arrived:
            arrived.add(n)
            for k in ((1, 3) if forwarded else (1, 2, 3)):
                recv(ref.at[:, slot(n, k)] if n == "att" else ref.at[slot(n, k), :], cx[n] + k)

    def stage1(n):
        acc, bs, br = getattr(R, "ac" + n), getattr(R, "bs" + n), getattr(R, "br" + n)
        b = group[n].b
        if n == "o":
            ready("att", R.xatt, False)
            ready("gb", R.xgb)
            bs[...] = dot(R.xatt[...], R.xgb[:, ds((1 - b) * 384, 384)]).astype(BF)
            send(bs, br, cs[n], group[n].bdev)
            acc[...] = dot(R.xatt[...], R.xgb[:, ds(b * 384, 384)])
            return
        if n[0] == "2":
            ready("act", R.xact, False)
            ready("gs", R.xgs)
        else:
            ready("gi", R.xgi, False)
            ready("first", R.xfirst)
        lhs, lo, rhs = operands[n]

        def other(i, _):
            bs[ds(i * 128, 128), :] = dot(lhs[:, ds(lo + i * 128, 128)], rhs[:, ds((1 - b) * 384, 384)], 0, 0).astype(BF)
            return 0

        def same(i, _):
            acc[ds(i * 128, 128), :] = dot(lhs[:, ds(lo + i * 128, 128)], rhs[:, ds(b * 384, 384)], 0, 0)
            return 0

        lax.fori_loop(0, 3, other, 0)
        send(bs, br, cs[n], group[n].bdev)
        lax.fori_loop(0, 3, same, 0)

    def stage2(n):
        acc, br, zr = (getattr(R, a + n) for a in ("ac", "br", "zr"))
        recv(br, cs[n])
        q = ROWS_OF[n] // 4
        for k in (3, 1, 2, 0):
            m = ds(zk[k] * q, q)
            v = acc[m, :] + br[m, :].astype(F32)
            if k % 2:
                br[m, :] = v.astype(BF)
                send(br.at[m, :], zr.at[k // 2], cs[n] + 1 + k // 2, zdev[1])
            else:
                acc[m, :] = v

    def stage2z(n):
        acc, br, zr = (getattr(R, a + n) for a in ("ac", "br", "zr"))
        recv(zr.at[1], cs[n] + 2)
        q = ROWS_OF[n] // 4
        m = ds(zk[2] * q, q)
        br[m, :] = (acc[m, :] + zr[1].astype(F32)).astype(BF)
        send(br.at[m, :], zr.at[2], cs[n] + 3, zdev[2])

    def stage3(n):
        acc, zr = getattr(R, "ac" + n), getattr(R, "zr" + n)
        q = ROWS_OF[n] // 4
        v = acc[ds(z * q, q), :]
        for i in (0, 2):
            recv(zr.at[i], cs[n] + 1 + i)
            v = v + zr[i].astype(F32)
        gatherA(n, v)

    def piece(n, zz):
        return regions[n][1](group[n].w[0], group[n].b, zz)

    def gatherA(n, v):
        p = piece(n, z)
        p[...] = v.astype(BF)
        send(p, p, cs[n] + 5, zdev[2])
        send(p, p, cs[n] + 4, zdev[1])

    def gatherZ(n):
        p = piece(n, zk[2])
        recv(p, cs[n] + 5)
        send(p, p, cs[n] + 6, zdev[1])

    def gatherB(n):
        for k in (1, 3):
            recv(piece(n, zk[k]), cs[n] + 3 + k)
        h = regions[n][0](group[n].w[0], group[n].b)
        send(h, h, cs[n] + 8, group[n].dev[2])
        send(h, h, cs[n] + 7, group[n].bdev)
        send(h, h, cs[n] + 9, group[n].dev[1])

    def gatherC(n):
        h = regions[n][0](group[n].w[0], 1 - group[n].b)
        recv(h, cs[n] + 7)
        send(h, h, cs[n] + 10, group[n].dev[2])
        send(h, h, cs[n] + 11, group[n].dev[1])

    def gatherD(n):
        h = regions[n][0](group[n].w[2], group[n].b)
        recv(h, cs[n] + 8)
        send(h, h, cs[n] + 12, group[n].dev[1])

    def gatherE(n):
        h = regions[n][0](group[n].w[2], 1 - group[n].b)
        recv(h, cs[n] + 10)
        send(h, h, cs[n] + 13, group[n].dev[1])

    def gatherF(n):
        g = group[n]
        recv(regions[n][0](g.w[1], g.b), cs[n] + 9)
        recv(regions[n][0](g.w[1], 1 - g.b), cs[n] + 11)
        recv(regions[n][0](g.w[3], g.b), cs[n] + 12)
        recv(regions[n][0](g.w[3], 1 - g.b), cs[n] + 13)

    def share_branch():
        for k in (1, 2, 3):
            send(R.attg.at[gy.w[k]], R.xatt.at[:, slot("att", 0)], cx["att"] + k, gy.dev[k])
        share("gb", R.xgb)

    def heads_in():
        for k in (1, 2, 3):
            recv(R.gag.at[zk[k]], cg + k)
        for h in range(3):
            R.ga3[h] = jnp.concatenate([R.gag[j, :, 64 * h:64 * h + 64] for j in range(4)], axis=0)

    def backward(h):
        def part(j, _):
            qs = ds(j * 256, 256)
            gah = R.ga3[h, qs, :]
            p = jnp.concatenate([R.pt[h, 512 * i:512 * i + 512, qs].astype(F32) * R.stat[h, j, i:i + 1, :]
                                 for i in range(2)], axis=0)
            pd = p * dot(R.v3[h], gah, 1, 1)
            gr = (pd - p * colsum(pd)).astype(BF)
            dk = dot(gr, R.q3[h, qs, :])
            dv = dot(p.astype(BF), gah)
            R.dk[...] = R.dk[...] + dk
            R.dv[...] = R.dv[...] + dv
            R.half[h, :, qs] = dot(R.k3[h], gr, 0, 0) * 0.125
            return 0

        R.dk[...] = jnp.zeros((L, HD), F32)
        R.dv[...] = jnp.zeros((L, HD), F32)
        lax.fori_loop(0, 2, part, 0)
        for ref, lo in ((R.dk, 64 * h), (R.dv, 192 + 64 * h)):
            R.kvs[:, lo:lo + 64] = ref[theirs, :].astype(BF)
            R.kvo[:, lo:lo + 64] = ref[ours, :]

    ck, cd, cq, ctb, csm, ctz = chan(1), chan(4), cs["q"], cs["t"], chan(6), chan(4)
    theirs, ours = ds((1 - y) * 512, 512), ds(y * 512, 512)

    def kv_out():
        send(R.kvs, R.kvr, ck, ydev)

    def kv_in():
        recv(R.kvr, ck)
        kv = (R.kvo[...] + R.kvr[...].astype(F32)).astype(BF)
        gq = jnp.concatenate([R.half[h] for h in range(3)], axis=0).T.astype(BF)
        R.gqkv[...] = jnp.concatenate([gq, kv], axis=1)
        for k in (2, 1, 3):
            send(R.gqkv.at[ds(zk[k] * T, T), :], R.dqin.at[z], cd + k, zdev[k])
        R.dqin[z] = R.gqkv[ds(z * T, T), :]

    def q0():
        def other(i, _):
            R.qs0[ds(i * 128, 128), :] = dot(R.elow[:, ds((1 - c) * 384 + i * 128, 128)], R.gqkv[...], 0, 0).astype(BF)
            return 0

        def same(i, _):
            R.qp[ds(i * 128, 128), :] = dot(R.elow[:, ds(c * 384 + i * 128, 128)], R.gqkv[...], 0, 0)
            return 0

        lax.fori_loop(0, 3, other, 0)
        send(R.qs0, R.qr0, cq, rdev[1])
        lax.fori_loop(0, 3, same, 0)

    def q1():
        recv(R.qr0, cq)
        R.qs1[...] = (R.qp[ds((1 - x) * 192, 192), :]
                      + R.qr0[ds((1 - x) * 192, 192), :].astype(F32)).astype(BF)
        send(R.qs1, R.qr1, cq + 1, rdev[2])

    def qsum(o):
        return (R.qp[ds(x * 192 + o, 96), :] + R.qr0[ds(x * 192 + o, 96), :].astype(F32)
                + R.qr1[ds(o, 96), :].astype(F32))

    def q2():
        recv(R.qr1, cq + 1)
        R.qs2[...] = qsum((1 - y) * 96).astype(BF)
        send(R.qs2, R.qr2, cq + 2, ydev)

    def q3():
        recv(R.qr2, cq + 2)
        gatherA("q", qsum(y * 96) + R.qr2[...].astype(F32))

    def entry():
        for k in (1, 2, 3):
            recv(R.dqin.at[zk[k]], cd + k)
        gq, gk, gv = (jnp.concatenate([R.dqin[j, :, 192 * i:192 * i + 192] for j in range(4)], axis=1) for i in range(3))
        R.sm[0:1, :] = colsum(gq.astype(F32))
        R.sm[1:2, :] = colsum(gv.astype(F32))
        ge = R.own[...] + dot(gq, R.Gwq[...], 1, 1) + dot(gk, R.Gwk[...], 1, 1) + dot(gv, R.Gwv[...], 1, 1)
        gel = ge.astype(BF)
        R.gtok[...] = gel
        R.gp[...] = dot(hot_of(me, 512, 0), gel)
        R.sm[12:14, :] = dot(hot_of(me, 16, 512), gel)[0:2, :]
        R.ts0[...] = R.gp[ds((1 - c) * 256, 256), :].astype(BF)
        send(R.ts0, R.tr0, ctb, rdev[1])
        R.sms[0] = R.sm[...]
        send(R.sms.at[0], R.smr.at[0], csm, rdev[1])

    gt = group["t"]

    def t1():
        recv(R.tr0, ctb)
        a = gt.w[0] // 2
        R.ts1[...] = (R.gp[ds(c * 256 + (1 - a) * 128, 128), :]
                      + R.tr0[ds((1 - a) * 128, 128), :].astype(F32)).astype(BF)
        send(R.ts1, R.tr1, ctb + 1, gt.dev[2])
        recv(R.smr.at[0], csm)
        R.sms[1] = R.sms[0] + R.smr[0]
        send(R.sms.at[1], R.smr.at[1], csm + 1, rdev[2])

    def tsum(b):
        lanes, a = ds(b * 384, 384), gt.w[0] // 2
        return (R.gp[ds(c * 256 + a * 128, 128), lanes] + R.tr0[ds(a * 128, 128), lanes].astype(F32)
                + R.tr1[:, lanes].astype(F32))

    def t2():
        recv(R.tr1, ctb + 1)
        R.ts2[...] = tsum(1 - gt.b).astype(BF)
        send(R.ts2, R.tr2, ctb + 2, gt.bdev)
        recv(R.smr.at[1], csm + 1)
        R.sms[2] = R.sms[1] + R.smr[1]
        send(R.sms.at[2], R.smr.at[2], csm + 2, ydev)

    def t3():
        recv(R.tr2, ctb + 2)
        tv = tsum(gt.b) + R.tr2[...].astype(F32)
        R.ts3[...] = tv.astype(BF)
        for k in (2, 1, 3):
            send(R.ts3.at[ds(zk[k] * 32, 32), :], R.tr3.at[k], ctz + k, zdev[k])
        R.gp[0:128, 0:384] = tv
        recv(R.smr.at[2], csm + 2)
        R.sms[3] = R.sms[2] + R.smr[2]
        for k in (2, 1, 3):
            send(R.sms.at[3], R.smr.at[2 + k], csm + 2 + k, zdev[k])

    def t4():
        fin = R.gp[ds(z * 32, 32), 0:384]
        for k in (1, 2, 3):
            recv(R.tr3.at[k], ctz + k)
            fin = fin + R.tr3[k].astype(F32)
        gatherA("t", fin)
        total = R.sms[3]
        for k in (1, 2, 3):
            recv(R.smr.at[2 + k], csm + 2 + k)
            total = total + R.smr[2 + k]
        R.Gs[...] = total

    def assemble():
        gatherF("q")

        def part(i, _):
            m = ds(i * 128, 128)
            for t, out in enumerate((R.Gwq, R.Gwk, R.Gwv)):
                out[m, :] = jnp.concatenate([R.Gq[j, m, 192 * t:192 * t + 192] for j in range(4)], axis=1)
            return 0

        lax.fori_loop(0, 6, part, 0)

    tasks = {"gs": lambda: pass_on("gs", R.xgs), "gb": lambda: pass_on("gb", R.xgb), "sb": share_branch, "in": heads_in, "kv": kv_out,
             "vk": kv_in, "q0": q0, "q1": q1, "q2": q2, "q3": q3, "en": entry, "t1": t1, "t2": t2, "t3": t3, "t4": t4,
             "as": assemble}
    for h in range(3):
        tasks["h%d" % h] = partial(backward, h)
    for n in STREAMS:
        for stage, f in zip("12z3ABCDEF", (stage1, stage2, stage2z, stage3, gatherZ, gatherB, gatherC, gatherD, gatherE, gatherF), strict=True):
            tasks[stage + n] = partial(f, n)
    for name in ORDER:
        tasks[name]()
    for cp in pending:
        cp.wait_send()


def mega(*args):
    any_, vm = pl.BlockSpec(memory_space=pltpu.HBM), pl.BlockSpec(memory_space=VMEM)
    square = VMEM((D, D), BF)
    return pl.pallas_call(
        kernel,
        out_shape=(VMEM((T, D), BF), VMEM((T, D), BF), VMEM((F, D), BF), VMEM((D, F), BF), square, square, square, square,
                   VMEM((512, D), BF), VMEM((16, D), F32)),
        in_specs=[any_, any_, vm, vm, any_, vm] + [any_] * 6,
        out_specs=(vm,) * 10,
        scratch_shapes=list(scratch().values()),
        compiler_params=pltpu.CompilerParams(collective_id=0, has_side_effects=True, vmem_limit_bytes=41 << 20),
    )(*args)


def finish_kernel(layer, gtok, g2, g1, go, gq, gk, gv, gt, gs, layer_o, gtok_o, t_o, q_o, k_o, v_o, o_o, o1, o2, tab, buf, wide, sem, sem2):
    whole = [pltpu.make_async_copy(a, b, sem2.at[i]) for i, (a, b) in enumerate(((layer, layer_o), (gtok, gtok_o)))]
    for cp in whole:
        cp.start()
    tab[0:512, :] = gt[...].astype(F32)
    tab[512:514, :] = gs[12:14, :]
    whole.append(pltpu.make_async_copy(tab, t_o, sem2.at[2]))
    whole[-1].start()
    chunks = [(g2, o2, buf, i) for i in range(12)] + [(g1, o1, wide, i) for i in range(12)]
    chunks += [(a, b, buf, i) for a, b in ((go, o_o), (gq, q_o), (gk, k_o), (gv, v_o)) for i in range(3)]
    flying = {}
    for n, (src, dst, stage, i) in enumerate(chunks):
        rows = 256 if stage is buf else 64
        slot = n % 4
        if n >= 4:
            flying[slot].wait()
        stage[slot] = src[i * rows:(i + 1) * rows, :].astype(F32)
        flying[slot] = pltpu.make_async_copy(stage.at[slot], dst.at[i * rows:(i + 1) * rows, :], sem.at[slot])
        flying[slot].start()
    for slot in range(4):
        flying[slot].wait()
    for cp in whole:
        cp.wait()


def finish(*args):
    S = jax.ShapeDtypeStruct
    square = S((D, D), F32)
    hbm, vm = pl.BlockSpec(memory_space=pltpu.HBM), pl.BlockSpec(memory_space=VMEM)
    return pl.pallas_call(
        finish_kernel,
        out_shape=(S((T, D), BF), S((T, D), BF), S((514, D), F32), square, square, square, square, S((D, F), F32), S((F, D), F32)),
        in_specs=[vm] * 10,
        out_specs=(hbm,) * 9,
        scratch_shapes=[VMEM((514, D), F32), VMEM((4, 256, D), F32), VMEM((4, 64, F), F32), pltpu.SemaphoreType.DMA((4,)),
                        pltpu.SemaphoreType.DMA((3,))],
        compiler_params=pltpu.CompilerParams(vmem_limit_bytes=20 << 20),
    )(*args)


def fast_device(tokens, cotangent, segment_ids, restarts, position_table, query_weight, query_bias, key_weight,
                value_weight, value_bias, out_weight, out_bias, first_gain, first_shift, inner_weight, inner_bias,
                outer_weight, outer_bias, second_gain, second_shift):
    vectors = (query_bias, value_bias, out_bias, first_gain, first_shift, outer_bias, second_gain, second_shift)
    small, at = jnp.zeros((16 * D,), F32), 0
    for v in vectors + (inner_bias,):
        small = small + jnp.pad(v.astype(F32), (at, 16 * D - at - v.shape[0]))
        at += v.shape[0]
    small = small.reshape(16, D)
    made = mega(
        tokens[0], cotangent[0], segment_ids, restarts, position_table, small, query_weight,
        key_weight, value_weight, out_weight, inner_weight, outer_weight)
    layer, gtok, table, gq, gk, gv, go, g1, g2 = finish(*made)
    gs = made[-1]
    return (layer[None], gtok[None], table, gq, gs[0], gk, gv, gs[1], go, gs[2], gs[3], gs[4], g1, gs[8:12].reshape(F), g2,
            gs[5], gs[6], gs[7])


HEADS = 12


epsilon = 1e-05


def carried_in(array, axis, combine, identity):
    count, place = (lax.axis_size(axis), lax.axis_index(axis))
    everything = lax.all_gather(array, axis)
    start = jnp.broadcast_to(jnp.asarray(identity, array.dtype), array.shape)

    def hop(k, before):
        reached = k < place
        new = combine(before, everything[k])
        return jnp.where(reached, new, before)

    return lax.fori_loop(0, count, hop, start)


def matmul(left, right):
    return jnp.dot(left, right, preferred_element_type=jnp.float32)


def matmul_t(left, right):
    return lax.dot_general(
        left, right, (((1,), (1,)), ((), ())), preferred_element_type=jnp.float32
    )


def outer_sum(left, right):
    return lax.dot_general(
        left, right, (((0,), (0,)), ((), ())), preferred_element_type=jnp.float32
    )


def norm_forward(value, gain, shift):
    centered = value - jnp.mean(value, axis=-1, keepdims=True)
    spread = jnp.mean(centered * centered, axis=-1, keepdims=True)
    inverse = lax.rsqrt(spread + epsilon)
    normal = centered * inverse
    return (normal * gain.astype(jnp.float32) + shift.astype(jnp.float32), normal, inverse)


def norm_backward(incoming, normal, inverse, gain):
    scaled = incoming * gain.astype(jnp.float32)
    centred = scaled - jnp.mean(scaled, axis=-1, keepdims=True)
    outgoing = inverse * (centred - normal * jnp.mean(scaled * normal, axis=-1, keepdims=True))
    return (outgoing, jnp.sum(incoming * normal, axis=0), jnp.sum(incoming, axis=0))


def block_size(key_count):
    for option in (1024, 512):
        return option
    return key_count


def make_forward(queries, query_segs, score_scale):
    rows_here, tok_count, head_count, head_depth = queries.shape

    def step(carry, piece, start):
        key_rows, value_rows, key_segs = piece
        key_count = key_rows.shape[1]
        size = block_size(key_count)

        def one_block(index, state):
            highest, denom, accum = state
            begin = index * size
            keys_blk = lax.dynamic_slice_in_dim(key_rows, begin, size, 1).reshape(
                rows_here, size, head_count, head_depth
            )
            values_blk = lax.dynamic_slice_in_dim(value_rows, begin, size, 1).reshape(
                rows_here, size, head_count, head_depth
            )
            segs_blk = lax.dynamic_slice_in_dim(key_segs, begin, size, 1)
            scores = (
                jnp.einsum("rqhd,rkhd->rhqk", queries, keys_blk, preferred_element_type=jnp.float32)
                * score_scale
            )
            allowed = query_segs[:, None, :, None] == segs_blk[:, None, None, :]
            scores = jnp.where(allowed, scores, -jnp.inf)
            newest = jnp.maximum(highest, jnp.max(scores, axis=-1))
            weights = jnp.exp(scores - newest[..., None])
            factor = jnp.exp(highest - newest)
            denom = denom * factor + jnp.sum(weights, axis=-1)
            update = jnp.einsum(
                "rhqk,rkhd->rqhd",
                weights.astype(jnp.bfloat16),
                values_blk,
                preferred_element_type=jnp.float32,
            )
            accum = accum * jnp.swapaxes(factor, 1, 2)[..., None] + update
            return (newest, denom, accum)

        return lax.fori_loop(0, key_count // size, one_block, carry)

    return step


def make_backward(queries, query_segs, grad_attend, delta, logsum, score_scale):
    rows_here, tok_count, head_count, head_depth = queries.shape

    def step(carry, piece, start):
        key_rows, value_rows, key_segs = piece
        key_count = key_rows.shape[1]
        size = block_size(key_count)

        def one_block(index, state):
            begin = index * size
            keys_blk = lax.dynamic_slice_in_dim(key_rows, begin, size, 1).reshape(
                rows_here, size, head_count, head_depth
            )
            values_blk = lax.dynamic_slice_in_dim(value_rows, begin, size, 1).reshape(
                rows_here, size, head_count, head_depth
            )
            segs_blk = lax.dynamic_slice_in_dim(key_segs, begin, size, 1)
            scores = (
                jnp.einsum("rqhd,rkhd->rhqk", queries, keys_blk, preferred_element_type=jnp.float32)
                * score_scale
            )
            allowed = query_segs[:, None, :, None] == segs_blk[:, None, None, :]
            scores = jnp.where(allowed, scores, -jnp.inf)
            probs = jnp.exp(scores - logsum[..., None])
            grad_p = jnp.einsum(
                "rqhd,rkhd->rhqk", grad_attend, values_blk, preferred_element_type=jnp.float32
            )
            grad_s = (probs * (grad_p - delta[..., None]) * score_scale).astype(jnp.bfloat16)
            grad_q = state[0] + jnp.einsum(
                "rhqk,rkhd->rqhd", grad_s, keys_blk, preferred_element_type=jnp.float32
            )
            grad_k, grad_v = (state[1], state[2])
            grad_v_blk = jnp.einsum(
                "rhqk,rqhd->rkhd",
                probs.astype(jnp.bfloat16),
                grad_attend,
                preferred_element_type=jnp.float32,
            )
            grad_k_blk = jnp.einsum(
                "rhqk,rqhd->rkhd", grad_s, queries, preferred_element_type=jnp.float32
            )
            grad_k = lax.dynamic_update_slice_in_dim(
                grad_k, grad_k_blk.reshape(rows_here, size, head_count * head_depth), begin, 1
            )
            grad_v = lax.dynamic_update_slice_in_dim(
                grad_v, grad_v_blk.reshape(rows_here, size, head_count * head_depth), begin, 1
            )
            return (grad_q, grad_k, grad_v)

        return lax.fori_loop(0, key_count // size, one_block, carry)

    return step


def per_device(
    tokens,
    cotangent,
    segment_ids,
    restarts,
    position_table,
    query_weight,
    query_bias,
    key_weight,
    value_weight,
    value_bias,
    out_weight,
    out_bias,
    first_gain,
    first_shift,
    inner_weight,
    inner_bias,
    outer_weight,
    outer_bias,
    second_gain,
    second_shift,
):
    rows_here, tok_count, model_width = tokens.shape
    head_count = HEADS
    head_depth = model_width // head_count
    score_scale = head_depth ** (-0.5)
    flat_count = rows_here * tok_count
    row_length = tok_count * lax.axis_size("seq")
    offset = lax.axis_index("seq") * tok_count
    places = offset + jnp.arange(tok_count, dtype=jnp.int32)[None, :]
    marked = jnp.where(restarts == 1, places, -1)
    earlier = carried_in(
        jnp.max(marked, axis=1), "seq", jnp.maximum, jnp.full((rows_here,), -1, jnp.int32)
    )
    latest = jnp.maximum(lax.cummax(marked, axis=1), earlier[:, None])
    positions = places - latest + 2
    onehot = (
        positions.reshape(flat_count, 1)
        == jnp.arange(position_table.shape[0], dtype=jnp.int32)[None, :]
    )
    entry = tokens.reshape(flat_count, model_width).astype(jnp.float32) + matmul(
        onehot.astype(jnp.bfloat16), position_table
    )
    entry_low = entry.astype(jnp.bfloat16)
    queries = (matmul(entry_low, query_weight) + query_bias.astype(jnp.float32)).astype(
        jnp.bfloat16
    )
    keys_low = matmul(entry_low, key_weight).astype(jnp.bfloat16)
    values_low = (matmul(entry_low, value_weight) + value_bias.astype(jnp.float32)).astype(
        jnp.bfloat16
    )
    query_heads = queries.reshape(rows_here, tok_count, head_count, head_depth)
    key_rows = keys_low.reshape(rows_here, tok_count, model_width)
    value_rows = values_low.reshape(rows_here, tok_count, model_width)
    start_state = (
        jnp.full((rows_here, head_count, tok_count), -1e30, jnp.float32),
        jnp.zeros((rows_here, head_count, tok_count), jnp.float32),
        jnp.zeros((rows_here, tok_count, head_count, head_depth), jnp.float32),
    )
    forward_step = make_forward(query_heads, segment_ids, score_scale)
    highest, denom, accum = forward_step(
        start_state,
        (
            lax.all_gather(key_rows, "seq", axis=1, tiled=True),
            lax.all_gather(value_rows, "seq", axis=1, tiled=True),
            lax.all_gather(segment_ids, "seq", axis=1, tiled=True),
        ),
        jnp.int32(0),
    )
    attend = accum / jnp.swapaxes(denom, 1, 2)[..., None]
    logsum = highest + jnp.log(denom)
    attended_low = attend.reshape(flat_count, model_width).astype(jnp.bfloat16)
    branch = matmul(attended_low, out_weight) + out_bias.astype(jnp.float32)
    first, first_normal, first_inverse = norm_forward(entry + branch, first_gain, first_shift)
    first_low = first.astype(jnp.bfloat16)
    inner = matmul(first_low, inner_weight) + inner_bias.astype(jnp.float32)
    activation, gelu_back = jax.vjp(partial(jax.nn.gelu, approximate=False), inner)
    active_low = activation.astype(jnp.bfloat16)
    second_in = first + matmul(active_low, outer_weight) + outer_bias.astype(jnp.float32)
    result, second_normal, second_inverse = norm_forward(second_in, second_gain, second_shift)
    layer_out = result.astype(jnp.bfloat16).reshape(rows_here, tok_count, model_width)
    incoming = cotangent.reshape(flat_count, model_width).astype(jnp.float32)
    grad_second, grad_gsecond, grad_ssecond = norm_backward(
        incoming, second_normal, second_inverse, second_gain
    )
    grad_second_low = grad_second.astype(jnp.bfloat16)
    grad_wouter = outer_sum(active_low, grad_second_low)
    grad_bouter = jnp.sum(grad_second_low.astype(jnp.float32), axis=0)
    grad_inner_low = gelu_back(matmul_t(grad_second_low, outer_weight))[0].astype(jnp.bfloat16)
    grad_winner = outer_sum(first_low, grad_inner_low)
    grad_binner = jnp.sum(grad_inner_low.astype(jnp.float32), axis=0)
    grad_first = grad_second + matmul_t(grad_inner_low, inner_weight)
    grad_first_in, grad_gfirst, grad_sfirst = norm_backward(
        grad_first, first_normal, first_inverse, first_gain
    )
    grad_branch_low = grad_first_in.astype(jnp.bfloat16)
    grad_wout = outer_sum(attended_low, grad_branch_low)
    grad_bout = jnp.sum(grad_branch_low.astype(jnp.float32), axis=0)
    grad_attend = (
        matmul_t(grad_branch_low, out_weight)
        .astype(jnp.bfloat16)
        .reshape(rows_here, tok_count, head_count, head_depth)
    )
    delta_rows = jnp.sum(grad_attend.astype(jnp.float32) * attend, axis=-1)
    delta = jnp.swapaxes(delta_rows, 1, 2)
    query_zero = jnp.zeros((rows_here, tok_count, head_count, head_depth), jnp.float32)
    back_state = (
        query_zero,
        jnp.zeros((rows_here, row_length, model_width), jnp.float32),
        jnp.zeros((rows_here, row_length, model_width), jnp.float32),
    )
    backward_step = make_backward(query_heads, segment_ids, grad_attend, delta, logsum, score_scale)
    back_out = backward_step(
        back_state,
        (
            lax.all_gather(key_rows, "seq", axis=1, tiled=True),
            lax.all_gather(value_rows, "seq", axis=1, tiled=True),
            lax.all_gather(segment_ids, "seq", axis=1, tiled=True),
        ),
        jnp.int32(0),
    )
    grad_q = back_out[0]
    grad_keys, grad_values = (
        lax.psum_scatter(back_out[1], "seq", scatter_dimension=1, tiled=True),
        lax.psum_scatter(back_out[2], "seq", scatter_dimension=1, tiled=True),
    )
    grad_query_low = grad_q.reshape(flat_count, model_width).astype(jnp.bfloat16)
    grad_key_low = grad_keys.reshape(flat_count, model_width).astype(jnp.bfloat16)
    grad_value_low = grad_values.reshape(flat_count, model_width).astype(jnp.bfloat16)
    grad_entry = (
        grad_first_in
        + matmul_t(grad_query_low, query_weight)
        + matmul_t(grad_key_low, key_weight)
        + matmul_t(grad_value_low, value_weight)
    )
    grad_wquery = outer_sum(entry_low, grad_query_low)
    grad_bquery = jnp.sum(grad_query_low.astype(jnp.float32), axis=0)
    grad_wkey = outer_sum(entry_low, grad_key_low)
    grad_wvalue = outer_sum(entry_low, grad_value_low)
    grad_bvalue = jnp.sum(grad_value_low.astype(jnp.float32), axis=0)
    grad_table = lax.dot_general(
        onehot.astype(jnp.float32),
        grad_entry,
        (((0,), (0,)), ((), ())),
        precision=lax.Precision.HIGHEST,
        preferred_element_type=jnp.float32,
    )
    grad_tokens = grad_entry.astype(jnp.bfloat16).reshape(rows_here, tok_count, model_width)
    pieces = (
        lax.psum_scatter(grad_wquery, "seq", scatter_dimension=0, tiled=True),
        lax.psum_scatter(grad_wkey, "seq", scatter_dimension=0, tiled=True),
        lax.psum_scatter(grad_wvalue, "seq", scatter_dimension=0, tiled=True),
        lax.psum_scatter(grad_wout, "seq", scatter_dimension=0, tiled=True),
        lax.psum_scatter(grad_winner, "seq", scatter_dimension=0, tiled=True),
        lax.psum_scatter(grad_wouter, "seq", scatter_dimension=0, tiled=True),
    )
    pieces = (
        lax.psum(pieces[0].astype(jnp.bfloat16), "rows").astype(jnp.float32),
        lax.psum(pieces[1].astype(jnp.bfloat16), "rows").astype(jnp.float32),
        lax.psum(pieces[2].astype(jnp.bfloat16), "rows").astype(jnp.float32),
        lax.psum(pieces[3].astype(jnp.bfloat16), "rows").astype(jnp.float32),
        lax.psum(pieces[4].astype(jnp.bfloat16), "rows").astype(jnp.float32),
        lax.psum(pieces[5].astype(jnp.bfloat16), "rows").astype(jnp.float32),
    )
    total_wquery, total_wkey, total_wvalue, total_wout, total_winner, total_wouter = (
        lax.all_gather(pieces[0].astype(jnp.bfloat16), "seq", axis=0, tiled=True).astype(
            jnp.float32
        ),
        lax.all_gather(pieces[1].astype(jnp.bfloat16), "seq", axis=0, tiled=True).astype(
            jnp.float32
        ),
        lax.all_gather(pieces[2].astype(jnp.bfloat16), "seq", axis=0, tiled=True).astype(
            jnp.float32
        ),
        lax.all_gather(pieces[3].astype(jnp.bfloat16), "seq", axis=0, tiled=True).astype(
            jnp.float32
        ),
        lax.all_gather(pieces[4].astype(jnp.bfloat16), "seq", axis=0, tiled=True).astype(
            jnp.float32
        ),
        lax.all_gather(pieces[5].astype(jnp.bfloat16), "seq", axis=0, tiled=True).astype(
            jnp.float32
        ),
    )
    smalls = lax.psum(
        (
            grad_table,
            grad_bquery,
            grad_bvalue,
            grad_bout,
            grad_gfirst,
            grad_sfirst,
            grad_binner,
            grad_bouter,
            grad_gsecond,
            grad_ssecond,
        ),
        ("seq", "rows"),
    )
    (
        total_table,
        total_bquery,
        total_bvalue,
        total_bout,
        total_gfirst,
        total_sfirst,
        total_binner,
        total_bouter,
        total_gsecond,
        total_ssecond,
    ) = smalls
    return (
        layer_out,
        grad_tokens,
        total_table,
        total_wquery,
        total_bquery,
        total_wkey,
        total_wvalue,
        total_bvalue,
        total_wout,
        total_bout,
        total_gfirst,
        total_sfirst,
        total_winner,
        total_binner,
        total_wouter,
        total_bouter,
        total_gsecond,
        total_ssecond,
    )


def solution(mesh):
    in_specs = (
        P("rows", "seq", None),
        P("rows", "seq", None),
        P("rows", "seq"),
        P("rows", "seq"),
        P(),
        P(),
        P(),
        P(),
        P(),
        P(),
        P(),
        P(),
        P(),
        P(),
        P(),
        P(),
        P(),
        P(),
        P(),
        P(),
    )
    out_specs = (
        P("rows", "seq", None),
        P("rows", "seq", None),
        P(),
        P(),
        P(),
        P(),
        P(),
        P(),
        P(),
        P(),
        P(),
        P(),
        P(),
        P(),
        P(),
        P(),
        P(),
        P(),
    )
    body = fast_device if mesh.shape["seq"] == 8 and mesh.shape["rows"] == 4 else per_device
    return jax.shard_map(
        body, mesh=mesh, in_specs=in_specs, out_specs=out_specs, check_vma=False
    )
```
